32 devices in a mesh: groups: 2 (over x), blk: 16 (over z, y, core).
Axes of the slice: x: 2, y: 2, z: 4, core: 2. Of those that a mesh axis runs over, the one named last changes fastest.
Arguments:
- plus_start: bfloat16 [32, 512, 2048], P('groups', 'blk'), parts along dimension 0, may hold values from -6 to 6
- reflection: bfloat16 [2, 32, 2048, 2048], P(None, None, 'blk'), may hold values from -0.125 to 0.125
- onset_times: int32 [32, 2048], P('groups'), parts along dimension 0, may hold values from 128 to 511
Outputs:
- upgoing: bfloat16 [32, 512, 2048], P('groups', 'blk'), parts along dimension 0
- downgoing: bfloat16 [32, 512, 2048], P('groups', 'blk'), parts along dimension 0
The draws below stay inside these ranges and needn't reach their ends.
There are 2 independent parts, one for each index of `groups`. The reference program is written for one: setup_inputs(seed, part) draws one part's arguments, and reference() takes and returns one part's arrays. A program takes and returns all parts, laid end to end along the dimension named above; an argument that names none is the same for every part. Nothing has to cross between parts.
All inputs are finite; a program needn't handle non-finite values.
Results may differ from the reference program's by a relative error of at most 0.035.
Values may be sent and summed in bfloat16 or wider, within the bound.
No kernel may reach another device: no remote copies, remote signals or barrier semaphores. Data moves between devices by JAX's collectives and lax.ppermute only.
A program may use at most 192 MiB of HBM per device.

```python
import math
import jax
import jax.numpy as jnp
from jax import lax

NX = 2048
NT = 512
NFW = 32
FREQ0 = 16
NP = 16
ITERS = 2


def touch_ends(drawn, stream_key, smallest, high):
    shape = drawn.shape
    place = [jax.random.randint(jax.random.fold_in(stream_key, axis), (), 0, shape[axis]) for axis in range(len(shape))]
    drawn = drawn.at[tuple(place)].set(smallest)
    longest = shape.index(max(shape))
    place[longest] = (place[longest] + 1) % shape[longest]
    return drawn.at[tuple(place)].set(high)


def spiked(drawn, stream_key, source, target, blocks, factor):
    def block_of(axis_at):
        return (jnp.arange(drawn.shape[axis_at]) // (drawn.shape[axis_at] // blocks)).reshape((-1,) + (1,) * (drawn.ndim - 1 - axis_at))

    near = jax.random.permutation(stream_key, blocks)[block_of(target)]
    far = (block_of(target) + blocks // 2) % blocks
    return jnp.where((block_of(source) == near) | (block_of(source) == far), factor * drawn, drawn)


def block_scale(key, dims, pieces, low, largest):
    def one(dim, blocks):
        steps = jax.random.uniform(jax.random.fold_in(jax.random.fold_in(key, 6), dim), (blocks,), jnp.float32, low / len(pieces), largest / len(pieces))
        return jnp.repeat(jnp.exp(steps), dims[dim] // blocks).reshape((-1,) + (1,) * (len(dims) - dim - 1))

    factor_of = one(*pieces[0])
    for cut in pieces[1:]:
        factor_of = factor_of * one(*cut)
    return factor_of


def noise(stream_key, shape, deviation, limit, shards=(), kind=jnp.bfloat16):
    array = jax.random.normal(stream_key, shape, jnp.float32) * deviation
    if len(shards) > 0:
        array = block_scale(stream_key, shape, shards, -0.22, 0.18) * array
    return jnp.clip(array, min=-limit, max=limit).astype(kind)


def noise_with(rng, dims, scale, bound, pieces, heavy, kind=jnp.bfloat16):
    drawn = scale * jax.random.normal(rng, dims, jnp.float32)
    if pieces:
        drawn = drawn * block_scale(rng, dims, pieces, -0.22, 0.18)
    return jnp.clip(spiked(drawn, jax.random.fold_in(rng, 3), *heavy), -bound, bound).astype(kind)


def setup_inputs(seed: int = 0, part: int = 0) -> dict:
    splits = jax.random.split(jax.random.key(seed), 4)
    own_keys = jax.random.split(jax.random.fold_in(splits[3], part), 4)
    plus_start = noise(own_keys[0], (NP, NT, NX), 1.0, 6.0, ((1, 16),))
    reflection = noise_with(splits[1], (2, NFW, NX, NX), (2 * NX) ** -0.5, 0.125, ((2, 16),), (2, 3, 16, 2.0))
    onset_times = touch_ends(jax.random.randint(own_keys[2], (NP, NX), NT // 4, NT), jax.random.fold_in(own_keys[2], 1), NT // 4, NT - 1).astype(jnp.int32)
    return {"plus_start": plus_start, "reflection": reflection, "onset_times": onset_times}


def make_tables():
    freqs = FREQ0 + jnp.arange(NFW, dtype=jnp.int32)
    samples = jnp.arange(NT, dtype=jnp.int32)
    turns = freqs[:, None] * samples[None, :] % NT
    phase = turns.astype(jnp.float32) * (2.0 * math.pi / NT)
    basis = jnp.concatenate([jnp.cos(phase), -jnp.sin(phase)], axis=0)
    forward = (basis * (1.0 / math.sqrt(NT))).astype(jnp.bfloat16)
    inverse = (basis * math.sqrt(2.0 / NFW)).astype(jnp.bfloat16)
    return (forward, inverse)

def analyze(field, forward):
    total = jnp.einsum('kt,ptx->kpx', forward.astype(jnp.float32), field.astype(jnp.float32), precision=lax.Precision.HIGHEST)
    return total.reshape(2, NFW, field.shape[0], field.shape[2]).astype(jnp.bfloat16)

def synthesize(spectrum, inverse):
    flat = spectrum.reshape(2 * NFW, spectrum.shape[2], spectrum.shape[3])
    return jnp.einsum('kt,kpx->ptx', inverse.astype(jnp.float32), flat.astype(jnp.float32), precision=lax.Precision.HIGHEST)

def matmul(left, right):
    return jnp.dot(left, right, precision=lax.Precision.HIGHEST, preferred_element_type=jnp.float32)

def convolve(reflection, spectrum):

    def single(index):
        panel = lax.dynamic_index_in_dim(reflection, index, 1, keepdims=False).astype(jnp.float32)
        focal = lax.dynamic_index_in_dim(spectrum, index, 1, keepdims=False).astype(jnp.float32)
        real_sum = matmul(focal[0], panel[0]) - matmul(focal[1], panel[1])
        imag_sum = matmul(focal[1], panel[0]) + matmul(focal[0], panel[1])
        return jnp.stack([real_sum, imag_sum])
    stacked = lax.map(single, jnp.arange(NFW, dtype=jnp.int32))
    return jnp.moveaxis(stacked, 0, 1)

def correlate(reflection, spectrum):

    def single(index):
        panel = lax.dynamic_index_in_dim(reflection, index, 1, keepdims=False).astype(jnp.float32)
        focal = lax.dynamic_index_in_dim(spectrum, index, 1, keepdims=False).astype(jnp.float32)
        real_sum = matmul(focal[0], panel[0].T) + matmul(focal[1], panel[1].T)
        imag_sum = matmul(focal[1], panel[0].T) - matmul(focal[0], panel[1].T)
        return jnp.stack([real_sum, imag_sum])
    stacked = lax.map(single, jnp.arange(NFW, dtype=jnp.int32))
    return jnp.moveaxis(stacked, 0, 1)

def reference(plus_start, reflection, onset_times):
    forward, inverse = make_tables()
    keep = jnp.arange(NT, dtype=jnp.int32)[None, :, None] < onset_times[:, None, :]
    spectrum_plus = analyze(plus_start, forward)
    upgoing = plus_start
    downgoing = plus_start
    for iteration in range(ITERS):
        upgoing_spec = convolve(reflection, spectrum_plus).astype(jnp.bfloat16)
        upgoing = jnp.where(keep, synthesize(upgoing_spec, inverse), 0.0).astype(jnp.bfloat16)
        spectrum_minus = analyze(upgoing, forward)
        downgoing_spec = correlate(reflection, spectrum_minus).astype(jnp.bfloat16)
        downgoing = (plus_start.astype(jnp.float32) + jnp.where(keep, synthesize(downgoing_spec, inverse), 0.0)).astype(jnp.bfloat16)
        if iteration + 1 < ITERS:
            spectrum_plus = analyze(downgoing, forward)
    return (upgoing, downgoing)
```

```python
import functools
import math

import jax
import jax.numpy as jnp
from jax import lax
from jax.experimental import pallas as pl
from jax.experimental.pallas import tpu as pltpu
from jax.sharding import PartitionSpec as P

NT = 512
NFW = 32
FREQ0 = 16
ITERS = 2
LANES = 128
F32 = jnp.float32
BF16 = jnp.bfloat16


def basis_of(samples):
    freqs = FREQ0 + jnp.arange(NFW, dtype=jnp.int32)
    turns = freqs[:, None] * samples[None, :] % NT
    phase = turns.astype(F32) * (2.0 * math.pi / NT)
    return jnp.stack([jnp.cos(phase), -jnp.sin(phase)], axis=1)


def tables_of(samples):
    basis = basis_of(samples).reshape(2 * NFW, samples.shape[0])
    forward = (basis * (1.0 / math.sqrt(NT))).astype(BF16)
    inverse = (basis * math.sqrt(2.0 / NFW)).astype(BF16)
    return forward, inverse.T


class Places:
    def __init__(self, axis, size):
        self.axis = axis
        self.size = size
        self.line = size // 4

    def core(self):
        return [(b, b ^ 1) for b in range(self.size)]

    def pair(self):
        return [(b, b ^ 2) for b in range(self.size)]

    def shift(self, step):
        return [(b, (b // 4 + step) % self.line * 4 + b % 4) for b in range(self.size)]

    def send(self, array, pairs):
        return lax.ppermute(array, self.axis, pairs)


def own_place(line):
    me = lax.axis_index("blk")
    return me, me // 4, (me // 2) % 2, me % 2


def chip_columns(line, ahead, flip, step):
    _, l, m, _ = own_place(line)
    other = lax.rem(l + step, line) if ahead else lax.rem(l - step + line, line)
    chip = other * 2 + (lax.rem(m + flip, 2))
    return pl.multiple_of(chip * (2 * LANES), 2 * LANES)


def relative(line):
    return [(flip, step) for flip in range(2) for step in range(line)]


def split_cores(core, block):
    low, high = block[:, :LANES], block[:, LANES:]
    first = core == 0
    return jnp.where(first, low, high), jnp.where(first, high, low)


def join_cores(core, own, other):
    first = core == 0
    return jnp.concatenate([jnp.where(first, own, other), jnp.where(first, other, own)], axis=1)


def analysis_kernel(line, rows, forward_ref, plus_ref, keep0, keep1, send0, send1):
    core = own_place(line)[3]
    keep, send = (keep0, keep1), (send0, send1)
    for p in range(rows):
        for flip, step in relative(line):
            columns = pl.ds(chip_columns(line, True, flip, step), 2 * LANES)
            block = jnp.dot(forward_ref[...], plus_ref[p, :, columns], preferred_element_type=F32)
            mine, theirs = split_cores(core, block.astype(BF16))
            keep[flip][step, p] = mine
            send[flip][step, p] = theirs


def first_analysis(plus_start, forward, line):
    focal, samples, width = plus_start.shape
    rows = 4
    out = jax.ShapeDtypeStruct((line, focal, 2 * NFW, LANES), BF16)
    out_spec = pl.BlockSpec((line, rows, 2 * NFW, LANES), lambda i: (0, i, 0, 0))
    return pl.pallas_call(
        functools.partial(analysis_kernel, line, rows),
        grid=(focal // rows,),
        in_specs=[
            pl.BlockSpec((2 * NFW, samples), lambda i: (0, 0)),
            pl.BlockSpec((rows, samples, width), lambda i: (i, 0, 0)),
        ],
        out_specs=[out_spec] * 4,
        out_shape=[out] * 4,
        compiler_params=pltpu.CompilerParams(vmem_limit_bytes=24 << 20),
        cost_estimate=pl.CostEstimate(
            flops=4 * NFW * focal * samples * width,
            bytes_accessed=2 * focal * samples * width + 4 * NFW * focal * width,
            transcendentals=0,
        ),
        name="first_analysis",
    )(forward, plus_start)


def convolve_kernel(line, rows, spec_ref, panel_ref, keep0, keep1, send0, send1):
    core = own_place(line)[3]
    keep, send = (keep0, keep1), (send0, send1)
    focal = spec_ref.shape[2]
    for w in range(rows):
        real, imag = spec_ref[w, 0], spec_ref[w, 1]
        left = jnp.concatenate(
            [jnp.concatenate([real, -imag], axis=1), jnp.concatenate([imag, real], axis=1)], axis=0
        )
        for flip, step in relative(line):
            columns = pl.ds(chip_columns(line, True, flip, step), 2 * LANES)
            panel = panel_ref[:, w, :, columns].reshape(2 * LANES, 2 * LANES)
            block = jnp.dot(left, panel, preferred_element_type=F32)
            mine, theirs = split_cores(core, block.astype(BF16))
            keep[flip][step, w] = mine.reshape(2, focal, LANES)
            send[flip][step, w] = theirs.reshape(2, focal, LANES)


def convolve(spectrum, reflection, line):
    focal = spectrum.shape[2]
    sources = reflection.shape[3]
    rows = 2
    out = jax.ShapeDtypeStruct((line, NFW, 2, focal, LANES), BF16)
    out_spec = pl.BlockSpec((line, rows, 2, focal, LANES), lambda i: (0, i, 0, 0, 0))
    return pl.pallas_call(
        functools.partial(convolve_kernel, line, rows),
        grid=(NFW // rows,),
        in_specs=[
            pl.BlockSpec((rows, 2, focal, LANES), lambda i: (i, 0, 0, 0)),
            pl.BlockSpec((2, rows, LANES, sources), lambda i: (0, i, 0, 0)),
        ],
        out_specs=[out_spec] * 4,
        out_shape=[out] * 4,
        compiler_params=pltpu.CompilerParams(vmem_limit_bytes=24 << 20),
        cost_estimate=pl.CostEstimate(
            flops=8 * NFW * focal * LANES * sources,
            bytes_accessed=4 * NFW * sources * (LANES + focal),
            transcendentals=0,
        ),
        name="convolve",
    )(spectrum, reflection)


def correlate_kernel(line, rows, *refs):
    core = own_place(line)[3]
    places = relative(line)
    own, other = refs[: len(places)], refs[len(places) : 2 * len(places)]
    panel_ref, out_ref = refs[2 * len(places) :]
    focal = out_ref.shape[2]
    for w in range(rows):
        total = jnp.zeros((2 * focal, 2 * LANES), F32)
        for at, (flip, step) in enumerate(places):
            columns = pl.ds(chip_columns(line, False, flip, step), 2 * LANES)
            panel = panel_ref[:, w, :, columns].reshape(2 * LANES, 2 * LANES)
            spec = join_cores(
                core, own[at][w].reshape(2 * focal, LANES), other[at][w].reshape(2 * focal, LANES)
            )
            total += lax.dot_general(spec, panel, (((1,), (1,)), ((), ())), preferred_element_type=F32)
        out_ref[w, 0] = total[:focal, :LANES] + total[focal:, LANES:]
        out_ref[w, 1] = total[focal:, :LANES] - total[:focal, LANES:]


def correlate(own, other, reflection, line):
    focal = own[0].shape[2]
    sources = reflection.shape[3]
    rows = 2
    spec_block = pl.BlockSpec((rows, 2, focal, LANES), lambda i: (i, 0, 0, 0))
    return pl.pallas_call(
        functools.partial(correlate_kernel, line, rows),
        grid=(NFW // rows,),
        in_specs=[spec_block] * (len(own) + len(other))
        + [pl.BlockSpec((2, rows, LANES, sources), lambda i: (0, i, 0, 0))],
        out_specs=spec_block,
        out_shape=jax.ShapeDtypeStruct((NFW, 2, focal, LANES), F32),
        compiler_params=pltpu.CompilerParams(vmem_limit_bytes=24 << 20),
        cost_estimate=pl.CostEstimate(
            flops=8 * NFW * focal * LANES * sources,
            bytes_accessed=4 * NFW * sources * (LANES + focal),
            transcendentals=0,
        ),
        name="correlate",
    )(*own, *other, reflection)


def window_kernel(parts, has_base, want_spec, *refs):
    refs = list(refs)
    forward_ref, inverse_ref, onset_ref = refs[:3]
    part_refs = refs[3 : 3 + parts]
    rest = refs[3 + parts :]
    base_ref = rest.pop(0) if has_base else None
    out_ref = rest.pop(0)
    spec_ref = rest.pop(0) if want_spec else None
    held, result = rest
    focal = out_ref.shape[2]
    k = 2 * NFW
    total = part_refs[0][...].astype(F32)
    for ref in part_refs[1:]:
        total += ref[...].astype(F32)
    held[...] = total.reshape(k * focal, LANES)
    me = lax.axis_index("blk")
    columns = pl.ds(pl.multiple_of(me * LANES, LANES), LANES)
    time = lax.broadcasted_iota(jnp.int32, (NT, 2 * LANES), 0)
    for p in range(0, focal, 2):
        pair = [held[pl.ds(p + q, k, stride=focal), :].astype(BF16) for q in range(2)]
        if spec_ref is not None:
            for q in range(2):
                spec_ref[p + q] = pair[q]
        field = jnp.dot(inverse_ref[...], jnp.concatenate(pair, axis=1), preferred_element_type=F32)
        onset = jnp.concatenate([onset_ref[p + q : p + q + 1, columns] for q in range(2)], axis=1)
        kept = jnp.where(time < onset, field, 0.0).astype(BF16)
        spectrum = jnp.dot(forward_ref[...], kept, preferred_element_type=F32)
        for q in range(2):
            result[pl.ds(p + q, k, stride=focal), :] = spectrum[:, q * LANES : (q + 1) * LANES]
    final = result[...].reshape(NFW, 2, focal, LANES)
    if base_ref is not None:
        final += base_ref[...].astype(F32)
    out_ref[...] = final.astype(BF16)


def window(parts, forward, inverse, onset_times, base=None, want_spec=False):
    focal = parts[0].shape[2]
    k = 2 * NFW
    operands = [forward, inverse, onset_times, *parts] + ([] if base is None else [base])
    whole = pl.BlockSpec(memory_space=pltpu.VMEM)
    out = [jax.ShapeDtypeStruct((NFW, 2, focal, LANES), BF16)]
    if want_spec:
        out.append(jax.ShapeDtypeStruct((focal, k, LANES), BF16))
    return pl.pallas_call(
        functools.partial(window_kernel, len(parts), base is not None, want_spec),
        in_specs=[whole] * len(operands),
        out_specs=[whole] * len(out),
        out_shape=out,
        scratch_shapes=[pltpu.VMEM((k * focal, LANES), F32)] * 2,
        compiler_params=pltpu.CompilerParams(vmem_limit_bytes=24 << 20),
        cost_estimate=pl.CostEstimate(
            flops=4 * k * NT * focal * LANES, bytes_accessed=2 * k * focal * LANES * 6, transcendentals=0
        ),
        name="window",
    )(*operands)


def field_kernel(line, rows, has_plus, *refs):
    core = own_place(line)[3]
    places = relative(line)
    inverse_ref, onset_ref = refs[:2]
    own, other = refs[2 : 2 + len(places)], refs[2 + len(places) : 2 + 2 * len(places)]
    rest = refs[2 + 2 * len(places) :]
    out_ref = rest[-1]
    samples = out_ref.shape[1]
    first = pl.program_id(0) * rows
    time = lax.axis_index("blk") * samples + lax.broadcasted_iota(jnp.int32, (samples, 2 * LANES), 0)
    for p in range(rows):
        for at, (flip, step) in enumerate(places):
            columns = pl.ds(chip_columns(line, False, flip, step), 2 * LANES)
            spec = join_cores(core, own[at][p], other[at][p])
            field = jnp.dot(inverse_ref[...], spec, preferred_element_type=F32)
            value = jnp.where(time < onset_ref[pl.ds(first + p, 1), columns], field, 0.0)
            if has_plus:
                value += rest[0][p, :, columns].astype(F32)
            out_ref[p, :, columns] = value.astype(BF16)


def field(own, other, inverse, onset_times, line, plus_start=None):
    focal, k, _ = own[0].shape
    samples = inverse.shape[0]
    width = onset_times.shape[1]
    rows = 4
    spec_block = pl.BlockSpec((rows, k, LANES), lambda i: (i, 0, 0))
    wide = pl.BlockSpec((rows, samples, width), lambda i: (i, 0, 0))
    plus = [] if plus_start is None else [plus_start]
    return pl.pallas_call(
        functools.partial(field_kernel, line, rows, bool(plus)),
        grid=(focal // rows,),
        in_specs=[
            pl.BlockSpec(inverse.shape, lambda i: (0, 0)),
            pl.BlockSpec(onset_times.shape, lambda i: (0, 0)),
        ]
        + [spec_block] * (len(own) + len(other))
        + [wide] * len(plus),
        out_specs=wide,
        out_shape=jax.ShapeDtypeStruct((focal, samples, width), BF16),
        compiler_params=pltpu.CompilerParams(vmem_limit_bytes=24 << 20),
        cost_estimate=pl.CostEstimate(
            flops=2 * k * focal * samples * width,
            bytes_accessed=2 * focal * width * (k + 2 * samples),
            transcendentals=0,
        ),
        name="field",
    )(inverse, onset_times, *own, *other, *plus)


def add(*parts):
    total = parts[0].astype(F32)
    for part in parts[1:]:
        total += part.astype(F32)
    return total


def reduce_scatter(places, keep0, keep1, send0, send1):
    got1 = places.send(send1, places.core())
    got0 = places.send(send0, places.core())
    order = list(range(1, places.line)) + [0]
    across = {}
    for step in order:
        across[step] = places.send(add(keep1[step], got1[step]).astype(BF16), places.pair())
    parts = [keep0[0], got0[0], across[0]]
    for step in order[:-1]:
        summed = add(keep0[step], got0[step], across[step]).astype(BF16)
        parts.append(places.send(summed, places.shift(step)))
    return parts


def all_gather(places, block):
    line = [block] + [places.send(block, places.shift(step)) for step in range(1, places.line)]
    own = line + [places.send(piece, places.pair()) for piece in line]
    other = [places.send(piece, places.core()) for piece in own]
    return own, other


def local(plus_start, reflection, onset_times):
    size = lax.axis_size("blk")
    places = Places("blk", size)
    line = places.line
    focal, samples, _ = plus_start.shape
    forward, inverse = tables_of(jnp.arange(NT, dtype=jnp.int32))
    own_samples = lax.axis_index("blk") * samples + jnp.arange(samples, dtype=jnp.int32)
    own_forward, own_inverse = tables_of(own_samples)

    parts = reduce_scatter(places, *first_analysis(plus_start, own_forward, line))
    start = add(*parts).astype(BF16)
    start = jnp.transpose(start, (1, 0, 2)).reshape(NFW, 2, focal, LANES)
    spectrum_plus = start
    for iteration in range(ITERS):
        last = iteration + 1 == ITERS
        parts = reduce_scatter(places, *convolve(spectrum_plus, reflection, line))
        windowed = window(parts, forward, inverse, onset_times, want_spec=last)
        gathered = all_gather(places, windowed[0])
        if last:
            upgoing_spec = all_gather(places, windowed[1])
        downgoing_spec = correlate(*gathered, reflection, line)
        if not last:
            (spectrum_plus,) = window([downgoing_spec], forward, inverse, onset_times, base=start)
    upgoing = field(*upgoing_spec, own_inverse, onset_times, line)
    final = jnp.transpose(
        downgoing_spec.astype(BF16).reshape(2 * NFW, focal, LANES), (1, 0, 2)
    )
    downgoing = field(*all_gather(places, final), own_inverse, onset_times, line, plus_start)
    return upgoing, downgoing


def analyze(values, forward):
    total = jnp.einsum("kt,ptx->kpx", forward, values, preferred_element_type=F32)
    return total.reshape(NFW, 2, values.shape[0], values.shape[2])


def synthesize(spectrum, inverse):
    flat = spectrum.reshape(2 * NFW, spectrum.shape[2], spectrum.shape[3])
    return jnp.einsum("tk,kpx->ptx", inverse, flat, preferred_element_type=F32)


def contract(form, left, right):
    return jnp.einsum(form, left, right, preferred_element_type=F32)


def local_any(plus_start, reflection, onset_times):
    samples = plus_start.shape[1]
    width = reflection.shape[2]
    me = lax.axis_index("blk")
    forward, inverse = tables_of(jnp.arange(NT, dtype=jnp.int32))
    own_forward, own_inverse = tables_of(me * samples + jnp.arange(samples, dtype=jnp.int32))
    onset = lax.dynamic_slice_in_dim(onset_times, me * width, width, 1)
    keep = jnp.arange(NT, dtype=jnp.int32)[None, :, None] < onset[:, None, :]
    time = me * samples + jnp.arange(samples, dtype=jnp.int32)
    own_keep = time[None, :, None] < onset_times[:, None, :]

    def scatter(partial):
        return lax.psum_scatter(partial.astype(BF16), "blk", scatter_dimension=3, tiled=True).astype(BF16)

    def gather(block):
        return lax.all_gather(block, "blk", axis=3, tiled=True)

    start = scatter(analyze(plus_start, own_forward))
    spectrum = start
    for iteration in range(ITERS):
        real = contract("wrs,wpr->wps", reflection[0], spectrum[:, 0]) - contract(
            "wrs,wpr->wps", reflection[1], spectrum[:, 1]
        )
        imag = contract("wrs,wpr->wps", reflection[0], spectrum[:, 1]) + contract(
            "wrs,wpr->wps", reflection[1], spectrum[:, 0]
        )
        upgoing_spec = scatter(jnp.stack([real, imag], axis=1))
        kept = jnp.where(keep, synthesize(upgoing_spec, inverse), 0.0).astype(BF16)
        minus = gather(analyze(kept, forward).astype(BF16))
        real = contract("wrs,wps->wpr", reflection[0], minus[:, 0]) + contract(
            "wrs,wps->wpr", reflection[1], minus[:, 1]
        )
        imag = contract("wrs,wps->wpr", reflection[0], minus[:, 1]) - contract(
            "wrs,wps->wpr", reflection[1], minus[:, 0]
        )
        downgoing_spec = jnp.stack([real, imag], axis=1).astype(BF16)
        if iteration + 1 < ITERS:
            kept = jnp.where(keep, synthesize(downgoing_spec, inverse), 0.0).astype(BF16)
            spectrum = (start.astype(F32) + analyze(kept, forward)).astype(BF16)
    upgoing = jnp.where(own_keep, synthesize(gather(upgoing_spec), own_inverse), 0.0).astype(BF16)
    change = jnp.where(own_keep, synthesize(gather(downgoing_spec), own_inverse), 0.0)
    return upgoing, (plus_start.astype(F32) + change).astype(BF16)


def solution(mesh):
    size = mesh.shape["blk"]

    def run(plus_start, reflection, onset_times):
        width = reflection.shape[2] // size
        fits = width == LANES and size % 4 == 0 and (plus_start.shape[1] // size) % 16 == 0
        return jax.shard_map(
            local if fits else local_any,
            mesh=mesh,
            in_specs=(P("groups", "blk", None), P(None, None, "blk", None), P("groups", None)),
            out_specs=(P("groups", "blk", None), P("groups", "blk", None)),
            check_vma=False,
        )(plus_start, reflection, onset_times)

    return run
```

```python
import functools
import math

import jax
import jax.numpy as jnp
from jax import lax
from jax.experimental import pallas as pl
from jax.experimental.pallas import tpu as pltpu
from jax.sharding import PartitionSpec as P

NT = 512
NFW = 32
FREQ0 = 16
ITERS = 2
LANES = 128
F32 = jnp.float32
BF16 = jnp.bfloat16


def basis_of(samples):
    freqs = FREQ0 + jnp.arange(NFW, dtype=jnp.int32)
    turns = freqs[:, None] * samples[None, :] % NT
    phase = turns.astype(F32) * (2.0 * math.pi / NT)
    return jnp.stack([jnp.cos(phase), -jnp.sin(phase)], axis=1)


def tables_of(samples):
    basis = basis_of(samples).reshape(2 * NFW, samples.shape[0])
    forward = (basis * (1.0 / math.sqrt(NT))).astype(BF16)
    inverse = (basis * math.sqrt(2.0 / NFW)).astype(BF16)
    return forward, inverse.T


class Places:
    def __init__(self, axis, size):
        self.axis = axis
        self.size = size
        self.line = size // 4

    def core(self):
        return [(b, b ^ 1) for b in range(self.size)]

    def pair(self):
        return [(b, b ^ 2) for b in range(self.size)]

    def shift(self, step):
        return [(b, (b // 4 + step) % self.line * 4 + b % 4) for b in range(self.size)]

    def send(self, array, pairs):
        return lax.ppermute(array, self.axis, pairs)


def own_place(line):
    me = lax.axis_index("blk")
    return me, me // 4, (me // 2) % 2, me % 2


def chip_columns(line, ahead, flip, step):
    _, l, m, _ = own_place(line)
    other = lax.rem(l + step, line) if ahead else lax.rem(l - step + line, line)
    chip = other * 2 + (lax.rem(m + flip, 2))
    return pl.multiple_of(chip * (2 * LANES), 2 * LANES)


def relative(line):
    return [(flip, step) for flip in range(2) for step in range(line)]


def split_cores(core, block):
    low, high = block[:, :LANES], block[:, LANES:]
    first = core == 0
    return jnp.where(first, low, high), jnp.where(first, high, low)


def join_cores(core, own, other):
    first = core == 0
    return jnp.concatenate([jnp.where(first, own, other), jnp.where(first, other, own)], axis=1)


def analysis_kernel(line, rows, forward_ref, plus_ref, keep0, keep1, send0, send1):
    core = own_place(line)[3]
    keep, send = (keep0, keep1), (send0, send1)
    for p in range(rows):
        for flip, step in relative(line):
            columns = pl.ds(chip_columns(line, True, flip, step), 2 * LANES)
            block = jnp.dot(forward_ref[...], plus_ref[p, :, columns], preferred_element_type=F32)
            mine, theirs = split_cores(core, block.astype(BF16))
            keep[flip][step, p] = mine
            send[flip][step, p] = theirs


def first_analysis(plus_start, forward, line):
    focal, samples, width = plus_start.shape
    rows = 4
    out = jax.ShapeDtypeStruct((line, focal, 2 * NFW, LANES), BF16)
    out_spec = pl.BlockSpec((line, rows, 2 * NFW, LANES), lambda i: (0, i, 0, 0))
    return pl.pallas_call(
        functools.partial(analysis_kernel, line, rows),
        grid=(focal // rows,),
        in_specs=[
            pl.BlockSpec((2 * NFW, samples), lambda i: (0, 0)),
            pl.BlockSpec((rows, samples, width), lambda i: (i, 0, 0)),
        ],
        out_specs=[out_spec] * 4,
        out_shape=[out] * 4,
        compiler_params=pltpu.CompilerParams(vmem_limit_bytes=24 << 20),
        cost_estimate=pl.CostEstimate(
            flops=4 * NFW * focal * samples * width,
            bytes_accessed=2 * focal * samples * width + 4 * NFW * focal * width,
            transcendentals=0,
        ),
        name="first_analysis",
    )(forward, plus_start)


def convolve_kernel(line, rows, chips_ref, spec_ref, *refs):
    core = own_place(line)[3]
    panels, (keep, send) = refs[:line], refs[line:]
    focal = spec_ref.shape[2]
    for w in range(rows):
        real, imag = spec_ref[w, 0], spec_ref[w, 1]
        left = jnp.concatenate(
            [jnp.concatenate([real, -imag], axis=1), jnp.concatenate([imag, real], axis=1)], axis=0
        )
        for step in range(line):
            panel = panels[step][:, w].reshape(2 * LANES, 2 * LANES)
            block = jnp.dot(left, panel, preferred_element_type=F32)
            mine, theirs = split_cores(core, block.astype(BF16))
            keep[step, w] = mine.reshape(2, focal, LANES)
            send[step, w] = theirs.reshape(2, focal, LANES)


def panel_specs(line, rows):
    def block(step):
        return pl.BlockSpec((2, rows, LANES, 2 * LANES), lambda i, chips: (0, i, 0, chips[step]))

    return [block(step) for step in range(line)]


def chips_of(line, ahead, flip):
    _, l, m, _ = own_place(line)
    steps = jnp.arange(line, dtype=jnp.int32)
    other = (l + steps) % line if ahead else (l - steps + line) % line
    return other * 2 + (m + flip) % 2


def convolve(spectrum, reflection, line, flip):
    focal = spectrum.shape[2]
    sources = reflection.shape[3] // 2
    rows = 4
    out = jax.ShapeDtypeStruct((line, NFW, 2, focal, LANES), BF16)
    out_spec = pl.BlockSpec((line, rows, 2, focal, LANES), lambda i, chips: (0, i, 0, 0, 0))
    return pl.pallas_call(
        functools.partial(convolve_kernel, line, rows),
        grid_spec=pltpu.PrefetchScalarGridSpec(
            num_scalar_prefetch=1,
            grid=(NFW // rows,),
            in_specs=[pl.BlockSpec((rows, 2, focal, LANES), lambda i, chips: (i, 0, 0, 0))]
            + panel_specs(line, rows),
            out_specs=[out_spec] * 2,
        ),
        out_shape=[out] * 2,
        compiler_params=pltpu.CompilerParams(vmem_limit_bytes=24 << 20),
        cost_estimate=pl.CostEstimate(
            flops=8 * NFW * focal * LANES * sources,
            bytes_accessed=4 * NFW * sources * (LANES + focal),
            transcendentals=0,
        ),
        name=f"convolve{flip}",
    )(chips_of(line, True, flip), spectrum, *[reflection] * line)


def correlate_kernel(line, rows, has_base, chips_ref, *refs):
    core = own_place(line)[3]
    own, other, panels = refs[:line], refs[line : 2 * line], refs[2 * line : 3 * line]
    base_ref = refs[3 * line] if has_base else None
    out_ref = refs[-1]
    focal = out_ref.shape[2]
    for w in range(rows):
        total = jnp.zeros((2 * LANES, 2 * focal), F32)
        for step in range(line):
            panel = panels[step][:, w].reshape(2 * LANES, 2 * LANES)
            spec = join_cores(
                core, own[step][w].reshape(2 * focal, LANES), other[step][w].reshape(2 * focal, LANES)
            )
            total += lax.dot_general(panel, spec, (((1,), (1,)), ((), ())), preferred_element_type=F32)
        total = total.T
        real = total[:focal, :LANES] + total[focal:, LANES:]
        imag = total[focal:, :LANES] - total[:focal, LANES:]
        if has_base:
            real += base_ref[w, 0]
            imag += base_ref[w, 1]
        out_ref[w, 0] = real
        out_ref[w, 1] = imag


def correlate(own, other, reflection, line, flip, base=None):
    focal = own[0].shape[2]
    sources = reflection.shape[3] // 2
    rows = 4
    spec_block = pl.BlockSpec((rows, 2, focal, LANES), lambda i, chips: (i, 0, 0, 0))
    more = [] if base is None else [base]
    return pl.pallas_call(
        functools.partial(correlate_kernel, line, rows, bool(more)),
        grid_spec=pltpu.PrefetchScalarGridSpec(
            num_scalar_prefetch=1,
            grid=(NFW // rows,),
            in_specs=[spec_block] * (2 * line) + panel_specs(line, rows) + [spec_block] * len(more),
            out_specs=spec_block,
        ),
        out_shape=jax.ShapeDtypeStruct((NFW, 2, focal, LANES), F32),
        compiler_params=pltpu.CompilerParams(vmem_limit_bytes=24 << 20),
        cost_estimate=pl.CostEstimate(
            flops=8 * NFW * focal * LANES * sources,
            bytes_accessed=4 * NFW * sources * (LANES + focal),
            transcendentals=0,
        ),
        name=f"correlate{flip}",
    )(chips_of(line, False, flip), *own, *other, *[reflection] * line, *more)


def window_kernel(parts, has_base, want_spec, *refs):
    refs = list(refs)
    forward_ref, inverse_ref, onset_ref = refs[:3]
    part_refs = refs[3 : 3 + parts]
    rest = refs[3 + parts :]
    base_ref = rest.pop(0) if has_base else None
    out_ref = rest.pop(0)
    spec_ref = rest.pop(0) if want_spec else None
    held, result = rest
    focal = out_ref.shape[2]
    k = 2 * NFW
    total = part_refs[0][...].astype(F32)
    for ref in part_refs[1:]:
        total += ref[...].astype(F32)
    held[...] = total.reshape(k * focal, LANES)
    me = lax.axis_index("blk")
    columns = pl.ds(pl.multiple_of(me * LANES, LANES), LANES)
    time = lax.broadcasted_iota(jnp.int32, (NT, 2 * LANES), 0)
    for p in range(0, focal, 2):
        pair = [held[pl.ds(p + q, k, stride=focal), :].astype(BF16) for q in range(2)]
        if spec_ref is not None:
            for q in range(2):
                spec_ref[p + q] = pair[q]
        field = jnp.dot(inverse_ref[...], jnp.concatenate(pair, axis=1), preferred_element_type=F32)
        onset = jnp.concatenate([onset_ref[p + q : p + q + 1, columns] for q in range(2)], axis=1)
        kept = jnp.where(time < onset, field, 0.0).astype(BF16)
        spectrum = jnp.dot(forward_ref[...], kept, preferred_element_type=F32)
        for q in range(2):
            result[pl.ds(p + q, k, stride=focal), :] = spectrum[:, q * LANES : (q + 1) * LANES]
    final = result[...].reshape(NFW, 2, focal, LANES)
    if base_ref is not None:
        final += base_ref[...].astype(F32)
    out_ref[...] = final.astype(BF16)


def window(parts, forward, inverse, onset_times, base=None, want_spec=False):
    focal = parts[0].shape[2]
    k = 2 * NFW
    operands = [forward, inverse, onset_times, *parts] + ([] if base is None else [base])
    whole = pl.BlockSpec(memory_space=pltpu.VMEM)
    out = [jax.ShapeDtypeStruct((NFW, 2, focal, LANES), BF16)]
    if want_spec:
        out.append(jax.ShapeDtypeStruct((focal, k, LANES), BF16))
    return pl.pallas_call(
        functools.partial(window_kernel, len(parts), base is not None, want_spec),
        in_specs=[whole] * len(operands),
        out_specs=[whole] * len(out),
        out_shape=out,
        scratch_shapes=[pltpu.VMEM((k * focal, LANES), F32)] * 2,
        compiler_params=pltpu.CompilerParams(vmem_limit_bytes=24 << 20),
        cost_estimate=pl.CostEstimate(
            flops=4 * k * NT * focal * LANES, bytes_accessed=2 * k * focal * LANES * 6, transcendentals=0
        ),
        name="window",
    )(*operands)


def field_kernel(line, rows, has_plus, *refs):
    core = own_place(line)[3]
    places = relative(line)
    inverse_ref, onset_ref = refs[:2]
    own, other = refs[2 : 2 + len(places)], refs[2 + len(places) : 2 + 2 * len(places)]
    rest = refs[2 + 2 * len(places) :]
    out_ref = rest[-1]
    samples = out_ref.shape[1]
    first = pl.program_id(0) * rows
    time = lax.axis_index("blk") * samples + lax.broadcasted_iota(jnp.int32, (samples, 2 * LANES), 0)
    for p in range(rows):
        for at, (flip, step) in enumerate(places):
            columns = pl.ds(chip_columns(line, False, flip, step), 2 * LANES)
            spec = join_cores(core, own[at][p], other[at][p])
            field = jnp.dot(inverse_ref[...], spec, preferred_element_type=F32)
            value = jnp.where(time < onset_ref[pl.ds(first + p, 1), columns], field, 0.0)
            if has_plus:
                value += rest[0][p, :, columns].astype(F32)
            out_ref[p, :, columns] = value.astype(BF16)


def field(own, other, inverse, onset_times, line, plus_start=None):
    focal, k, _ = own[0][0].shape
    samples = inverse.shape[0]
    width = onset_times.shape[1]
    rows = 4
    spec_block = pl.BlockSpec((rows, k, LANES), lambda i: (i, 0, 0))
    wide = pl.BlockSpec((rows, samples, width), lambda i: (i, 0, 0))
    own, other = sum(own, []), sum(other, [])
    plus = [] if plus_start is None else [plus_start]
    return pl.pallas_call(
        functools.partial(field_kernel, line, rows, bool(plus)),
        grid=(focal // rows,),
        in_specs=[
            pl.BlockSpec(inverse.shape, lambda i: (0, 0)),
            pl.BlockSpec(onset_times.shape, lambda i: (0, 0)),
        ]
        + [spec_block] * (len(own) + len(other))
        + [wide] * len(plus),
        out_specs=wide,
        out_shape=jax.ShapeDtypeStruct((focal, samples, width), BF16),
        compiler_params=pltpu.CompilerParams(vmem_limit_bytes=24 << 20),
        cost_estimate=pl.CostEstimate(
            flops=2 * k * focal * samples * width,
            bytes_accessed=2 * focal * width * (k + 2 * samples),
            transcendentals=0,
        ),
        name="field",
    )(inverse, onset_times, *own, *other, *plus)


def add(*parts):
    total = parts[0].astype(F32)
    for part in parts[1:]:
        total += part.astype(F32)
    return total


def after(value, *others):
    return lax.optimization_barrier((value, *others))[0]


def far_first(line):
    return sorted(range(line), key=lambda step: -min(step, line - step))


def reduce_scatter(places, keep0, keep1, send0, send1):
    got1 = places.send(send1, places.core())
    got0 = places.send(send0, places.core())
    order = far_first(places.line)
    across = {}
    ready = got1
    for step in order:
        ready = add(keep1[step], after(got1, ready)[step]).astype(BF16)
        across[step] = places.send(ready, places.pair())
    parts = [keep0[0], got0[0], across[0]]
    ready = got0
    for step in order[:-1]:
        ready = add(keep0[step], after(got0, ready)[step], across[step]).astype(BF16)
        parts.append(places.send(ready, places.shift(step)))
    return parts


def all_gather(places, block):
    near_first = far_first(places.line)[::-1]
    line = {0: block}
    for step in near_first[1:]:
        line[step] = places.send(block, places.shift(step))
    across = {step: places.send(line[step], places.pair()) for step in near_first}
    own = [[side[step] for step in range(places.line)] for side in (line, across)]
    other = [[places.send(piece, places.core()) for piece in side] for side in own]
    return own, other


def local(plus_start, reflection, onset_times):
    size = lax.axis_size("blk")
    places = Places("blk", size)
    line = places.line
    focal, samples, _ = plus_start.shape
    forward, inverse = tables_of(jnp.arange(NT, dtype=jnp.int32))
    own_samples = lax.axis_index("blk") * samples + jnp.arange(samples, dtype=jnp.int32)
    own_forward, own_inverse = tables_of(own_samples)

    parts = reduce_scatter(places, *first_analysis(plus_start, own_forward, line))
    start = add(*parts).astype(BF16)
    start = jnp.transpose(start, (1, 0, 2)).reshape(NFW, 2, focal, LANES)
    spectrum_plus = start
    for iteration in range(ITERS):
        last = iteration + 1 == ITERS
        keep1, send1 = convolve(spectrum_plus, reflection, line, 1)
        keep0, send0 = convolve(after(spectrum_plus, keep1), reflection, line, 0)
        parts = reduce_scatter(places, keep0, keep1, send0, send1)
        windowed = window(parts, forward, inverse, onset_times, want_spec=last)
        gathered = all_gather(places, windowed[0])
        if last:
            upgoing_spec = all_gather(places, windowed[1])
        own, other = gathered
        downgoing_spec = correlate(own[0], other[0], reflection, line, 0)
        downgoing_spec = correlate(own[1], other[1], reflection, line, 1, downgoing_spec)
        if not last:
            (spectrum_plus,) = window([downgoing_spec], forward, inverse, onset_times, base=start)
    upgoing = field(*upgoing_spec, own_inverse, onset_times, line)
    final = jnp.transpose(
        downgoing_spec.astype(BF16).reshape(2 * NFW, focal, LANES), (1, 0, 2)
    )
    downgoing = field(*all_gather(places, final), own_inverse, onset_times, line, plus_start)
    return upgoing, downgoing


def analyze(values, forward):
    total = jnp.einsum("kt,ptx->kpx", forward, values, preferred_element_type=F32)
    return total.reshape(NFW, 2, values.shape[0], values.shape[2])


def synthesize(spectrum, inverse):
    flat = spectrum.reshape(2 * NFW, spectrum.shape[2], spectrum.shape[3])
    return jnp.einsum("tk,kpx->ptx", inverse, flat, preferred_element_type=F32)


def contract(form, left, right):
    return jnp.einsum(form, left, right, preferred_element_type=F32)


def local_any(plus_start, reflection, onset_times):
    samples = plus_start.shape[1]
    width = reflection.shape[2]
    me = lax.axis_index("blk")
    forward, inverse = tables_of(jnp.arange(NT, dtype=jnp.int32))
    own_forward, own_inverse = tables_of(me * samples + jnp.arange(samples, dtype=jnp.int32))
    onset = lax.dynamic_slice_in_dim(onset_times, me * width, width, 1)
    keep = jnp.arange(NT, dtype=jnp.int32)[None, :, None] < onset[:, None, :]
    time = me * samples + jnp.arange(samples, dtype=jnp.int32)
    own_keep = time[None, :, None] < onset_times[:, None, :]

    def scatter(partial):
        return lax.psum_scatter(partial.astype(BF16), "blk", scatter_dimension=3, tiled=True).astype(BF16)

    def gather(block):
        return lax.all_gather(block, "blk", axis=3, tiled=True)

    start = scatter(analyze(plus_start, own_forward))
    spectrum = start
    for iteration in range(ITERS):
        real = contract("wrs,wpr->wps", reflection[0], spectrum[:, 0]) - contract(
            "wrs,wpr->wps", reflection[1], spectrum[:, 1]
        )
        imag = contract("wrs,wpr->wps", reflection[0], spectrum[:, 1]) + contract(
            "wrs,wpr->wps", reflection[1], spectrum[:, 0]
        )
        upgoing_spec = scatter(jnp.stack([real, imag], axis=1))
        kept = jnp.where(keep, synthesize(upgoing_spec, inverse), 0.0).astype(BF16)
        minus = gather(analyze(kept, forward).astype(BF16))
        real = contract("wrs,wps->wpr", reflection[0], minus[:, 0]) + contract(
            "wrs,wps->wpr", reflection[1], minus[:, 1]
        )
        imag = contract("wrs,wps->wpr", reflection[0], minus[:, 1]) - contract(
            "wrs,wps->wpr", reflection[1], minus[:, 0]
        )
        downgoing_spec = jnp.stack([real, imag], axis=1).astype(BF16)
        if iteration + 1 < ITERS:
            kept = jnp.where(keep, synthesize(downgoing_spec, inverse), 0.0).astype(BF16)
            spectrum = (start.astype(F32) + analyze(kept, forward)).astype(BF16)
    upgoing = jnp.where(own_keep, synthesize(gather(upgoing_spec), own_inverse), 0.0).astype(BF16)
    change = jnp.where(own_keep, synthesize(gather(downgoing_spec), own_inverse), 0.0)
    return upgoing, (plus_start.astype(F32) + change).astype(BF16)


def solution(mesh):
    size = mesh.shape["blk"]

    def run(plus_start, reflection, onset_times):
        width = reflection.shape[2] // size
        fits = width == LANES and size % 4 == 0 and (plus_start.shape[1] // size) % 16 == 0
        return jax.shard_map(
            local if fits else local_any,
            mesh=mesh,
            in_specs=(P("groups", "blk", None), P(None, None, "blk", None), P("groups", None)),
            out_specs=(P("groups", "blk", None), P("groups", "blk", None)),
            check_vma=False,
        )(plus_start, reflection, onset_times)

    return run
```

```python
import functools
import math

import jax
import jax.numpy as jnp
from jax import lax
from jax.experimental import pallas as pl
from jax.experimental.pallas import tpu as pltpu
from jax.sharding import PartitionSpec as P

NT = 512
NFW = 32
FREQ0 = 16
ITERS = 2
LANES = 128
F32 = jnp.float32
BF16 = jnp.bfloat16


def basis_of(samples):
    freqs = FREQ0 + jnp.arange(NFW, dtype=jnp.int32)
    turns = freqs[:, None] * samples[None, :] % NT
    phase = turns.astype(F32) * (2.0 * math.pi / NT)
    return jnp.stack([jnp.cos(phase), -jnp.sin(phase)], axis=1)


def tables_of(samples):
    basis = basis_of(samples).reshape(2 * NFW, samples.shape[0])
    forward = (basis * (1.0 / math.sqrt(NT))).astype(BF16)
    inverse = (basis * math.sqrt(2.0 / NFW)).astype(BF16)
    return forward, inverse.T


class Places:
    def __init__(self, axis, size):
        self.axis = axis
        self.size = size
        self.line = size // 4

    def core(self):
        return [(b, b ^ 1) for b in range(self.size)]

    def pair(self):
        return [(b, b ^ 2) for b in range(self.size)]

    def shift(self, step):
        return [(b, (b // 4 + step) % self.line * 4 + b % 4) for b in range(self.size)]

    def send(self, array, pairs):
        return lax.ppermute(array, self.axis, pairs)


def own_place(line):
    me = lax.axis_index("blk")
    return me, me // 4, (me // 2) % 2, me % 2


def chip_columns(line, ahead, flip, step):
    _, l, m, _ = own_place(line)
    other = lax.rem(l + step, line) if ahead else lax.rem(l - step + line, line)
    chip = other * 2 + (lax.rem(m + flip, 2))
    return pl.multiple_of(chip * (2 * LANES), 2 * LANES)


def relative(line):
    return [(flip, step) for flip in range(2) for step in range(line)]


def split_cores(core, block):
    low, high = block[:, :LANES], block[:, LANES:]
    first = core == 0
    return jnp.where(first, low, high), jnp.where(first, high, low)


def join_cores(core, own, other):
    first = core == 0
    return jnp.concatenate([jnp.where(first, own, other), jnp.where(first, other, own)], axis=1)


def analysis_kernel(line, rows, forward_ref, plus_ref, keep0, keep1, send0, send1):
    core = own_place(line)[3]
    keep, send = (keep0, keep1), (send0, send1)
    for p in range(rows):
        for flip, step in relative(line):
            columns = pl.ds(chip_columns(line, True, flip, step), 2 * LANES)
            block = jnp.dot(forward_ref[...], plus_ref[p, :, columns], preferred_element_type=F32)
            mine, theirs = split_cores(core, block.astype(BF16))
            keep[flip][step, p] = mine
            send[flip][step, p] = theirs


def first_analysis(plus_start, forward, line):
    focal, samples, width = plus_start.shape
    rows = 4
    out = jax.ShapeDtypeStruct((line, focal, 2 * NFW, LANES), BF16)
    out_spec = pl.BlockSpec((line, rows, 2 * NFW, LANES), lambda i: (0, i, 0, 0))
    return pl.pallas_call(
        functools.partial(analysis_kernel, line, rows),
        grid=(focal // rows,),
        in_specs=[
            pl.BlockSpec((2 * NFW, samples), lambda i: (0, 0)),
            pl.BlockSpec((rows, samples, width), lambda i: (i, 0, 0)),
        ],
        out_specs=[out_spec] * 4,
        out_shape=[out] * 4,
        compiler_params=pltpu.CompilerParams(vmem_limit_bytes=16 << 20),
        cost_estimate=pl.CostEstimate(
            flops=4 * NFW * focal * samples * width,
            bytes_accessed=2 * focal * samples * width + 4 * NFW * focal * width,
            transcendentals=0,
        ),
        name="first_analysis",
    )(forward, plus_start)


def convolve_kernel(line, flip, spec_ref, panel_ref, keep, send):
    core = own_place(line)[3]
    focal = spec_ref.shape[2]

    def body(w, carry):
        real, imag = spec_ref[w, 0], spec_ref[w, 1]
        left = jnp.concatenate(
            [jnp.concatenate([real, -imag], axis=1), jnp.concatenate([imag, real], axis=1)], axis=0
        )
        for step in range(line):
            columns = pl.ds(chip_columns(line, True, flip, step), 2 * LANES)
            panel = panel_ref[:, w, :, columns].reshape(2 * LANES, 2 * LANES)
            block = jnp.dot(left, panel, preferred_element_type=F32)
            mine, theirs = split_cores(core, block.astype(BF16))
            keep[step, w] = mine.reshape(2, focal, LANES)
            send[step, w] = theirs.reshape(2, focal, LANES)
        return carry

    lax.fori_loop(0, NFW, body, 0, unroll=2)


VMEM = pl.BlockSpec(memory_space=pltpu.VMEM)
SMALL = pltpu.CompilerParams(vmem_limit_bytes=12 << 20)


def hold_kernel(parts, source, target, sems):
    depth = source.shape[1] // parts
    copies = [
        pltpu.make_async_copy(
            source.at[:, pl.ds(i * depth, depth)], target.at[:, pl.ds(i * depth, depth)], sems.at[i]
        )
        for i in range(parts)
    ]
    for copy in copies:
        copy.start()
    for copy in copies:
        copy.wait()


def hold(reflection):
    parts = 8
    return pl.pallas_call(
        functools.partial(hold_kernel, parts),
        in_specs=[pl.BlockSpec(memory_space=pl.ANY)],
        out_specs=VMEM,
        out_shape=jax.ShapeDtypeStruct(reflection.shape, reflection.dtype),
        scratch_shapes=[pltpu.SemaphoreType.DMA((parts,))],
        compiler_params=SMALL,
        cost_estimate=pl.CostEstimate(flops=0, bytes_accessed=2 * reflection.size, transcendentals=0),
        name="hold",
    )(reflection)


def panel_cost(focal, sources):
    return pl.CostEstimate(
        flops=8 * NFW * focal * LANES * sources,
        bytes_accessed=4 * NFW * sources * (LANES + focal),
        transcendentals=0,
    )


def convolve(spectrum, reflection, line, flip):
    focal = spectrum.shape[2]
    out = jax.ShapeDtypeStruct((line, NFW, 2, focal, LANES), BF16)
    return pl.pallas_call(
        functools.partial(convolve_kernel, line, flip),
        in_specs=[VMEM] * 2,
        out_specs=[VMEM] * 2,
        out_shape=[out] * 2,
        compiler_params=SMALL,
        cost_estimate=panel_cost(focal, reflection.shape[3] // 2),
        name=f"convolve{flip}",
    )(spectrum, reflection)


def correlate_kernel(line, flip, has_base, *refs):
    core = own_place(line)[3]
    own, other, panel_ref = refs[:line], refs[line : 2 * line], refs[2 * line]
    base_ref = refs[2 * line + 1] if has_base else None
    out_ref = refs[-1]
    focal = out_ref.shape[2]

    def body(w, carry):
        total = jnp.zeros((2 * LANES, 2 * focal), F32)
        for step in range(line):
            columns = pl.ds(chip_columns(line, False, flip, step), 2 * LANES)
            panel = panel_ref[:, w, :, columns].reshape(2 * LANES, 2 * LANES)
            spec = join_cores(
                core, own[step][w].reshape(2 * focal, LANES), other[step][w].reshape(2 * focal, LANES)
            )
            total += lax.dot_general(panel, spec, (((1,), (1,)), ((), ())), preferred_element_type=F32)
        total = total.T
        real = total[:focal, :LANES] + total[focal:, LANES:]
        imag = total[focal:, :LANES] - total[:focal, LANES:]
        if has_base:
            real += base_ref[w, 0]
            imag += base_ref[w, 1]
        out_ref[w, 0] = real
        out_ref[w, 1] = imag
        return carry

    lax.fori_loop(0, NFW, body, 0, unroll=2)


def correlate(own, other, reflection, line, flip, base=None):
    focal = own[0].shape[2]
    more = [] if base is None else [base]
    return pl.pallas_call(
        functools.partial(correlate_kernel, line, flip, bool(more)),
        in_specs=[VMEM] * (2 * line + 1 + len(more)),
        out_specs=VMEM,
        out_shape=jax.ShapeDtypeStruct((NFW, 2, focal, LANES), F32),
        compiler_params=SMALL,
        cost_estimate=panel_cost(focal, reflection.shape[3] // 2),
        name=f"correlate{flip}",
    )(*own, *other, reflection, *more)


def window_kernel(parts, has_base, want_spec, *refs):
    refs = list(refs)
    forward_ref, inverse_ref, onset_ref = refs[:3]
    part_refs = refs[3 : 3 + parts]
    rest = refs[3 + parts :]
    base_ref = rest.pop(0) if has_base else None
    out_ref = rest.pop(0)
    spec_ref = rest.pop(0) if want_spec else None
    held, result = rest
    focal = out_ref.shape[2]
    k = 2 * NFW
    total = part_refs[0][...].astype(F32)
    for ref in part_refs[1:]:
        total += ref[...].astype(F32)
    held[...] = total.reshape(k * focal, LANES)
    me = lax.axis_index("blk")
    columns = pl.ds(pl.multiple_of(me * LANES, LANES), LANES)
    time = lax.broadcasted_iota(jnp.int32, (NT, 2 * LANES), 0)
    for p in range(0, focal, 2):
        pair = [held[pl.ds(p + q, k, stride=focal), :].astype(BF16) for q in range(2)]
        if spec_ref is not None:
            for q in range(2):
                spec_ref[p + q] = pair[q]
        field = jnp.dot(inverse_ref[...], jnp.concatenate(pair, axis=1), preferred_element_type=F32)
        onset = jnp.concatenate([onset_ref[p + q : p + q + 1, columns] for q in range(2)], axis=1)
        kept = jnp.where(time < onset, field, 0.0).astype(BF16)
        spectrum = jnp.dot(forward_ref[...], kept, preferred_element_type=F32)
        for q in range(2):
            result[pl.ds(p + q, k, stride=focal), :] = spectrum[:, q * LANES : (q + 1) * LANES]
    final = result[...].reshape(NFW, 2, focal, LANES)
    if base_ref is not None:
        final += base_ref[...].astype(F32)
    out_ref[...] = final.astype(BF16)


def window(parts, forward, inverse, onset_times, base=None, want_spec=False):
    focal = parts[0].shape[2]
    k = 2 * NFW
    operands = [forward, inverse, onset_times, *parts] + ([] if base is None else [base])
    whole = pl.BlockSpec(memory_space=pltpu.VMEM)
    out = [jax.ShapeDtypeStruct((NFW, 2, focal, LANES), BF16)]
    if want_spec:
        out.append(jax.ShapeDtypeStruct((focal, k, LANES), BF16))
    return pl.pallas_call(
        functools.partial(window_kernel, len(parts), base is not None, want_spec),
        in_specs=[whole] * len(operands),
        out_specs=[whole] * len(out),
        out_shape=out,
        scratch_shapes=[pltpu.VMEM((k * focal, LANES), F32)] * 2,
        compiler_params=pltpu.CompilerParams(vmem_limit_bytes=16 << 20),
        cost_estimate=pl.CostEstimate(
            flops=4 * k * NT * focal * LANES, bytes_accessed=2 * k * focal * LANES * 6, transcendentals=0
        ),
        name="window",
    )(*operands)


def field_kernel(line, rows, has_plus, *refs):
    core = own_place(line)[3]
    places = relative(line)
    inverse_ref, onset_ref = refs[:2]
    own, other = refs[2 : 2 + len(places)], refs[2 + len(places) : 2 + 2 * len(places)]
    rest = refs[2 + 2 * len(places) :]
    out_ref = rest[-1]
    samples = out_ref.shape[1]
    first = pl.program_id(0) * rows
    time = lax.axis_index("blk") * samples + lax.broadcasted_iota(jnp.int32, (samples, 2 * LANES), 0)
    for p in range(rows):
        for at, (flip, step) in enumerate(places):
            columns = pl.ds(chip_columns(line, False, flip, step), 2 * LANES)
            spec = join_cores(core, own[at][p], other[at][p])
            field = jnp.dot(inverse_ref[...], spec, preferred_element_type=F32)
            value = jnp.where(time < onset_ref[pl.ds(first + p, 1), columns], field, 0.0)
            if has_plus:
                value += rest[0][p, :, columns].astype(F32)
            out_ref[p, :, columns] = value.astype(BF16)


def field(own, other, inverse, onset_times, line, plus_start=None):
    focal, k, _ = own[0][0].shape
    samples = inverse.shape[0]
    width = onset_times.shape[1]
    rows = 4
    spec_block = pl.BlockSpec((rows, k, LANES), lambda i: (i, 0, 0))
    wide = pl.BlockSpec((rows, samples, width), lambda i: (i, 0, 0))
    own, other = sum(own, []), sum(other, [])
    plus = [] if plus_start is None else [plus_start]
    return pl.pallas_call(
        functools.partial(field_kernel, line, rows, bool(plus)),
        grid=(focal // rows,),
        in_specs=[
            pl.BlockSpec(inverse.shape, lambda i: (0, 0)),
            pl.BlockSpec(onset_times.shape, lambda i: (0, 0)),
        ]
        + [spec_block] * (len(own) + len(other))
        + [wide] * len(plus),
        out_specs=wide,
        out_shape=jax.ShapeDtypeStruct((focal, samples, width), BF16),
        compiler_params=pltpu.CompilerParams(vmem_limit_bytes=16 << 20),
        cost_estimate=pl.CostEstimate(
            flops=2 * k * focal * samples * width,
            bytes_accessed=2 * focal * width * (k + 2 * samples),
            transcendentals=0,
        ),
        name="field",
    )(inverse, onset_times, *own, *other, *plus)


def add(*parts):
    total = parts[0].astype(F32)
    for part in parts[1:]:
        total += part.astype(F32)
    return total


def after(value, *others):
    return lax.optimization_barrier((value, *others))[0]


def far_first(line):
    return sorted(range(line), key=lambda step: -min(step, line - step))


def reduce_scatter(places, keep0, keep1, send0, send1):
    got1 = places.send(send1, places.core())
    got0 = places.send(send0, places.core())
    order = far_first(places.line)
    across = {}
    ready = got1
    for step in order:
        ready = add(keep1[step], after(got1, ready)[step]).astype(BF16)
        across[step] = places.send(ready, places.pair())
    parts = [keep0[0], got0[0], across[0]]
    ready = got0
    for step in order[:-1]:
        ready = add(keep0[step], after(got0, ready)[step], across[step]).astype(BF16)
        parts.append(places.send(ready, places.shift(step)))
    return parts


def all_gather(places, block):
    near_first = far_first(places.line)[::-1]
    line = {0: block}
    for step in near_first[1:]:
        line[step] = places.send(block, places.shift(step))
    across = {step: places.send(line[step], places.pair()) for step in near_first}
    own = [[side[step] for step in range(places.line)] for side in (line, across)]
    other = [[places.send(piece, places.core()) for piece in side] for side in own]
    return own, other


def local(plus_start, reflection, onset_times):
    size = lax.axis_size("blk")
    places = Places("blk", size)
    line = places.line
    focal, samples, _ = plus_start.shape
    forward, inverse = tables_of(jnp.arange(NT, dtype=jnp.int32))
    own_samples = lax.axis_index("blk") * samples + jnp.arange(samples, dtype=jnp.int32)
    own_forward, own_inverse = tables_of(own_samples)

    parts = reduce_scatter(places, *first_analysis(plus_start, own_forward, line))
    start = add(*parts).astype(BF16)
    start = jnp.transpose(start, (1, 0, 2)).reshape(NFW, 2, focal, LANES)
    spectrum_plus = start
    reflection = hold(reflection)
    for iteration in range(ITERS):
        last = iteration + 1 == ITERS
        keep1, send1 = convolve(spectrum_plus, reflection, line, 1)
        keep0, send0 = convolve(after(spectrum_plus, keep1), reflection, line, 0)
        parts = reduce_scatter(places, keep0, keep1, send0, send1)
        windowed = window(parts, forward, inverse, onset_times, want_spec=last)
        gathered = all_gather(places, windowed[0])
        if last:
            upgoing_spec = all_gather(places, windowed[1])
        own, other = gathered
        downgoing_spec = correlate(own[0], other[0], reflection, line, 0)
        downgoing_spec = correlate(own[1], other[1], reflection, line, 1, downgoing_spec)
        if not last:
            (spectrum_plus,) = window([downgoing_spec], forward, inverse, onset_times, base=start)
    upgoing = field(*upgoing_spec, own_inverse, onset_times, line)
    final = jnp.transpose(
        downgoing_spec.astype(BF16).reshape(2 * NFW, focal, LANES), (1, 0, 2)
    )
    downgoing = field(*all_gather(places, final), own_inverse, onset_times, line, plus_start)
    return upgoing, downgoing


def analyze(values, forward):
    total = jnp.einsum("kt,ptx->kpx", forward, values, preferred_element_type=F32)
    return total.reshape(NFW, 2, values.shape[0], values.shape[2])


def synthesize(spectrum, inverse):
    flat = spectrum.reshape(2 * NFW, spectrum.shape[2], spectrum.shape[3])
    return jnp.einsum("tk,kpx->ptx", inverse, flat, preferred_element_type=F32)


def contract(form, left, right):
    return jnp.einsum(form, left, right, preferred_element_type=F32)


def local_any(plus_start, reflection, onset_times):
    samples = plus_start.shape[1]
    width = reflection.shape[2]
    me = lax.axis_index("blk")
    forward, inverse = tables_of(jnp.arange(NT, dtype=jnp.int32))
    own_forward, own_inverse = tables_of(me * samples + jnp.arange(samples, dtype=jnp.int32))
    onset = lax.dynamic_slice_in_dim(onset_times, me * width, width, 1)
    keep = jnp.arange(NT, dtype=jnp.int32)[None, :, None] < onset[:, None, :]
    time = me * samples + jnp.arange(samples, dtype=jnp.int32)
    own_keep = time[None, :, None] < onset_times[:, None, :]

    def scatter(partial):
        return lax.psum_scatter(partial.astype(BF16), "blk", scatter_dimension=3, tiled=True).astype(BF16)

    def gather(block):
        return lax.all_gather(block, "blk", axis=3, tiled=True)

    start = scatter(analyze(plus_start, own_forward))
    spectrum = start
    for iteration in range(ITERS):
        real = contract("wrs,wpr->wps", reflection[0], spectrum[:, 0]) - contract(
            "wrs,wpr->wps", reflection[1], spectrum[:, 1]
        )
        imag = contract("wrs,wpr->wps", reflection[0], spectrum[:, 1]) + contract(
            "wrs,wpr->wps", reflection[1], spectrum[:, 0]
        )
        upgoing_spec = scatter(jnp.stack([real, imag], axis=1))
        kept = jnp.where(keep, synthesize(upgoing_spec, inverse), 0.0).astype(BF16)
        minus = gather(analyze(kept, forward).astype(BF16))
        real = contract("wrs,wps->wpr", reflection[0], minus[:, 0]) + contract(
            "wrs,wps->wpr", reflection[1], minus[:, 1]
        )
        imag = contract("wrs,wps->wpr", reflection[0], minus[:, 1]) - contract(
            "wrs,wps->wpr", reflection[1], minus[:, 0]
        )
        downgoing_spec = jnp.stack([real, imag], axis=1).astype(BF16)
        if iteration + 1 < ITERS:
            kept = jnp.where(keep, synthesize(downgoing_spec, inverse), 0.0).astype(BF16)
            spectrum = (start.astype(F32) + analyze(kept, forward)).astype(BF16)
    upgoing = jnp.where(own_keep, synthesize(gather(upgoing_spec), own_inverse), 0.0).astype(BF16)
    change = jnp.where(own_keep, synthesize(gather(downgoing_spec), own_inverse), 0.0)
    return upgoing, (plus_start.astype(F32) + change).astype(BF16)


def solution(mesh):
    size = mesh.shape["blk"]

    def run(plus_start, reflection, onset_times):
        width = reflection.shape[2] // size
        fits = width == LANES and size % 4 == 0 and (plus_start.shape[1] // size) % 16 == 0
        return jax.shard_map(
            local if fits else local_any,
            mesh=mesh,
            in_specs=(P("groups", "blk", None), P(None, None, "blk", None), P("groups", None)),
            out_specs=(P("groups", "blk", None), P("groups", "blk", None)),
            check_vma=False,
        )(plus_start, reflection, onset_times)

    return run
```

```python
import functools
import math

import jax
import jax.numpy as jnp
from jax import lax
from jax.experimental import pallas as pl
from jax.experimental.pallas import tpu as pltpu
from jax.sharding import PartitionSpec as P

NT = 512
NFW = 32
FREQ0 = 16
ITERS = 2
LANES = 128
F32 = jnp.float32
BF16 = jnp.bfloat16


def basis_of(samples):
    freqs = FREQ0 + jnp.arange(NFW, dtype=jnp.int32)
    turns = freqs[:, None] * samples[None, :] % NT
    phase = turns.astype(F32) * (2.0 * math.pi / NT)
    return jnp.stack([jnp.cos(phase), -jnp.sin(phase)], axis=1)


def tables_of(samples):
    basis = basis_of(samples).reshape(2 * NFW, samples.shape[0])
    forward = (basis * (1.0 / math.sqrt(NT))).astype(BF16)
    inverse = (basis * math.sqrt(2.0 / NFW)).astype(BF16)
    return forward, inverse.T


class Places:
    def __init__(self, axis, size):
        self.axis = axis
        self.size = size
        self.line = size // 4

    def core(self):
        return [(b, b ^ 1) for b in range(self.size)]

    def pair(self):
        return [(b, b ^ 2) for b in range(self.size)]

    def shift(self, step):
        return [(b, (b // 4 + step) % self.line * 4 + b % 4) for b in range(self.size)]

    def send(self, array, pairs):
        return lax.ppermute(array, self.axis, pairs)


def own_place(line):
    me = lax.axis_index("blk")
    return me, me // 4, (me // 2) % 2, me % 2


def chip_columns(line, ahead, flip, step):
    _, l, m, _ = own_place(line)
    other = lax.rem(l + step, line) if ahead else lax.rem(l - step + line, line)
    chip = other * 2 + (lax.rem(m + flip, 2))
    return pl.multiple_of(chip * (2 * LANES), 2 * LANES)


def relative(line):
    return [(flip, step) for flip in range(2) for step in range(line)]


def split_cores(core, block):
    low, high = block[:, :LANES], block[:, LANES:]
    first = core == 0
    return jnp.where(first, low, high), jnp.where(first, high, low)


def join_cores(core, own, other):
    first = core == 0
    return jnp.concatenate([jnp.where(first, own, other), jnp.where(first, other, own)], axis=1)


def analysis_kernel(line, rows, forward_ref, plus_ref, keep0, keep1, send0, send1):
    core = own_place(line)[3]
    keep, send = (keep0, keep1), (send0, send1)
    for p in range(rows):
        for flip, step in relative(line):
            columns = pl.ds(chip_columns(line, True, flip, step), 2 * LANES)
            block = jnp.dot(forward_ref[...], plus_ref[p, :, columns], preferred_element_type=F32)
            mine, theirs = split_cores(core, block.astype(BF16))
            keep[flip][step, p] = mine
            send[flip][step, p] = theirs


def first_analysis(plus_start, forward, line):
    focal, samples, width = plus_start.shape
    rows = 4
    out = jax.ShapeDtypeStruct((line, focal, 2 * NFW, LANES), BF16)
    out_spec = pl.BlockSpec((line, rows, 2 * NFW, LANES), lambda i: (0, i, 0, 0))
    return pl.pallas_call(
        functools.partial(analysis_kernel, line, rows),
        grid=(focal // rows,),
        in_specs=[
            pl.BlockSpec((2 * NFW, samples), lambda i: (0, 0)),
            pl.BlockSpec((rows, samples, width), lambda i: (i, 0, 0)),
        ],
        out_specs=[out_spec] * 4,
        out_shape=[out] * 4,
        compiler_params=pltpu.CompilerParams(vmem_limit_bytes=16 << 20),
        cost_estimate=pl.CostEstimate(
            flops=4 * NFW * focal * samples * width,
            bytes_accessed=2 * focal * samples * width + 4 * NFW * focal * width,
            transcendentals=0,
        ),
        name="first_analysis",
    )(forward, plus_start)


def fetch_panels(line, ahead, flip, panel_ref, held, sems):
    chunks, _, _, rows = held.shape[:4]

    def copy(chunk, step):
        columns = pl.ds(chip_columns(line, ahead, flip, step), 2 * LANES)
        source = panel_ref.at[:, pl.ds(chunk * rows, rows), :, columns]
        return pltpu.make_async_copy(source, held.at[chunk, step], sems.at[chunk, step])

    for chunk in range(chunks):
        for step in range(line):
            copy(chunk, step).start()

    def wait(chunk):
        for step in range(line):
            copy(chunk, step).wait()

    return wait


CHUNKS = 8


def panel_scratch(line):
    rows = NFW // CHUNKS
    return [
        pltpu.VMEM((CHUNKS, line, 2, rows, LANES, 2 * LANES), BF16),
        pltpu.SemaphoreType.DMA((CHUNKS, line)),
    ]


def convolve_kernel(line, flip, spec_ref, panel_ref, keep, send, held, sems):
    core = own_place(line)[3]
    focal = spec_ref.shape[2]
    rows = held.shape[3]
    wait = fetch_panels(line, True, flip, panel_ref, held, sems)

    def body(chunk, carry):
        wait(chunk)
        for row in range(rows):
            w = chunk * rows + row
            real, imag = spec_ref[w, 0], spec_ref[w, 1]
            left = jnp.concatenate(
                [jnp.concatenate([real, -imag], axis=1), jnp.concatenate([imag, real], axis=1)], axis=0
            )
            for step in range(line):
                panel = held[chunk, step, :, row].reshape(2 * LANES, 2 * LANES)
                block = jnp.dot(left, panel, preferred_element_type=F32)
                mine, theirs = split_cores(core, block.astype(BF16))
                keep[step, w] = mine.reshape(2, focal, LANES)
                send[step, w] = theirs.reshape(2, focal, LANES)
        return carry

    lax.fori_loop(0, CHUNKS, body, 0)


VMEM = pl.BlockSpec(memory_space=pltpu.VMEM)
ANY = pl.BlockSpec(memory_space=pl.ANY)
MEDIUM = pltpu.CompilerParams(vmem_limit_bytes=24 << 20)


def panel_cost(focal, sources):
    return pl.CostEstimate(
        flops=8 * NFW * focal * LANES * sources,
        bytes_accessed=4 * NFW * sources * (LANES + focal),
        transcendentals=0,
    )


def convolve(spectrum, reflection, line, flip):
    focal = spectrum.shape[2]
    out = jax.ShapeDtypeStruct((line, NFW, 2, focal, LANES), BF16)
    return pl.pallas_call(
        functools.partial(convolve_kernel, line, flip),
        in_specs=[VMEM, ANY],
        out_specs=[VMEM] * 2,
        out_shape=[out] * 2,
        scratch_shapes=panel_scratch(line),
        compiler_params=MEDIUM,
        cost_estimate=panel_cost(focal, reflection.shape[3] // 2),
        name=f"convolve{flip}",
    )(spectrum, reflection)


def correlate_kernel(line, flip, has_base, final, *refs):
    core = own_place(line)[3]
    own, other, panel_ref = refs[:line], refs[line : 2 * line], refs[2 * line]
    base_ref = refs[2 * line + 1] if has_base else None
    out_ref, held, sems, *spare = refs[2 * line + 1 + has_base :]
    focal = own[0].shape[2]
    rows = held.shape[3]
    wait = fetch_panels(line, False, flip, panel_ref, held, sems)

    def body(chunk, carry):
        wait(chunk)
        for row in range(rows):
            w = chunk * rows + row
            total = jnp.zeros((2 * focal, 2 * LANES), F32)
            for step in range(line):
                panel = held[chunk, step, :, row].reshape(2 * LANES, 2 * LANES)
                spec = join_cores(
                    core, own[step][w].reshape(2 * focal, LANES), other[step][w].reshape(2 * focal, LANES)
                )
                total += lax.dot_general(spec, panel, (((1,), (1,)), ((), ())), preferred_element_type=F32)
            real = total[:focal, :LANES] + total[focal:, LANES:]
            imag = total[focal:, :LANES] - total[:focal, LANES:]
            if has_base:
                real += base_ref[w, 0]
                imag += base_ref[w, 1]
            if final:
                spare[0][pl.ds(2 * w * focal, focal), :] = real
                spare[0][pl.ds((2 * w + 1) * focal, focal), :] = imag
            else:
                out_ref[w, 0] = real
                out_ref[w, 1] = imag
        return carry

    lax.fori_loop(0, CHUNKS, body, 0)
    if final:
        for p in range(focal):
            out_ref[p] = spare[0][pl.ds(p, 2 * NFW, stride=focal), :].astype(BF16)


def correlate(own, other, reflection, line, flip, base=None, final=False):
    focal = own[0].shape[2]
    more = [] if base is None else [base]
    shape = jax.ShapeDtypeStruct((NFW, 2, focal, LANES), F32)
    if final:
        shape = jax.ShapeDtypeStruct((focal, 2 * NFW, LANES), BF16)
    spare = [pltpu.VMEM((2 * NFW * focal, LANES), F32)] if final else []
    return pl.pallas_call(
        functools.partial(correlate_kernel, line, flip, bool(more), final),
        in_specs=[VMEM] * (2 * line) + [ANY] + [VMEM] * len(more),
        out_specs=VMEM,
        out_shape=shape,
        scratch_shapes=panel_scratch(line) + spare,
        compiler_params=MEDIUM,
        cost_estimate=panel_cost(focal, reflection.shape[3] // 2),
        name=f"correlate{flip}",
    )(*own, *other, reflection, *more)


def windowed_spectrum(pair, onset, forward, inverse):
    time = lax.broadcasted_iota(jnp.int32, (NT, 2 * LANES), 0)
    values = jnp.dot(inverse, jnp.concatenate(pair, axis=1), preferred_element_type=F32)
    kept = jnp.where(time < jnp.concatenate(onset, axis=1), values, 0.0).astype(BF16)
    return jnp.dot(forward, kept, preferred_element_type=F32)


def window_kernel(parts, has_base, want_spec, *refs):
    refs = list(refs)
    forward_ref, inverse_ref, onset_ref = refs[:3]
    part_refs = refs[3 : 3 + parts]
    rest = refs[3 + parts :]
    base_ref = rest.pop(0) if has_base else None
    out_ref = rest.pop(0)
    held, result = rest
    focal = part_refs[0].shape[2]
    k = 2 * NFW
    total = part_refs[0][...].astype(F32)
    for ref in part_refs[1:]:
        total += ref[...].astype(F32)
    held[...] = total.reshape(k * focal, LANES)
    me = lax.axis_index("blk")
    columns = pl.ds(pl.multiple_of(me * LANES, LANES), LANES)
    if want_spec:
        for p in range(focal):
            out_ref[p] = held[pl.ds(p, k, stride=focal), :].astype(BF16)
        return
    for p in range(0, focal, 2):
        pair = [held[pl.ds(p + q, k, stride=focal), :].astype(BF16) for q in range(2)]
        onset = [onset_ref[p + q : p + q + 1, columns] for q in range(2)]
        spectrum = windowed_spectrum(pair, onset, forward_ref[...], inverse_ref[...])
        for q in range(2):
            result[pl.ds(p + q, k, stride=focal), :] = spectrum[:, q * LANES : (q + 1) * LANES]
    final = result[...].reshape(NFW, 2, focal, LANES)
    if base_ref is not None:
        final += base_ref[...].astype(F32)
    out_ref[...] = final.astype(BF16)


def window(parts, forward, inverse, onset_times, base=None, want_spec=False):
    focal = parts[0].shape[2]
    k = 2 * NFW
    operands = [forward, inverse, onset_times, *parts] + ([] if base is None else [base])
    out = jax.ShapeDtypeStruct((NFW, 2, focal, LANES), BF16)
    if want_spec:
        out = jax.ShapeDtypeStruct((focal, k, LANES), BF16)
    return pl.pallas_call(
        functools.partial(window_kernel, len(parts), base is not None, want_spec),
        in_specs=[VMEM] * len(operands),
        out_specs=VMEM,
        out_shape=out,
        scratch_shapes=[pltpu.VMEM((k * focal, LANES), F32)] * 2,
        compiler_params=pltpu.CompilerParams(vmem_limit_bytes=16 << 20),
        cost_estimate=pl.CostEstimate(
            flops=4 * k * NT * focal * LANES, bytes_accessed=2 * k * focal * LANES * 6, transcendentals=0
        ),
        name="window",
    )(*operands)


def window_at_kernel(line, flip, step, forward_ref, inverse_ref, onset_ref, spec_ref, out_ref, result):
    core = own_place(line)[3]
    focal, k, _ = spec_ref.shape
    start = chip_columns(line, False, flip, step) + core * LANES
    columns = pl.ds(pl.multiple_of(start, LANES), LANES)
    for p in range(0, focal, 2):
        onset = [onset_ref[p + q : p + q + 1, columns] for q in range(2)]
        pair = [spec_ref[p + q] for q in range(2)]
        spectrum = windowed_spectrum(pair, onset, forward_ref[...], inverse_ref[...])
        for q in range(2):
            result[pl.ds(p + q, k, stride=focal), :] = spectrum[:, q * LANES : (q + 1) * LANES]
    out_ref[...] = result[...].reshape(NFW, 2, focal, LANES).astype(BF16)


def window_at(spec, forward, inverse, onset_times, line, flip, step):
    focal, k, _ = spec.shape
    return pl.pallas_call(
        functools.partial(window_at_kernel, line, flip, step),
        in_specs=[VMEM] * 4,
        out_specs=VMEM,
        out_shape=jax.ShapeDtypeStruct((NFW, 2, focal, LANES), BF16),
        scratch_shapes=[pltpu.VMEM((k * focal, LANES), F32)],
        compiler_params=pltpu.CompilerParams(vmem_limit_bytes=16 << 20),
        cost_estimate=pl.CostEstimate(
            flops=4 * k * NT * focal * LANES, bytes_accessed=2 * k * focal * LANES * 6, transcendentals=0
        ),
        name="window_at",
    )(forward, inverse, onset_times, spec)


def field_kernel(line, rows, has_plus, *refs):
    core = own_place(line)[3]
    places = relative(line)
    inverse_ref, onset_ref = refs[:2]
    own, other = refs[2 : 2 + len(places)], refs[2 + len(places) : 2 + 2 * len(places)]
    rest = refs[2 + 2 * len(places) :]
    out_ref = rest[-1]
    samples = out_ref.shape[1]
    first = pl.program_id(0) * rows
    time = lax.axis_index("blk") * samples + lax.broadcasted_iota(jnp.int32, (samples, 2 * LANES), 0)
    for p in range(rows):
        for at, (flip, step) in enumerate(places):
            columns = pl.ds(chip_columns(line, False, flip, step), 2 * LANES)
            spec = join_cores(core, own[at][p], other[at][p])
            field = jnp.dot(inverse_ref[...], spec, preferred_element_type=F32)
            value = jnp.where(time < onset_ref[pl.ds(first + p, 1), columns], field, 0.0)
            if has_plus:
                value += rest[0][p, :, columns].astype(F32)
            out_ref[p, :, columns] = value.astype(BF16)


def field(own, other, inverse, onset_times, line, plus_start=None):
    focal, k, _ = own[0][0].shape
    samples = inverse.shape[0]
    width = onset_times.shape[1]
    rows = 4
    spec_block = pl.BlockSpec((rows, k, LANES), lambda i: (i, 0, 0))
    wide = pl.BlockSpec((rows, samples, width), lambda i: (i, 0, 0))
    own, other = sum(own, []), sum(other, [])
    plus = [] if plus_start is None else [plus_start]
    return pl.pallas_call(
        functools.partial(field_kernel, line, rows, bool(plus)),
        grid=(focal // rows,),
        in_specs=[
            pl.BlockSpec(inverse.shape, lambda i: (0, 0)),
            pl.BlockSpec(onset_times.shape, lambda i: (0, 0)),
        ]
        + [spec_block] * (len(own) + len(other))
        + [wide] * len(plus),
        out_specs=wide,
        out_shape=jax.ShapeDtypeStruct((focal, samples, width), BF16),
        compiler_params=pltpu.CompilerParams(vmem_limit_bytes=40 << 20),
        cost_estimate=pl.CostEstimate(
            flops=2 * k * focal * samples * width,
            bytes_accessed=2 * focal * width * (k + 2 * samples),
            transcendentals=0,
        ),
        name="field",
    )(inverse, onset_times, *own, *other, *plus)


def add(*parts):
    total = parts[0].astype(F32)
    for part in parts[1:]:
        total += part.astype(F32)
    return total


def after(value, *others):
    return lax.optimization_barrier((value, *others))[0]


def far_first(line):
    return sorted(range(line), key=lambda step: -min(step, line - step))


def across_pair(places, keep, send):
    got = places.send(send, places.core())
    across = {}
    for step in far_first(places.line):
        across[step] = places.send(add(keep[step], got[step]).astype(BF16), places.pair())
    return got, across


def along_line(places, keep, send, across):
    got = places.send(send, places.core())
    parts = [keep[0], got[0], across[0]]
    ready = got
    for step in far_first(places.line)[:-1]:
        ready = add(keep[step], after(got, ready)[step], across[step]).astype(BF16)
        parts.append(places.send(ready, places.shift(step)))
    return parts


def gather_chips(places, block):
    near_first = far_first(places.line)[::-1]
    line, across = {0: block}, {}
    ready = block
    for step in near_first[1:]:
        away = min(step, places.line - step)
        ready = block if away == 1 else after(block, line[near_first[1]])
        line[step] = places.send(ready, places.shift(step))
    for step in near_first:
        across[step] = places.send(line[step], places.pair())
    return [[side[step] for step in range(places.line)] for side in (line, across)]


def other_cores(places, sides):
    return [[places.send(piece, places.core()) for piece in side] for side in sides]


def local(plus_start, reflection, onset_times):
    size = lax.axis_size("blk")
    places = Places("blk", size)
    line = places.line
    focal, samples, _ = plus_start.shape
    forward, inverse = tables_of(jnp.arange(NT, dtype=jnp.int32))
    own_samples = lax.axis_index("blk") * samples + jnp.arange(samples, dtype=jnp.int32)
    own_forward, own_inverse = tables_of(own_samples)

    keep0, keep1, send0, send1 = first_analysis(plus_start, own_forward, line)
    _, across = across_pair(places, keep1, send1)
    start = add(*along_line(places, keep0, send0, across)).astype(BF16)
    start = jnp.transpose(start, (1, 0, 2)).reshape(NFW, 2, focal, LANES)
    spectrum_plus = start
    for iteration in range(ITERS):
        last = iteration + 1 == ITERS
        keep1, send1 = convolve(spectrum_plus, reflection, line, 1)
        got1, across = across_pair(places, keep1, send1)
        keep0, send0 = convolve(after(spectrum_plus, got1), reflection, line, 0)
        parts = along_line(places, keep0, send0, across)
        if last:
            upgoing_spec = gather_chips(
                places, window(parts, forward, inverse, onset_times, want_spec=True)
            )
            own = [
                [
                    window_at(piece, forward, inverse, onset_times, line, flip, step)
                    for step, piece in enumerate(side)
                ]
                for flip, side in enumerate(upgoing_spec)
            ]
        else:
            own = gather_chips(places, window(parts, forward, inverse, onset_times))
        other = other_cores(places, own)
        downgoing_spec = correlate(own[0], other[0], reflection, line, 0)
        downgoing_spec = correlate(own[1], other[1], reflection, line, 1, downgoing_spec, last)
        if not last:
            spectrum_plus = window([downgoing_spec], forward, inverse, onset_times, base=start)
    other = other_cores(places, upgoing_spec)
    upgoing = field(upgoing_spec, other, own_inverse, onset_times, line)
    own = gather_chips(places, downgoing_spec)
    downgoing = field(own, other_cores(places, own), own_inverse, onset_times, line, plus_start)
    return upgoing, downgoing


def analyze(values, forward):
    total = jnp.einsum("kt,ptx->kpx", forward, values, preferred_element_type=F32)
    return total.reshape(NFW, 2, values.shape[0], values.shape[2])


def synthesize(spectrum, inverse):
    flat = spectrum.reshape(2 * NFW, spectrum.shape[2], spectrum.shape[3])
    return jnp.einsum("tk,kpx->ptx", inverse, flat, preferred_element_type=F32)


def contract(form, left, right):
    return jnp.einsum(form, left, right, preferred_element_type=F32)


def local_any(plus_start, reflection, onset_times):
    samples = plus_start.shape[1]
    width = reflection.shape[2]
    me = lax.axis_index("blk")
    forward, inverse = tables_of(jnp.arange(NT, dtype=jnp.int32))
    own_forward, own_inverse = tables_of(me * samples + jnp.arange(samples, dtype=jnp.int32))
    onset = lax.dynamic_slice_in_dim(onset_times, me * width, width, 1)
    keep = jnp.arange(NT, dtype=jnp.int32)[None, :, None] < onset[:, None, :]
    time = me * samples + jnp.arange(samples, dtype=jnp.int32)
    own_keep = time[None, :, None] < onset_times[:, None, :]

    def scatter(partial):
        return lax.psum_scatter(partial.astype(BF16), "blk", scatter_dimension=3, tiled=True).astype(BF16)

    def gather(block):
        return lax.all_gather(block, "blk", axis=3, tiled=True)

    start = scatter(analyze(plus_start, own_forward))
    spectrum = start
    for iteration in range(ITERS):
        real = contract("wrs,wpr->wps", reflection[0], spectrum[:, 0]) - contract(
            "wrs,wpr->wps", reflection[1], spectrum[:, 1]
        )
        imag = contract("wrs,wpr->wps", reflection[0], spectrum[:, 1]) + contract(
            "wrs,wpr->wps", reflection[1], spectrum[:, 0]
        )
        upgoing_spec = scatter(jnp.stack([real, imag], axis=1))
        kept = jnp.where(keep, synthesize(upgoing_spec, inverse), 0.0).astype(BF16)
        minus = gather(analyze(kept, forward).astype(BF16))
        real = contract("wrs,wps->wpr", reflection[0], minus[:, 0]) + contract(
            "wrs,wps->wpr", reflection[1], minus[:, 1]
        )
        imag = contract("wrs,wps->wpr", reflection[0], minus[:, 1]) - contract(
            "wrs,wps->wpr", reflection[1], minus[:, 0]
        )
        downgoing_spec = jnp.stack([real, imag], axis=1).astype(BF16)
        if iteration + 1 < ITERS:
            kept = jnp.where(keep, synthesize(downgoing_spec, inverse), 0.0).astype(BF16)
            spectrum = (start.astype(F32) + analyze(kept, forward)).astype(BF16)
    upgoing = jnp.where(own_keep, synthesize(gather(upgoing_spec), own_inverse), 0.0).astype(BF16)
    change = jnp.where(own_keep, synthesize(gather(downgoing_spec), own_inverse), 0.0)
    return upgoing, (plus_start.astype(F32) + change).astype(BF16)


def solution(mesh):
    size = mesh.shape["blk"]

    def run(plus_start, reflection, onset_times):
        width = reflection.shape[2] // size
        fits = width == LANES and size % 4 == 0 and (plus_start.shape[1] // size) % 16 == 0
        return jax.shard_map(
            local if fits else local_any,
            mesh=mesh,
            in_specs=(P("groups", "blk", None), P(None, None, "blk", None), P("groups", None)),
            out_specs=(P("groups", "blk", None), P("groups", "blk", None)),
            check_vma=False,
        )(plus_start, reflection, onset_times)

    return run
```

```python
import functools
import math

import jax
import jax.numpy as jnp
from jax import lax
from jax.experimental import pallas as pl
from jax.experimental.pallas import tpu as pltpu
from jax.sharding import PartitionSpec as P

NT = 512
NFW = 32
FREQ0 = 16
ITERS = 2
LANES = 128
F32 = jnp.float32
BF16 = jnp.bfloat16


def basis_of(samples):
    freqs = FREQ0 + jnp.arange(NFW, dtype=jnp.int32)
    turns = freqs[:, None] * samples[None, :] % NT
    phase = turns.astype(F32) * (2.0 * math.pi / NT)
    return jnp.stack([jnp.cos(phase), -jnp.sin(phase)], axis=1)


def tables_of(samples):
    basis = basis_of(samples).reshape(2 * NFW, samples.shape[0])
    forward = (basis * (1.0 / math.sqrt(NT))).astype(BF16)
    inverse = (basis * math.sqrt(2.0 / NFW)).astype(BF16)
    return forward, inverse.T


class Places:
    def __init__(self, axis, size):
        self.axis = axis
        self.size = size
        self.line = size // 4

    def core(self):
        return [(b, b ^ 1) for b in range(self.size)]

    def pair(self):
        return [(b, b ^ 2) for b in range(self.size)]

    def shift(self, step):
        return [(b, (b // 4 + step) % self.line * 4 + b % 4) for b in range(self.size)]

    def send(self, array, pairs):
        return lax.ppermute(array, self.axis, pairs)


def own_place(line):
    me = lax.axis_index("blk")
    return me, me // 4, (me // 2) % 2, me % 2


def chip_columns(line, ahead, flip, step):
    _, l, m, _ = own_place(line)
    other = lax.rem(l + step, line) if ahead else lax.rem(l - step + line, line)
    chip = other * 2 + (lax.rem(m + flip, 2))
    return pl.multiple_of(chip * (2 * LANES), 2 * LANES)


def relative(line):
    return [(flip, step) for flip in range(2) for step in range(line)]


def split_cores(core, block):
    low, high = block[:, :LANES], block[:, LANES:]
    first = core == 0
    return jnp.where(first, low, high), jnp.where(first, high, low)


def join_cores(core, own, other):
    first = core == 0
    return jnp.concatenate([jnp.where(first, own, other), jnp.where(first, other, own)], axis=1)


VMEM = pl.BlockSpec(memory_space=pltpu.VMEM)
ANY = pl.BlockSpec(memory_space=pl.ANY)
CHUNKS = 8
STRIPS = 4


def limit(mebibytes):
    return pltpu.CompilerParams(vmem_limit_bytes=mebibytes << 20)


def strip_copies(source, target, sems, strips):
    rows = source.shape[0] // strips

    def copy(strip):
        part = pl.ds(strip * rows, rows)
        return pltpu.make_async_copy(source.at[part], target.at[part], sems.at[strip])

    return copy, rows


def analysis_kernel(line, forward_ref, plus_ref, keep0, keep1, send0, send1, held, sems):
    core = own_place(line)[3]
    keep, send = (keep0, keep1), (send0, send1)
    copy, rows = strip_copies(plus_ref, held, sems, STRIPS)
    for strip in range(STRIPS):
        copy(strip).start()

    def body(strip, carry):
        copy(strip).wait()
        for row in range(rows):
            p = strip * rows + row
            for flip, step in relative(line):
                columns = pl.ds(chip_columns(line, True, flip, step), 2 * LANES)
                block = jnp.dot(forward_ref[...], held[p, :, columns], preferred_element_type=F32)
                mine, theirs = split_cores(core, block.astype(BF16))
                keep[flip][step, p] = mine
                send[flip][step, p] = theirs
        return carry

    lax.fori_loop(0, STRIPS, body, 0)


def first_analysis(plus_start, forward, line):
    focal, samples, width = plus_start.shape
    out = jax.ShapeDtypeStruct((line, focal, 2 * NFW, LANES), BF16)
    return pl.pallas_call(
        functools.partial(analysis_kernel, line),
        in_specs=[VMEM, ANY],
        out_specs=[VMEM] * 4,
        out_shape=[out] * 4,
        scratch_shapes=[pltpu.VMEM(plus_start.shape, BF16), pltpu.SemaphoreType.DMA((STRIPS,))],
        compiler_params=limit(8),
        cost_estimate=pl.CostEstimate(
            flops=4 * NFW * focal * samples * width,
            bytes_accessed=2 * focal * samples * width + 4 * NFW * focal * width,
            transcendentals=0,
        ),
        name="first_analysis",
    )(forward, plus_start)


def fetch_panels(line, ahead, flip, panel_ref, held, sems):
    chunks, _, _, rows = held.shape[:4]

    def copy(chunk, step):
        columns = pl.ds(chip_columns(line, ahead, flip, step), 2 * LANES)
        source = panel_ref.at[:, pl.ds(chunk * rows, rows), :, columns]
        return pltpu.make_async_copy(source, held.at[chunk, step], sems.at[chunk, step])

    for chunk in range(chunks):
        for step in range(line):
            copy(chunk, step).start()

    def wait(chunk):
        for step in range(line):
            copy(chunk, step).wait()

    return wait


def panel_scratch(line):
    rows = NFW // CHUNKS
    return [
        pltpu.VMEM((CHUNKS, line, 2, rows, LANES, 2 * LANES), BF16),
        pltpu.SemaphoreType.DMA((CHUNKS, line)),
    ]


def convolve_kernel(line, spec_ref, panel_ref, keep0, keep1, send0, send1, held, sems):
    core = own_place(line)[3]
    keep, send = (keep0, keep1), (send0, send1)
    focal = spec_ref.shape[2]
    rows = NFW // CHUNKS

    def copy(chunk):
        part = pl.ds(chunk * rows, rows)
        return pltpu.make_async_copy(panel_ref.at[:, part], held.at[:, part], sems.at[chunk])

    for chunk in range(CHUNKS):
        copy(chunk).start()

    def body(chunk, carry):
        copy(chunk).wait()
        for row in range(rows):
            w = chunk * rows + row
            real, imag = spec_ref[w, 0], spec_ref[w, 1]
            left = jnp.concatenate(
                [jnp.concatenate([real, -imag], axis=1), jnp.concatenate([imag, real], axis=1)], axis=0
            )
            for flip, step in relative(line):
                columns = pl.ds(chip_columns(line, True, flip, step), 2 * LANES)
                panel = held[:, w, :, columns].reshape(2 * LANES, 2 * LANES)
                block = jnp.dot(left, panel, preferred_element_type=F32)
                mine, theirs = split_cores(core, block.astype(BF16))
                keep[flip][step, w] = mine.reshape(2, focal, LANES)
                send[flip][step, w] = theirs.reshape(2, focal, LANES)
        return carry

    lax.fori_loop(0, CHUNKS, body, 0)


def panel_cost(focal, sources):
    return pl.CostEstimate(
        flops=8 * NFW * focal * LANES * sources,
        bytes_accessed=4 * NFW * sources * (LANES + focal),
        transcendentals=0,
    )


def convolve(spectrum, reflection, line):
    focal = spectrum.shape[2]
    out = jax.ShapeDtypeStruct((line, NFW, 2, focal, LANES), BF16)
    return pl.pallas_call(
        functools.partial(convolve_kernel, line),
        in_specs=[VMEM, ANY],
        out_specs=[VMEM] * 4,
        out_shape=[out] * 4,
        scratch_shapes=[pltpu.VMEM(reflection.shape, BF16), pltpu.SemaphoreType.DMA((CHUNKS,))],
        compiler_params=limit(36),
        cost_estimate=panel_cost(focal, reflection.shape[3]),
        name="convolve",
    )(spectrum, reflection)


def correlate_kernel(line, flip, has_base, final, *refs):
    core = own_place(line)[3]
    own, other, panel_ref = refs[:line], refs[line : 2 * line], refs[2 * line]
    base_ref = refs[2 * line + 1] if has_base else None
    out_ref, held, sems, *spare = refs[2 * line + 1 + has_base :]
    focal = own[0].shape[2]
    rows = held.shape[3]
    wait = fetch_panels(line, False, flip, panel_ref, held, sems)

    def body(chunk, carry):
        wait(chunk)
        for row in range(rows):
            w = chunk * rows + row
            total = jnp.zeros((2 * focal, 2 * LANES), F32)
            for step in range(line):
                panel = held[chunk, step, :, row].reshape(2 * LANES, 2 * LANES)
                spec = join_cores(
                    core, own[step][w].reshape(2 * focal, LANES), other[step][w].reshape(2 * focal, LANES)
                )
                total += lax.dot_general(spec, panel, (((1,), (1,)), ((), ())), preferred_element_type=F32)
            real = total[:focal, :LANES] + total[focal:, LANES:]
            imag = total[focal:, :LANES] - total[:focal, LANES:]
            if has_base:
                real += base_ref[w, 0]
                imag += base_ref[w, 1]
            if final:
                spare[0][pl.ds(2 * w * focal, focal), :] = real
                spare[0][pl.ds((2 * w + 1) * focal, focal), :] = imag
            else:
                out_ref[w, 0] = real
                out_ref[w, 1] = imag
        return carry

    lax.fori_loop(0, CHUNKS, body, 0)
    if final:
        for p in range(focal):
            out_ref[p] = spare[0][pl.ds(p, 2 * NFW, stride=focal), :].astype(BF16)


def correlate(own, other, reflection, line, flip, base=None, final=False):
    focal = own[0].shape[2]
    more = [] if base is None else [base]
    shape = jax.ShapeDtypeStruct((NFW, 2, focal, LANES), F32)
    if final:
        shape = jax.ShapeDtypeStruct((focal, 2 * NFW, LANES), BF16)
    spare = [pltpu.VMEM((2 * NFW * focal, LANES), F32)] if final else []
    return pl.pallas_call(
        functools.partial(correlate_kernel, line, flip, bool(more), final),
        in_specs=[VMEM] * (2 * line) + [ANY] + [VMEM] * len(more),
        out_specs=VMEM,
        out_shape=shape,
        scratch_shapes=panel_scratch(line) + spare,
        compiler_params=limit(24),
        cost_estimate=panel_cost(focal, reflection.shape[3] // 2),
        name=f"correlate{flip}",
    )(*own, *other, reflection, *more)


def windowed_spectrum(pair, onset, forward, inverse):
    time = lax.broadcasted_iota(jnp.int32, (NT, 2 * LANES), 0)
    values = jnp.dot(inverse, jnp.concatenate(pair, axis=1), preferred_element_type=F32)
    kept = jnp.where(time < jnp.concatenate(onset, axis=1), values, 0.0).astype(BF16)
    return jnp.dot(forward, kept, preferred_element_type=F32)


def window_kernel(parts, has_base, want_spec, *refs):
    refs = list(refs)
    forward_ref, inverse_ref, onset_ref = refs[:3]
    part_refs = refs[3 : 3 + parts]
    rest = refs[3 + parts :]
    base_ref = rest.pop(0) if has_base else None
    out_ref = rest.pop(0)
    held, result = rest
    focal = part_refs[0].shape[2]
    k = 2 * NFW
    total = part_refs[0][...].astype(F32)
    for ref in part_refs[1:]:
        total += ref[...].astype(F32)
    held[...] = total.reshape(k * focal, LANES)
    me = lax.axis_index("blk")
    columns = pl.ds(pl.multiple_of(me * LANES, LANES), LANES)
    if want_spec:
        for p in range(focal):
            out_ref[p] = held[pl.ds(p, k, stride=focal), :].astype(BF16)
        return
    for p in range(0, focal, 2):
        pair = [held[pl.ds(p + q, k, stride=focal), :].astype(BF16) for q in range(2)]
        onset = [onset_ref[p + q : p + q + 1, columns] for q in range(2)]
        spectrum = windowed_spectrum(pair, onset, forward_ref[...], inverse_ref[...])
        for q in range(2):
            result[pl.ds(p + q, k, stride=focal), :] = spectrum[:, q * LANES : (q + 1) * LANES]
    final = result[...].reshape(NFW, 2, focal, LANES)
    if base_ref is not None:
        final += base_ref[...].astype(F32)
    out_ref[...] = final.astype(BF16)


def window(parts, forward, inverse, onset_times, base=None, want_spec=False):
    focal = parts[0].shape[2]
    k = 2 * NFW
    operands = [forward, inverse, onset_times, *parts] + ([] if base is None else [base])
    out = jax.ShapeDtypeStruct((NFW, 2, focal, LANES), BF16)
    if want_spec:
        out = jax.ShapeDtypeStruct((focal, k, LANES), BF16)
    return pl.pallas_call(
        functools.partial(window_kernel, len(parts), base is not None, want_spec),
        in_specs=[VMEM] * len(operands),
        out_specs=VMEM,
        out_shape=out,
        scratch_shapes=[pltpu.VMEM((k * focal, LANES), F32)] * 2,
        compiler_params=limit(8),
        cost_estimate=pl.CostEstimate(
            flops=4 * k * NT * focal * LANES, bytes_accessed=2 * k * focal * LANES * 6, transcendentals=0
        ),
        name="window",
    )(*operands)


def window_at_kernel(line, flip, step, forward_ref, inverse_ref, onset_ref, spec_ref, out_ref, result):
    core = own_place(line)[3]
    focal, k, _ = spec_ref.shape
    start = chip_columns(line, False, flip, step) + core * LANES
    columns = pl.ds(pl.multiple_of(start, LANES), LANES)
    for p in range(0, focal, 2):
        onset = [onset_ref[p + q : p + q + 1, columns] for q in range(2)]
        pair = [spec_ref[p + q] for q in range(2)]
        spectrum = windowed_spectrum(pair, onset, forward_ref[...], inverse_ref[...])
        for q in range(2):
            result[pl.ds(p + q, k, stride=focal), :] = spectrum[:, q * LANES : (q + 1) * LANES]
    out_ref[...] = result[...].reshape(NFW, 2, focal, LANES).astype(BF16)


def window_at(spec, forward, inverse, onset_times, line, flip, step):
    focal, k, _ = spec.shape
    return pl.pallas_call(
        functools.partial(window_at_kernel, line, flip, step),
        in_specs=[VMEM] * 4,
        out_specs=VMEM,
        out_shape=jax.ShapeDtypeStruct((NFW, 2, focal, LANES), BF16),
        scratch_shapes=[pltpu.VMEM((k * focal, LANES), F32)],
        compiler_params=limit(8),
        cost_estimate=pl.CostEstimate(
            flops=4 * k * NT * focal * LANES, bytes_accessed=2 * k * focal * LANES * 6, transcendentals=0
        ),
        name="window_at",
    )(forward, inverse, onset_times, spec)


def field_kernel(line, has_plus, inverse_ref, onset_ref, *refs):
    core = own_place(line)[3]
    places = relative(line)
    own, other = refs[: len(places)], refs[len(places) : 2 * len(places)]
    rest = list(refs[2 * len(places) :])
    plus_ref = rest.pop(0) if has_plus else None
    out_ref, made, out_sems, *spare = rest
    samples = out_ref.shape[1]
    out_copy, rows = strip_copies(made, out_ref, out_sems, STRIPS)
    if has_plus:
        plus, plus_sems = spare
        plus_copy, _ = strip_copies(plus_ref, plus, plus_sems, STRIPS)
        for strip in range(STRIPS):
            plus_copy(strip).start()
    time = lax.axis_index("blk") * samples + lax.broadcasted_iota(jnp.int32, (samples, 2 * LANES), 0)

    def body(strip, carry):
        if has_plus:
            plus_copy(strip).wait()
        for row in range(rows):
            p = strip * rows + row
            for at, (flip, step) in enumerate(places):
                columns = pl.ds(chip_columns(line, False, flip, step), 2 * LANES)
                spec = join_cores(core, own[at][p], other[at][p])
                values = jnp.dot(inverse_ref[...], spec, preferred_element_type=F32)
                values = jnp.where(time < onset_ref[pl.ds(p, 1), columns], values, 0.0)
                if has_plus:
                    values += plus[p, :, columns].astype(F32)
                made[p, :, columns] = values.astype(BF16)
        out_copy(strip).start()
        return carry

    lax.fori_loop(0, STRIPS, body, 0)
    for strip in range(STRIPS):
        out_copy(strip).wait()


def field(own, other, inverse, onset_times, line, plus_start=None):
    own, other = sum(own, []), sum(other, [])
    focal, k, _ = own[0].shape
    samples = inverse.shape[0]
    shape = (focal, samples, onset_times.shape[1])
    plus = [] if plus_start is None else [plus_start]
    moved = [pltpu.VMEM(shape, BF16), pltpu.SemaphoreType.DMA((STRIPS,))]
    return pl.pallas_call(
        functools.partial(field_kernel, line, bool(plus)),
        in_specs=[VMEM] * (2 + len(own) + len(other)) + [ANY] * len(plus),
        out_specs=ANY,
        out_shape=jax.ShapeDtypeStruct(shape, BF16),
        scratch_shapes=moved * (1 + len(plus)),
        compiler_params=limit(12),
        cost_estimate=pl.CostEstimate(
            flops=2 * k * math.prod(shape),
            bytes_accessed=4 * math.prod(shape) + 2 * k * focal * shape[2],
            transcendentals=0,
        ),
        name="field",
    )(inverse, onset_times, *own, *other, *plus)


def add(*parts):
    total = parts[0].astype(F32)
    for part in parts[1:]:
        total += part.astype(F32)
    return total


def after(value, *others):
    return lax.optimization_barrier((value, *others))[0] if others else value


def reduce_scatter(places, keep0, keep1, send0, send1):
    got1 = places.send(send1, places.core())
    got0 = places.send(send0, places.core())
    far = [add(keep, got).astype(BF16) for keep, got in zip(keep1, got1)]
    beside = {}
    if places.line > 1:
        beside[1] = places.send(far[1], places.shift(1))
    across = {step: places.send(far[step], places.pair()) for step in range(2, places.line)}
    across[0] = places.send(add(keep1[0], got1[0], *beside.values()).astype(BF16), places.pair())
    parts = [keep0[0], got0[0], across[0]]
    first = []
    for step in range(1, places.line):
        terms = [keep0[step], got0[step]] + ([across[step]] if step in across else [])
        ready = add(*terms).astype(BF16)
        if step > 2:
            ready = after(ready, *first)
        parts.append(places.send(ready, places.shift(step)))
        if step == 1:
            first = [parts[-1]]
    return parts


def gather_chips(places, block, work=None):
    size = places.line
    near = [1, size - 1] if size > 2 else [1] if size > 1 else []
    far = list(range(2, size - 1))
    made = {}

    def run(flip, steps, pieces, *others):
        if work is None:
            return []
        for step in steps:
            made[flip, step] = work(after(pieces[step], *others), flip, step)
        return [made[flip, step] for step in steps]

    line = {0: block}
    for step in near:
        line[step] = places.send(block, places.shift(step))
    across = {0: places.send(block, places.pair())}
    own = run(0, [0], line)
    for step in far:
        line[step] = places.send(after(block, line[1], *own), places.shift(step))
    for step in near:
        if step == 1:
            across[step] = places.send(across[0], places.shift(1))
        else:
            across[step] = places.send(line[step], places.pair())
    middle = run(1, [0], across) + run(0, near, line)
    for step in far:
        across[step] = places.send(after(line[step], *middle), places.pair())
    late = run(0, far, line) + run(1, near, across)
    run(1, far, across, *late)
    pieces = [[side[step] for step in range(size)] for side in (line, across)]
    results = [[made[flip, step] for step in range(size)] for flip in range(2)] if work else None
    return pieces, results


def swap_cores(places, pieces):
    return [places.send(piece, places.core()) for piece in pieces]


def local(plus_start, reflection, onset_times):
    size = lax.axis_size("blk")
    places = Places("blk", size)
    line = places.line
    focal, samples, _ = plus_start.shape
    forward, inverse = tables_of(jnp.arange(NT, dtype=jnp.int32))
    own_samples = lax.axis_index("blk") * samples + jnp.arange(samples, dtype=jnp.int32)
    own_forward, own_inverse = tables_of(own_samples)

    def window_piece(piece, flip, step):
        return window_at(piece, forward, inverse, onset_times, line, flip, step)

    parts = reduce_scatter(places, *first_analysis(plus_start, own_forward, line))
    start = add(*parts).astype(BF16)
    start = jnp.transpose(start, (1, 0, 2)).reshape(NFW, 2, focal, LANES)
    spectrum_plus = start
    for iteration in range(ITERS):
        last = iteration + 1 == ITERS
        parts = reduce_scatter(places, *convolve(spectrum_plus, reflection, line))
        windowed = window(parts, forward, inverse, onset_times, want_spec=last)
        if last:
            upgoing_spec, own = gather_chips(places, windowed, window_piece)
        else:
            own, _ = gather_chips(places, windowed)
        half = correlate(own[0], swap_cores(places, own[0]), reflection, line, 0)
        across = [own[1][step] if step in (0, line - 1) else after(own[1][step], half) for step in range(line)]
        downgoing_spec = correlate(own[1], swap_cores(places, across), reflection, line, 1, half, last)
        if not last:
            spectrum_plus = window([downgoing_spec], forward, inverse, onset_times, base=start)
    other = [swap_cores(places, side) for side in upgoing_spec]
    upgoing = field(upgoing_spec, other, own_inverse, onset_times, line)

    def before_far(piece, flip, step):
        return upgoing if (flip, step) == (0, 0) else piece

    own, _ = gather_chips(places, downgoing_spec, before_far)
    other = [swap_cores(places, side) for side in own]
    downgoing = field(own, other, own_inverse, onset_times, line, plus_start)
    return upgoing, downgoing


def analyze(values, forward):
    total = jnp.einsum("kt,ptx->kpx", forward, values, preferred_element_type=F32)
    return total.reshape(NFW, 2, values.shape[0], values.shape[2])


def synthesize(spectrum, inverse):
    flat = spectrum.reshape(2 * NFW, spectrum.shape[2], spectrum.shape[3])
    return jnp.einsum("tk,kpx->ptx", inverse, flat, preferred_element_type=F32)


def contract(form, left, right):
    return jnp.einsum(form, left, right, preferred_element_type=F32)


def local_any(plus_start, reflection, onset_times):
    samples = plus_start.shape[1]
    width = reflection.shape[2]
    me = lax.axis_index("blk")
    forward, inverse = tables_of(jnp.arange(NT, dtype=jnp.int32))
    own_forward, own_inverse = tables_of(me * samples + jnp.arange(samples, dtype=jnp.int32))
    onset = lax.dynamic_slice_in_dim(onset_times, me * width, width, 1)
    keep = jnp.arange(NT, dtype=jnp.int32)[None, :, None] < onset[:, None, :]
    time = me * samples + jnp.arange(samples, dtype=jnp.int32)
    own_keep = time[None, :, None] < onset_times[:, None, :]

    def scatter(partial):
        return lax.psum_scatter(partial.astype(BF16), "blk", scatter_dimension=3, tiled=True).astype(BF16)

    def gather(block):
        return lax.all_gather(block, "blk", axis=3, tiled=True)

    start = scatter(analyze(plus_start, own_forward))
    spectrum = start
    for iteration in range(ITERS):
        real = contract("wrs,wpr->wps", reflection[0], spectrum[:, 0]) - contract(
            "wrs,wpr->wps", reflection[1], spectrum[:, 1]
        )
        imag = contract("wrs,wpr->wps", reflection[0], spectrum[:, 1]) + contract(
            "wrs,wpr->wps", reflection[1], spectrum[:, 0]
        )
        upgoing_spec = scatter(jnp.stack([real, imag], axis=1))
        kept = jnp.where(keep, synthesize(upgoing_spec, inverse), 0.0).astype(BF16)
        minus = gather(analyze(kept, forward).astype(BF16))
        real = contract("wrs,wps->wpr", reflection[0], minus[:, 0]) + contract(
            "wrs,wps->wpr", reflection[1], minus[:, 1]
        )
        imag = contract("wrs,wps->wpr", reflection[0], minus[:, 1]) - contract(
            "wrs,wps->wpr", reflection[1], minus[:, 0]
        )
        downgoing_spec = jnp.stack([real, imag], axis=1).astype(BF16)
        if iteration + 1 < ITERS:
            kept = jnp.where(keep, synthesize(downgoing_spec, inverse), 0.0).astype(BF16)
            spectrum = (start.astype(F32) + analyze(kept, forward)).astype(BF16)
    upgoing = jnp.where(own_keep, synthesize(gather(upgoing_spec), own_inverse), 0.0).astype(BF16)
    change = jnp.where(own_keep, synthesize(gather(downgoing_spec), own_inverse), 0.0)
    return upgoing, (plus_start.astype(F32) + change).astype(BF16)


def solution(mesh):
    size = mesh.shape["blk"]

    def run(plus_start, reflection, onset_times):
        width = reflection.shape[2] // size
        fits = width == LANES and size % 4 == 0 and (plus_start.shape[1] // size) % 16 == 0
        return jax.shard_map(
            local if fits else local_any,
            mesh=mesh,
            in_specs=(P("groups", "blk", None), P(None, None, "blk", None), P("groups", None)),
            out_specs=(P("groups", "blk", None), P("groups", "blk", None)),
            check_vma=False,
        )(plus_start, reflection, onset_times)

    return run
```

```python
import functools
import math

import jax
import jax.numpy as jnp
from jax import lax
from jax.experimental import pallas as pl
from jax.experimental.pallas import tpu as pltpu
from jax.sharding import PartitionSpec as P

NT = 512
NFW = 32
FREQ0 = 16
ITERS = 2
LANES = 128
F32 = jnp.float32
BF16 = jnp.bfloat16


def basis_of(samples):
    freqs = FREQ0 + jnp.arange(NFW, dtype=jnp.int32)
    turns = freqs[:, None] * samples[None, :] % NT
    phase = turns.astype(F32) * (2.0 * math.pi / NT)
    return jnp.stack([jnp.cos(phase), -jnp.sin(phase)], axis=1)


def tables_of(samples):
    basis = basis_of(samples).reshape(2 * NFW, samples.shape[0])
    forward = (basis * (1.0 / math.sqrt(NT))).astype(BF16)
    inverse = (basis * math.sqrt(2.0 / NFW)).astype(BF16)
    return forward, inverse.T


class Places:
    def __init__(self, axis, size):
        self.axis = axis
        self.size = size
        self.line = size // 4

    def core(self):
        return [(b, b ^ 1) for b in range(self.size)]

    def pair(self):
        return [(b, b ^ 2) for b in range(self.size)]

    def shift(self, step):
        return [(b, (b // 4 + step) % self.line * 4 + b % 4) for b in range(self.size)]

    def send(self, array, pairs):
        return lax.ppermute(array, self.axis, pairs)


def own_place(line):
    me = lax.axis_index("blk")
    return me, me // 4, (me // 2) % 2, me % 2


def chip_columns(line, ahead, flip, step):
    _, l, m, _ = own_place(line)
    other = lax.rem(l + step, line) if ahead else lax.rem(l - step + line, line)
    chip = other * 2 + (lax.rem(m + flip, 2))
    return pl.multiple_of(chip * (2 * LANES), 2 * LANES)


def relative(line):
    return [(flip, step) for flip in range(2) for step in range(line)]


def split_cores(core, block):
    low, high = block[:, :LANES], block[:, LANES:]
    first = core == 0
    return jnp.where(first, low, high), jnp.where(first, high, low)


def join_cores(core, own, other):
    first = core == 0
    return jnp.concatenate([jnp.where(first, own, other), jnp.where(first, other, own)], axis=1)


VMEM = pl.BlockSpec(memory_space=pltpu.VMEM)
ANY = pl.BlockSpec(memory_space=pl.ANY)
CHUNKS = 8
STRIPS = 4
SLOTS = 4


def limit(mebibytes):
    return pltpu.CompilerParams(vmem_limit_bytes=mebibytes << 20)


def strip_copies(source, target, sems, strips):
    rows = source.shape[0] // strips

    def copy(strip):
        part = pl.ds(strip * rows, rows)
        return pltpu.make_async_copy(source.at[part], target.at[part], sems.at[strip])

    return copy, rows


def analysis_kernel(line, forward_ref, plus_ref, keep0, keep1, send0, send1, held, sems):
    core = own_place(line)[3]
    keep, send = (keep0, keep1), (send0, send1)
    copy, rows = strip_copies(plus_ref, held, sems, STRIPS)
    for strip in range(STRIPS):
        copy(strip).start()

    def body(strip, carry):
        copy(strip).wait()
        for row in range(rows):
            p = strip * rows + row
            for flip, step in relative(line):
                columns = pl.ds(chip_columns(line, True, flip, step), 2 * LANES)
                block = jnp.dot(forward_ref[...], held[p, :, columns], preferred_element_type=F32)
                mine, theirs = split_cores(core, block.astype(BF16))
                keep[flip][step, p] = mine
                send[flip][step, p] = theirs
        return carry

    lax.fori_loop(0, STRIPS, body, 0)


def first_analysis(plus_start, forward, line):
    focal, samples, width = plus_start.shape
    out = jax.ShapeDtypeStruct((line, focal, 2 * NFW, LANES), BF16)
    return pl.pallas_call(
        functools.partial(analysis_kernel, line),
        in_specs=[VMEM, ANY],
        out_specs=[VMEM] * 4,
        out_shape=[out] * 4,
        scratch_shapes=[pltpu.VMEM(plus_start.shape, BF16), pltpu.SemaphoreType.DMA((STRIPS,))],
        compiler_params=limit(8),
        cost_estimate=pl.CostEstimate(
            flops=4 * NFW * focal * samples * width,
            bytes_accessed=2 * focal * samples * width + 4 * NFW * focal * width,
            transcendentals=0,
        ),
        name="first_analysis",
    )(forward, plus_start)


def fetch_panels(line, ahead, flip, panel_ref, held, sems):
    chunks, _, _, rows = held.shape[:4]

    def copy(chunk, step):
        columns = pl.ds(chip_columns(line, ahead, flip, step), 2 * LANES)
        source = panel_ref.at[:, pl.ds(chunk * rows, rows), :, columns]
        return pltpu.make_async_copy(source, held.at[chunk, step], sems.at[chunk, step])

    for chunk in range(chunks):
        for step in range(line):
            copy(chunk, step).start()

    def wait(chunk):
        for step in range(line):
            copy(chunk, step).wait()

    return wait


def panel_scratch(line):
    rows = NFW // CHUNKS
    return [
        pltpu.VMEM((CHUNKS, line, 2, rows, LANES, 2 * LANES), BF16),
        pltpu.SemaphoreType.DMA((CHUNKS, line)),
    ]


def convolve_kernel(line, spec_ref, panel_ref, keep0, keep1, send0, send1, held, sems):
    core = own_place(line)[3]
    keep, send = (keep0, keep1), (send0, send1)
    focal = spec_ref.shape[2]
    rows = NFW // CHUNKS

    slots = held.shape[0]

    def copy(chunk):
        slot = lax.rem(chunk, slots)
        part = pl.ds(chunk * rows, rows)
        return pltpu.make_async_copy(panel_ref.at[:, part], held.at[slot], sems.at[slot])

    for chunk in range(slots):
        copy(chunk).start()

    def body(chunk, carry):
        copy(chunk).wait()
        slot = lax.rem(chunk, slots)
        for row in range(rows):
            w = chunk * rows + row
            real, imag = spec_ref[w, 0], spec_ref[w, 1]
            left = jnp.concatenate(
                [jnp.concatenate([real, -imag], axis=1), jnp.concatenate([imag, real], axis=1)], axis=0
            )
            for flip, step in relative(line):
                columns = pl.ds(chip_columns(line, True, flip, step), 2 * LANES)
                panel = held[slot, :, row, :, columns].reshape(2 * LANES, 2 * LANES)
                block = jnp.dot(left, panel, preferred_element_type=F32)
                mine, theirs = split_cores(core, block.astype(BF16))
                keep[flip][step, w] = mine.reshape(2, focal, LANES)
                send[flip][step, w] = theirs.reshape(2, focal, LANES)

        @pl.when(chunk + slots < CHUNKS)
        def _():
            copy(chunk + slots).start()

        return carry

    lax.fori_loop(0, CHUNKS, body, 0)


def panel_cost(focal, sources):
    return pl.CostEstimate(
        flops=8 * NFW * focal * LANES * sources,
        bytes_accessed=4 * NFW * sources * (LANES + focal),
        transcendentals=0,
    )


def convolve(spectrum, reflection, line):
    focal = spectrum.shape[2]
    out = jax.ShapeDtypeStruct((line, NFW, 2, focal, LANES), BF16)
    return pl.pallas_call(
        functools.partial(convolve_kernel, line),
        in_specs=[VMEM, ANY],
        out_specs=[VMEM] * 4,
        out_shape=[out] * 4,
        scratch_shapes=[
            pltpu.VMEM((SLOTS, 2, NFW // CHUNKS, LANES, reflection.shape[3]), BF16),
            pltpu.SemaphoreType.DMA((SLOTS,)),
        ],
        compiler_params=limit(20),
        cost_estimate=panel_cost(focal, reflection.shape[3]),
        name="convolve",
    )(spectrum, reflection)


def correlate_kernel(line, flip, has_base, final, *refs):
    core = own_place(line)[3]
    own, other, panel_ref = refs[:line], refs[line : 2 * line], refs[2 * line]
    base_ref = refs[2 * line + 1] if has_base else None
    out_ref, held, sems, *spare = refs[2 * line + 1 + has_base :]
    focal = own[0].shape[2]
    rows = held.shape[3]
    wait = fetch_panels(line, False, flip, panel_ref, held, sems)

    def body(chunk, carry):
        wait(chunk)
        for row in range(rows):
            w = chunk * rows + row
            panels, specs = [], []
            for step in range(line):
                panels.append(held[chunk, step, :, row].reshape(2 * LANES, 2 * LANES))
                mine, theirs = own[step][w], other[step][w]
                specs.append(
                    join_cores(core, mine.reshape(2 * focal, LANES), theirs.reshape(2 * focal, LANES))
                )
            total = lax.dot_general(
                jnp.concatenate(specs, axis=1),
                jnp.concatenate(panels, axis=1),
                (((1,), (1,)), ((), ())),
                preferred_element_type=F32,
            )
            real = total[:focal, :LANES] + total[focal:, LANES:]
            imag = total[focal:, :LANES] - total[:focal, LANES:]
            if has_base:
                real += base_ref[w, 0]
                imag += base_ref[w, 1]
            if final:
                spare[0][pl.ds(2 * w * focal, focal), :] = real
                spare[0][pl.ds((2 * w + 1) * focal, focal), :] = imag
            else:
                out_ref[w, 0] = real
                out_ref[w, 1] = imag
        return carry

    lax.fori_loop(0, CHUNKS, body, 0)
    if final:
        for p in range(focal):
            out_ref[p] = spare[0][pl.ds(p, 2 * NFW, stride=focal), :].astype(BF16)


def correlate(own, other, reflection, line, flip, base=None, final=False):
    focal = own[0].shape[2]
    more = [] if base is None else [base]
    shape = jax.ShapeDtypeStruct((NFW, 2, focal, LANES), F32)
    if final:
        shape = jax.ShapeDtypeStruct((focal, 2 * NFW, LANES), BF16)
    spare = [pltpu.VMEM((2 * NFW * focal, LANES), F32)] if final else []
    return pl.pallas_call(
        functools.partial(correlate_kernel, line, flip, bool(more), final),
        in_specs=[VMEM] * (2 * line) + [ANY] + [VMEM] * len(more),
        out_specs=VMEM,
        out_shape=shape,
        scratch_shapes=panel_scratch(line) + spare,
        compiler_params=limit(24),
        cost_estimate=panel_cost(focal, reflection.shape[3] // 2),
        name=f"correlate{flip}",
    )(*own, *other, reflection, *more)


def windowed_spectrum(pair, onset, forward, inverse):
    time = lax.broadcasted_iota(jnp.int32, (NT, 2 * LANES), 0)
    values = jnp.dot(inverse, jnp.concatenate(pair, axis=1), preferred_element_type=F32)
    kept = jnp.where(time < jnp.concatenate(onset, axis=1), values, 0.0).astype(BF16)
    return jnp.dot(forward, kept, preferred_element_type=F32)


def window_kernel(parts, has_base, want_spec, *refs):
    refs = list(refs)
    forward_ref, inverse_ref, onset_ref = refs[:3]
    part_refs = refs[3 : 3 + parts]
    rest = refs[3 + parts :]
    base_ref = rest.pop(0) if has_base else None
    out_ref = rest.pop(0)
    held, result = rest
    focal = part_refs[0].shape[2]
    k = 2 * NFW
    total = part_refs[0][...].astype(F32)
    for ref in part_refs[1:]:
        total += ref[...].astype(F32)
    held[...] = total.reshape(k * focal, LANES)
    me = lax.axis_index("blk")
    columns = pl.ds(pl.multiple_of(me * LANES, LANES), LANES)
    if want_spec:
        for p in range(focal):
            out_ref[p] = held[pl.ds(p, k, stride=focal), :].astype(BF16)
        return
    for p in range(0, focal, 2):
        pair = [held[pl.ds(p + q, k, stride=focal), :].astype(BF16) for q in range(2)]
        onset = [onset_ref[p + q : p + q + 1, columns] for q in range(2)]
        spectrum = windowed_spectrum(pair, onset, forward_ref[...], inverse_ref[...])
        for q in range(2):
            result[pl.ds(p + q, k, stride=focal), :] = spectrum[:, q * LANES : (q + 1) * LANES]
    final = result[...].reshape(NFW, 2, focal, LANES)
    if base_ref is not None:
        final += base_ref[...].astype(F32)
    out_ref[...] = final.astype(BF16)


def window(parts, forward, inverse, onset_times, base=None, want_spec=False):
    focal = parts[0].shape[2]
    k = 2 * NFW
    operands = [forward, inverse, onset_times, *parts] + ([] if base is None else [base])
    out = jax.ShapeDtypeStruct((NFW, 2, focal, LANES), BF16)
    if want_spec:
        out = jax.ShapeDtypeStruct((focal, k, LANES), BF16)
    return pl.pallas_call(
        functools.partial(window_kernel, len(parts), base is not None, want_spec),
        in_specs=[VMEM] * len(operands),
        out_specs=VMEM,
        out_shape=out,
        scratch_shapes=[pltpu.VMEM((k * focal, LANES), F32)] * 2,
        compiler_params=limit(8),
        cost_estimate=pl.CostEstimate(
            flops=4 * k * NT * focal * LANES, bytes_accessed=2 * k * focal * LANES * 6, transcendentals=0
        ),
        name="window",
    )(*operands)


def window_at_kernel(line, flip, step, forward_ref, inverse_ref, onset_ref, spec_ref, out_ref, result):
    core = own_place(line)[3]
    focal, k, _ = spec_ref.shape
    start = chip_columns(line, False, flip, step) + core * LANES
    columns = pl.ds(pl.multiple_of(start, LANES), LANES)
    for p in range(0, focal, 2):
        onset = [onset_ref[p + q : p + q + 1, columns] for q in range(2)]
        pair = [spec_ref[p + q] for q in range(2)]
        spectrum = windowed_spectrum(pair, onset, forward_ref[...], inverse_ref[...])
        for q in range(2):
            result[pl.ds(p + q, k, stride=focal), :] = spectrum[:, q * LANES : (q + 1) * LANES]
    out_ref[...] = result[...].reshape(NFW, 2, focal, LANES).astype(BF16)


def window_at(spec, forward, inverse, onset_times, line, flip, step):
    focal, k, _ = spec.shape
    return pl.pallas_call(
        functools.partial(window_at_kernel, line, flip, step),
        in_specs=[VMEM] * 4,
        out_specs=VMEM,
        out_shape=jax.ShapeDtypeStruct((NFW, 2, focal, LANES), BF16),
        scratch_shapes=[pltpu.VMEM((k * focal, LANES), F32)],
        compiler_params=limit(8),
        cost_estimate=pl.CostEstimate(
            flops=4 * k * NT * focal * LANES, bytes_accessed=2 * k * focal * LANES * 6, transcendentals=0
        ),
        name="window_at",
    )(forward, inverse, onset_times, spec)


def field_kernel(line, has_plus, inverse_ref, onset_ref, *refs):
    core = own_place(line)[3]
    places = relative(line)
    own, other = refs[: len(places)], refs[len(places) : 2 * len(places)]
    rest = list(refs[2 * len(places) :])
    plus_ref = rest.pop(0) if has_plus else None
    out_ref, made, out_sems, *spare = rest
    samples = out_ref.shape[1]
    out_copy, rows = strip_copies(made, out_ref, out_sems, STRIPS)
    if has_plus:
        plus, plus_sems = spare
        plus_copy, _ = strip_copies(plus_ref, plus, plus_sems, STRIPS)
        for strip in range(STRIPS):
            plus_copy(strip).start()
    time = lax.axis_index("blk") * samples + lax.broadcasted_iota(jnp.int32, (samples, 2 * LANES), 0)

    def body(strip, carry):
        if has_plus:
            plus_copy(strip).wait()
        for row in range(rows):
            p = strip * rows + row
            for at, (flip, step) in enumerate(places):
                columns = pl.ds(chip_columns(line, False, flip, step), 2 * LANES)
                spec = join_cores(core, own[at][p], other[at][p])
                values = jnp.dot(inverse_ref[...], spec, preferred_element_type=F32)
                values = jnp.where(time < onset_ref[pl.ds(p, 1), columns], values, 0.0)
                if has_plus:
                    values += plus[p, :, columns].astype(F32)
                made[p, :, columns] = values.astype(BF16)
        out_copy(strip).start()
        return carry

    lax.fori_loop(0, STRIPS, body, 0)
    for strip in range(STRIPS):
        out_copy(strip).wait()


def field(own, other, inverse, onset_times, line, plus_start=None):
    own, other = sum(own, []), sum(other, [])
    focal, k, _ = own[0].shape
    samples = inverse.shape[0]
    shape = (focal, samples, onset_times.shape[1])
    plus = [] if plus_start is None else [plus_start]
    moved = [pltpu.VMEM(shape, BF16), pltpu.SemaphoreType.DMA((STRIPS,))]
    return pl.pallas_call(
        functools.partial(field_kernel, line, bool(plus)),
        in_specs=[VMEM] * (2 + len(own) + len(other)) + [ANY] * len(plus),
        out_specs=ANY,
        out_shape=jax.ShapeDtypeStruct(shape, BF16),
        scratch_shapes=moved * (1 + len(plus)),
        compiler_params=limit(12),
        cost_estimate=pl.CostEstimate(
            flops=2 * k * math.prod(shape),
            bytes_accessed=4 * math.prod(shape) + 2 * k * focal * shape[2],
            transcendentals=0,
        ),
        name="field",
    )(inverse, onset_times, *own, *other, *plus)


def add(*parts):
    total = parts[0].astype(F32)
    for part in parts[1:]:
        total += part.astype(F32)
    return total


def after(value, *others):
    return lax.optimization_barrier((value, *others))[0] if others else value


def reduce_scatter(places, keep0, keep1, send0, send1):
    size = places.line
    got1 = places.send(send1, places.core())
    got0 = places.send(send0, places.core())
    far = [add(keep, got).astype(BF16) for keep, got in zip(keep1, got1)]
    across = {step: places.send(far[step], places.pair()) for step in range(2, size)}
    beside = [places.send(far[1], places.shift(1))] if size > 1 else []
    parts = [keep0[0], got0[0]]

    def pass_on(steps, shift):
        carried = []
        for step in steps:
            terms = [keep0[step], got0[step], *([across[step]] if step in across else []), *carried]
            carried = [places.send(add(*terms).astype(BF16), places.shift(shift))]
        return carried

    parts += pass_on(range(size // 2, 0, -1), 1)
    parts += pass_on(range(size // 2 + 1, size), size - 1)
    across[0] = places.send(add(keep1[0], got1[0], *beside).astype(BF16), places.pair())
    return parts + [across[0]]


def gather_chips(places, block, work=None):
    size = places.line
    near = [1, size - 1] if size > 2 else [1] if size > 1 else []
    far = list(range(2, size - 1))
    made = {}

    def run(flip, steps, pieces, *others):
        if work is None:
            return []
        for step in steps:
            made[flip, step] = work(after(pieces[step], *others), flip, step)
        return [made[flip, step] for step in steps]

    line = {0: block}
    for step in near:
        line[step] = places.send(block, places.shift(step))
    across = {0: places.send(block, places.pair())}
    own = run(0, [0], line)
    for step in range(2, size // 2 + 1):
        line[step] = places.send(after(line[step - 1], *own), places.shift(1))
    for step in range(size - 2, size // 2, -1):
        line[step] = places.send(after(line[step + 1], *own), places.shift(size - 1))
    for step in near:
        if step == 1:
            across[step] = places.send(across[0], places.shift(1))
        else:
            across[step] = places.send(line[step], places.pair())
    middle = run(1, [0], across) + run(0, near, line)
    for step in far:
        across[step] = places.send(after(line[step], *middle), places.pair())
    late = run(0, far, line) + run(1, near, across)
    run(1, far, across, *late)
    pieces = [[side[step] for step in range(size)] for side in (line, across)]
    results = [[made[flip, step] for step in range(size)] for flip in range(2)] if work else None
    return pieces, results


def swap_cores(places, pieces):
    return [places.send(piece, places.core()) for piece in pieces]


def local(plus_start, reflection, onset_times):
    size = lax.axis_size("blk")
    places = Places("blk", size)
    line = places.line
    focal, samples, _ = plus_start.shape
    forward, inverse = tables_of(jnp.arange(NT, dtype=jnp.int32))
    own_samples = lax.axis_index("blk") * samples + jnp.arange(samples, dtype=jnp.int32)
    own_forward, own_inverse = tables_of(own_samples)

    def window_piece(piece, flip, step):
        return window_at(piece, forward, inverse, onset_times, line, flip, step)

    parts = reduce_scatter(places, *first_analysis(plus_start, own_forward, line))
    start = add(*parts).astype(BF16)
    start = jnp.transpose(start, (1, 0, 2)).reshape(NFW, 2, focal, LANES)
    spectrum_plus = start
    for iteration in range(ITERS):
        last = iteration + 1 == ITERS
        parts = reduce_scatter(places, *convolve(spectrum_plus, reflection, line))
        windowed = window(parts, forward, inverse, onset_times, want_spec=last)
        if last:
            upgoing_spec, own = gather_chips(places, windowed, window_piece)
        else:
            own, _ = gather_chips(places, windowed)
        half = correlate(own[0], swap_cores(places, own[0]), reflection, line, 0)
        across = [own[1][step] if step in (0, line - 1) else after(own[1][step], half) for step in range(line)]
        downgoing_spec = correlate(own[1], swap_cores(places, across), reflection, line, 1, half, last)
        if not last:
            spectrum_plus = window([downgoing_spec], forward, inverse, onset_times, base=start)
    other = [swap_cores(places, side) for side in upgoing_spec]
    upgoing = field(upgoing_spec, other, own_inverse, onset_times, line)

    def before_far(piece, flip, step):
        return upgoing if (flip, step) == (1, 0) else piece

    own, _ = gather_chips(places, downgoing_spec, before_far)
    other = [swap_cores(places, side) for side in own]
    downgoing = field(own, other, own_inverse, onset_times, line, plus_start)
    return upgoing, downgoing


def analyze(values, forward):
    total = jnp.einsum("kt,ptx->kpx", forward, values, preferred_element_type=F32)
    return total.reshape(NFW, 2, values.shape[0], values.shape[2])


def synthesize(spectrum, inverse):
    flat = spectrum.reshape(2 * NFW, spectrum.shape[2], spectrum.shape[3])
    return jnp.einsum("tk,kpx->ptx", inverse, flat, preferred_element_type=F32)


def contract(form, left, right):
    return jnp.einsum(form, left, right, preferred_element_type=F32)


def local_any(plus_start, reflection, onset_times):
    samples = plus_start.shape[1]
    width = reflection.shape[2]
    me = lax.axis_index("blk")
    forward, inverse = tables_of(jnp.arange(NT, dtype=jnp.int32))
    own_forward, own_inverse = tables_of(me * samples + jnp.arange(samples, dtype=jnp.int32))
    onset = lax.dynamic_slice_in_dim(onset_times, me * width, width, 1)
    keep = jnp.arange(NT, dtype=jnp.int32)[None, :, None] < onset[:, None, :]
    time = me * samples + jnp.arange(samples, dtype=jnp.int32)
    own_keep = time[None, :, None] < onset_times[:, None, :]

    def scatter(partial):
        return lax.psum_scatter(partial.astype(BF16), "blk", scatter_dimension=3, tiled=True).astype(BF16)

    def gather(block):
        return lax.all_gather(block, "blk", axis=3, tiled=True)

    start = scatter(analyze(plus_start, own_forward))
    spectrum = start
    for iteration in range(ITERS):
        real = contract("wrs,wpr->wps", reflection[0], spectrum[:, 0]) - contract(
            "wrs,wpr->wps", reflection[1], spectrum[:, 1]
        )
        imag = contract("wrs,wpr->wps", reflection[0], spectrum[:, 1]) + contract(
            "wrs,wpr->wps", reflection[1], spectrum[:, 0]
        )
        upgoing_spec = scatter(jnp.stack([real, imag], axis=1))
        kept = jnp.where(keep, synthesize(upgoing_spec, inverse), 0.0).astype(BF16)
        minus = gather(analyze(kept, forward).astype(BF16))
        real = contract("wrs,wps->wpr", reflection[0], minus[:, 0]) + contract(
            "wrs,wps->wpr", reflection[1], minus[:, 1]
        )
        imag = contract("wrs,wps->wpr", reflection[0], minus[:, 1]) - contract(
            "wrs,wps->wpr", reflection[1], minus[:, 0]
        )
        downgoing_spec = jnp.stack([real, imag], axis=1).astype(BF16)
        if iteration + 1 < ITERS:
            kept = jnp.where(keep, synthesize(downgoing_spec, inverse), 0.0).astype(BF16)
            spectrum = (start.astype(F32) + analyze(kept, forward)).astype(BF16)
    upgoing = jnp.where(own_keep, synthesize(gather(upgoing_spec), own_inverse), 0.0).astype(BF16)
    change = jnp.where(own_keep, synthesize(gather(downgoing_spec), own_inverse), 0.0)
    return upgoing, (plus_start.astype(F32) + change).astype(BF16)


def solution(mesh):
    size = mesh.shape["blk"]

    def run(plus_start, reflection, onset_times):
        width = reflection.shape[2] // size
        fits = width == LANES and size % 4 == 0 and (plus_start.shape[1] // size) % 16 == 0
        return jax.shard_map(
            local if fits else local_any,
            mesh=mesh,
            in_specs=(P("groups", "blk", None), P(None, None, "blk", None), P("groups", None)),
            out_specs=(P("groups", "blk", None), P("groups", "blk", None)),
            check_vma=False,
        )(plus_start, reflection, onset_times)

    return run
```

```python
import functools
import math

import jax
import jax.numpy as jnp
from jax import lax
from jax.experimental import pallas as pl
from jax.experimental.pallas import tpu as pltpu
from jax.sharding import PartitionSpec as P

NT = 512
NFW = 32
FREQ0 = 16
ITERS = 2
SURE = 128
LANES = 128
F32 = jnp.float32
BF16 = jnp.bfloat16


def basis_of(samples):
    freqs = FREQ0 + jnp.arange(NFW, dtype=jnp.int32)
    turns = freqs[:, None] * samples[None, :] % NT
    phase = turns.astype(F32) * (2.0 * math.pi / NT)
    return jnp.stack([jnp.cos(phase), -jnp.sin(phase)], axis=1)


def tables_of(samples):
    basis = basis_of(samples).reshape(2 * NFW, samples.shape[0])
    forward = (basis * (1.0 / math.sqrt(NT))).astype(BF16)
    inverse = (basis * math.sqrt(2.0 / NFW)).astype(BF16)
    return forward, inverse.T


class Places:
    def __init__(self, axis, size):
        self.axis = axis
        self.size = size
        self.line = size // 4

    def core(self):
        return [(b, b ^ 1) for b in range(self.size)]

    def pair(self):
        return [(b, b ^ 2) for b in range(self.size)]

    def shift(self, step):
        return [(b, (b // 4 + step) % self.line * 4 + b % 4) for b in range(self.size)]

    def send(self, array, pairs):
        return lax.ppermute(array, self.axis, pairs)


def own_place(line):
    me = lax.axis_index("blk")
    return me, me // 4, (me // 2) % 2, me % 2


def chip_columns(line, ahead, flip, step):
    _, l, m, _ = own_place(line)
    other = lax.rem(l + step, line) if ahead else lax.rem(l - step + line, line)
    chip = other * 2 + (lax.rem(m + flip, 2))
    return pl.multiple_of(chip * (2 * LANES), 2 * LANES)


def relative(line):
    return [(flip, step) for flip in range(2) for step in range(line)]


def split_cores(core, block):
    low, high = block[:, :LANES], block[:, LANES:]
    first = core == 0
    return jnp.where(first, low, high), jnp.where(first, high, low)


def join_cores(core, own, other):
    first = core == 0
    return jnp.concatenate([jnp.where(first, own, other), jnp.where(first, other, own)], axis=1)


VMEM = pl.BlockSpec(memory_space=pltpu.VMEM)
ANY = pl.BlockSpec(memory_space=pl.ANY)
CHUNKS = 8
STRIPS = 4
SLOTS = 4


def limit(mebibytes):
    return pltpu.CompilerParams(vmem_limit_bytes=mebibytes << 20)


def strip_copies(source, target, sems, strips):
    rows = source.shape[0] // strips

    def copy(strip):
        part = pl.ds(strip * rows, rows)
        return pltpu.make_async_copy(source.at[part], target.at[part], sems.at[strip])

    return copy, rows


def analysis_kernel(line, forward_ref, plus_ref, keep0, keep1, send0, send1, held, sems):
    core = own_place(line)[3]
    keep, send = (keep0, keep1), (send0, send1)
    copy, rows = strip_copies(plus_ref, held, sems, STRIPS)
    for strip in range(STRIPS):
        copy(strip).start()

    def body(strip, carry):
        copy(strip).wait()
        for row in range(rows):
            p = strip * rows + row
            for flip, step in relative(line):
                columns = pl.ds(chip_columns(line, True, flip, step), 2 * LANES)
                block = jnp.dot(forward_ref[...], held[p, :, columns], preferred_element_type=F32)
                mine, theirs = split_cores(core, block.astype(BF16))
                keep[flip][step, p] = mine
                send[flip][step, p] = theirs
        return carry

    lax.fori_loop(0, STRIPS, body, 0)


def first_analysis(plus_start, forward, line):
    focal, samples, width = plus_start.shape
    out = jax.ShapeDtypeStruct((line, focal, 2 * NFW, LANES), BF16)
    return pl.pallas_call(
        functools.partial(analysis_kernel, line),
        in_specs=[VMEM, ANY],
        out_specs=[VMEM] * 4,
        out_shape=[out] * 4,
        scratch_shapes=[pltpu.VMEM(plus_start.shape, BF16), pltpu.SemaphoreType.DMA((STRIPS,))],
        compiler_params=limit(8),
        cost_estimate=pl.CostEstimate(
            flops=4 * NFW * focal * samples * width,
            bytes_accessed=2 * focal * samples * width + 4 * NFW * focal * width,
            transcendentals=0,
        ),
        name="first_analysis",
    )(forward, plus_start)


def fetch_panels(line, ahead, flip, panel_ref, held, sems):
    chunks, _, _, rows = held.shape[:4]

    def copy(chunk, step):
        columns = pl.ds(chip_columns(line, ahead, flip, step), 2 * LANES)
        source = panel_ref.at[:, pl.ds(chunk * rows, rows), :, columns]
        return pltpu.make_async_copy(source, held.at[chunk, step], sems.at[chunk, step])

    for chunk in range(chunks):
        for step in range(line):
            copy(chunk, step).start()

    def wait(chunk):
        for step in range(line):
            copy(chunk, step).wait()

    return wait


def panel_scratch(line):
    rows = NFW // CHUNKS
    return [
        pltpu.VMEM((CHUNKS, line, 2, rows, LANES, 2 * LANES), BF16),
        pltpu.SemaphoreType.DMA((CHUNKS, line)),
    ]


def convolve_kernel(line, spec_ref, panel_ref, keep0, keep1, send0, send1, held, sems):
    core = own_place(line)[3]
    keep, send = (keep0, keep1), (send0, send1)
    focal = spec_ref.shape[2]
    rows = NFW // CHUNKS

    slots = held.shape[0]

    def copy(chunk):
        slot = lax.rem(chunk, slots)
        part = pl.ds(chunk * rows, rows)
        return pltpu.make_async_copy(panel_ref.at[:, part], held.at[slot], sems.at[slot])

    for chunk in range(slots):
        copy(chunk).start()

    def body(chunk, carry):
        copy(chunk).wait()
        slot = lax.rem(chunk, slots)
        for row in range(rows):
            w = chunk * rows + row
            real, imag = spec_ref[w, 0], spec_ref[w, 1]
            left = jnp.concatenate(
                [jnp.concatenate([real, -imag], axis=1), jnp.concatenate([imag, real], axis=1)], axis=0
            )
            for flip, step in relative(line):
                columns = pl.ds(chip_columns(line, True, flip, step), 2 * LANES)
                panel = held[slot, :, row, :, columns].reshape(2 * LANES, 2 * LANES)
                block = jnp.dot(left, panel, preferred_element_type=F32)
                mine, theirs = split_cores(core, block.astype(BF16))
                keep[flip][step, w] = mine.reshape(2, focal, LANES)
                send[flip][step, w] = theirs.reshape(2, focal, LANES)

        @pl.when(chunk + slots < CHUNKS)
        def _():
            copy(chunk + slots).start()

        return carry

    lax.fori_loop(0, CHUNKS, body, 0)


def panel_cost(focal, sources):
    return pl.CostEstimate(
        flops=8 * NFW * focal * LANES * sources,
        bytes_accessed=4 * NFW * sources * (LANES + focal),
        transcendentals=0,
    )


def convolve(spectrum, reflection, line):
    focal = spectrum.shape[2]
    out = jax.ShapeDtypeStruct((line, NFW, 2, focal, LANES), BF16)
    return pl.pallas_call(
        functools.partial(convolve_kernel, line),
        in_specs=[VMEM, ANY],
        out_specs=[VMEM] * 4,
        out_shape=[out] * 4,
        scratch_shapes=[
            pltpu.VMEM((SLOTS, 2, NFW // CHUNKS, LANES, reflection.shape[3]), BF16),
            pltpu.SemaphoreType.DMA((SLOTS,)),
        ],
        compiler_params=limit(20),
        cost_estimate=panel_cost(focal, reflection.shape[3]),
        name="convolve",
    )(spectrum, reflection)


def correlate_kernel(line, flip, has_base, *refs):
    core = own_place(line)[3]
    own, other, panel_ref = refs[:line], refs[line : 2 * line], refs[2 * line]
    base_ref = refs[2 * line + 1] if has_base else None
    out_ref, held, sems = refs[2 * line + 1 + has_base :]
    focal = own[0].shape[2]
    rows = held.shape[3]
    wait = fetch_panels(line, False, flip, panel_ref, held, sems)

    def body(chunk, carry):
        wait(chunk)
        for row in range(rows):
            w = chunk * rows + row
            panels, specs = [], []
            for step in range(line):
                panels.append(held[chunk, step, :, row].reshape(2 * LANES, 2 * LANES))
                mine, theirs = own[step][w], other[step][w]
                specs.append(
                    join_cores(core, mine.reshape(2 * focal, LANES), theirs.reshape(2 * focal, LANES))
                )
            total = lax.dot_general(
                jnp.concatenate(specs, axis=1),
                jnp.concatenate(panels, axis=1),
                (((1,), (1,)), ((), ())),
                preferred_element_type=F32,
            )
            real = total[:focal, :LANES] + total[focal:, LANES:]
            imag = total[focal:, :LANES] - total[:focal, LANES:]
            if has_base:
                real += base_ref[w, 0]
                imag += base_ref[w, 1]
            out_ref[w, 0] = real
            out_ref[w, 1] = imag
        return carry

    lax.fori_loop(0, CHUNKS, body, 0)


def correlate(own, other, reflection, line, flip, base=None):
    focal = own[0].shape[2]
    more = [] if base is None else [base]
    shape = jax.ShapeDtypeStruct((NFW, 2, focal, LANES), F32)
    return pl.pallas_call(
        functools.partial(correlate_kernel, line, flip, bool(more)),
        in_specs=[VMEM] * (2 * line) + [ANY] + [VMEM] * len(more),
        out_specs=VMEM,
        out_shape=shape,
        scratch_shapes=panel_scratch(line),
        compiler_params=limit(24),
        cost_estimate=panel_cost(focal, reflection.shape[3] // 2),
        name=f"correlate{flip}",
    )(*own, *other, reflection, *more)


def correlate_all_kernel(line, *refs):
    core = own_place(line)[3]
    places = relative(line)
    own, other = refs[: len(places)], refs[len(places) : 2 * len(places)]
    panel_ref, out_ref, held, sems, total_ref = refs[2 * len(places) :]
    focal = out_ref.shape[0]
    rows = NFW // CHUNKS
    slots = held.shape[0]

    def copy(chunk):
        slot = lax.rem(chunk, slots)
        part = pl.ds(chunk * rows, rows)
        return pltpu.make_async_copy(panel_ref.at[:, part], held.at[slot], sems.at[slot])

    for chunk in range(slots):
        copy(chunk).start()

    def body(chunk, carry):
        copy(chunk).wait()
        slot = lax.rem(chunk, slots)
        for row in range(rows):
            w = chunk * rows + row
            panels, specs = [], []
            for at, (flip, step) in enumerate(places):
                columns = pl.ds(chip_columns(line, False, flip, step), 2 * LANES)
                panels.append(held[slot, :, row, :, columns].reshape(2 * LANES, 2 * LANES))
                mine, theirs = own[at][w], other[at][w]
                specs.append(
                    join_cores(core, mine.reshape(2 * focal, LANES), theirs.reshape(2 * focal, LANES))
                )
            total = lax.dot_general(
                jnp.concatenate(specs, axis=1),
                jnp.concatenate(panels, axis=1),
                (((1,), (1,)), ((), ())),
                preferred_element_type=F32,
            )
            real = total[:focal, :LANES] + total[focal:, LANES:]
            imag = total[focal:, :LANES] - total[:focal, LANES:]
            total_ref[pl.ds(2 * w * focal, focal), :] = real
            total_ref[pl.ds((2 * w + 1) * focal, focal), :] = imag

        @pl.when(chunk + slots < CHUNKS)
        def _():
            copy(chunk + slots).start()

        return carry

    lax.fori_loop(0, CHUNKS, body, 0)
    for p in range(focal):
        out_ref[p] = total_ref[pl.ds(p, 2 * NFW, stride=focal), :].astype(BF16)


def correlate_all(own, other, reflection, line):
    own, other = sum(own, []), sum(other, [])
    focal = own[0].shape[2]
    return pl.pallas_call(
        functools.partial(correlate_all_kernel, line),
        in_specs=[VMEM] * (2 * len(own)) + [ANY],
        out_specs=VMEM,
        out_shape=jax.ShapeDtypeStruct((focal, 2 * NFW, LANES), BF16),
        scratch_shapes=[
            pltpu.VMEM((SLOTS, 2, NFW // CHUNKS, LANES, reflection.shape[3]), BF16),
            pltpu.SemaphoreType.DMA((SLOTS,)),
            pltpu.VMEM((2 * NFW * focal, LANES), F32),
        ],
        compiler_params=limit(22),
        cost_estimate=panel_cost(focal, reflection.shape[3]),
        name="correlate_all",
    )(*own, *other, reflection)


def windowed_spectrum(pair, onset, forward, inverse):
    time = SURE + lax.broadcasted_iota(jnp.int32, (NT - SURE, 2 * LANES), 0)
    spectra = jnp.concatenate(pair, axis=1)
    values = jnp.dot(inverse, spectra, preferred_element_type=F32)
    kept = jnp.where(time < jnp.concatenate(onset, axis=1), values, 0.0).astype(BF16)
    return jnp.dot(forward, jnp.concatenate([kept, spectra], axis=0), preferred_element_type=F32)


def window_kernel(parts, has_base, want_spec, *refs):
    refs = list(refs)
    forward_ref, inverse_ref, onset_ref = refs[:3]
    part_refs = refs[3 : 3 + parts]
    rest = refs[3 + parts :]
    base_ref = rest.pop(0) if has_base else None
    out_ref = rest.pop(0)
    held, result = rest
    focal = part_refs[0].shape[2]
    k = 2 * NFW
    total = part_refs[0][...].astype(F32)
    for ref in part_refs[1:]:
        total += ref[...].astype(F32)
    held[...] = total.reshape(k * focal, LANES)
    me = lax.axis_index("blk")
    columns = pl.ds(pl.multiple_of(me * LANES, LANES), LANES)
    if want_spec:
        for p in range(focal):
            out_ref[p] = held[pl.ds(p, k, stride=focal), :].astype(BF16)
        return
    for p in range(0, focal, 2):
        pair = [held[pl.ds(p + q, k, stride=focal), :].astype(BF16) for q in range(2)]
        onset = [onset_ref[p + q : p + q + 1, columns] for q in range(2)]
        spectrum = windowed_spectrum(pair, onset, forward_ref[...], inverse_ref[...])
        for q in range(2):
            result[pl.ds(p + q, k, stride=focal), :] = spectrum[:, q * LANES : (q + 1) * LANES]
    final = result[...].reshape(NFW, 2, focal, LANES)
    if base_ref is not None:
        final += base_ref[...].astype(F32)
    out_ref[...] = final.astype(BF16)


def window(parts, forward, inverse, onset_times, base=None, want_spec=False):
    focal = parts[0].shape[2]
    k = 2 * NFW
    operands = [forward, inverse, onset_times, *parts] + ([] if base is None else [base])
    out = jax.ShapeDtypeStruct((NFW, 2, focal, LANES), BF16)
    if want_spec:
        out = jax.ShapeDtypeStruct((focal, k, LANES), BF16)
    return pl.pallas_call(
        functools.partial(window_kernel, len(parts), base is not None, want_spec),
        in_specs=[VMEM] * len(operands),
        out_specs=VMEM,
        out_shape=out,
        scratch_shapes=[pltpu.VMEM((k * focal, LANES), F32)] * 2,
        compiler_params=limit(8),
        cost_estimate=pl.CostEstimate(
            flops=4 * k * NT * focal * LANES, bytes_accessed=2 * k * focal * LANES * 6, transcendentals=0
        ),
        name="window",
    )(*operands)


def window_at_kernel(line, flip, step, forward_ref, inverse_ref, onset_ref, spec_ref, out_ref, result):
    core = own_place(line)[3]
    focal, k, _ = spec_ref.shape
    start = chip_columns(line, False, flip, step) + core * LANES
    columns = pl.ds(pl.multiple_of(start, LANES), LANES)
    for p in range(0, focal, 2):
        onset = [onset_ref[p + q : p + q + 1, columns] for q in range(2)]
        pair = [spec_ref[p + q] for q in range(2)]
        spectrum = windowed_spectrum(pair, onset, forward_ref[...], inverse_ref[...])
        for q in range(2):
            result[pl.ds(p + q, k, stride=focal), :] = spectrum[:, q * LANES : (q + 1) * LANES]
    out_ref[...] = result[...].reshape(NFW, 2, focal, LANES).astype(BF16)


def window_at(spec, forward, inverse, onset_times, line, flip, step):
    focal, k, _ = spec.shape
    return pl.pallas_call(
        functools.partial(window_at_kernel, line, flip, step),
        in_specs=[VMEM] * 4,
        out_specs=VMEM,
        out_shape=jax.ShapeDtypeStruct((NFW, 2, focal, LANES), BF16),
        scratch_shapes=[pltpu.VMEM((k * focal, LANES), F32)],
        compiler_params=limit(8),
        cost_estimate=pl.CostEstimate(
            flops=4 * k * NT * focal * LANES, bytes_accessed=2 * k * focal * LANES * 6, transcendentals=0
        ),
        name="window_at",
    )(forward, inverse, onset_times, spec)


def half_field_kernel(line, inverse_ref, onset_ref, *refs):
    core = own_place(line)[3]
    places = relative(line)
    own, (keep, send) = refs[: len(places)], refs[len(places) :]
    focal = keep.shape[0]
    samples = keep.shape[1]
    first = (lax.axis_index("blk") // 2) * (2 * samples)
    time = first + lax.broadcasted_iota(jnp.int32, (2 * samples, 2 * LANES), 0)

    for p in range(focal):
        for at in range(0, len(places), 2):
            onset = []
            for flip, step in places[at : at + 2]:
                start = chip_columns(line, False, flip, step) + core * LANES
                onset.append(onset_ref[p : p + 1, pl.ds(pl.multiple_of(start, LANES), LANES)])
            spec = jnp.concatenate([own[at][p], own[at + 1][p]], axis=1)
            values = jnp.dot(inverse_ref[...], spec, preferred_element_type=F32)
            values = jnp.where(time < jnp.concatenate(onset, axis=1), values, 0.0)
            low, high = values[:samples].astype(BF16), values[samples:].astype(BF16)
            columns = pl.ds(at * LANES, 2 * LANES)
            keep[p, :, columns] = jnp.where(core == 0, low, high)
            send[p, :, columns] = jnp.where(core == 0, high, low)


def half_field(own, inverse, onset_times, line):
    own = sum(own, [])
    focal, k, _ = own[0].shape
    shape = (focal, inverse.shape[0] // 2, len(own) * LANES)
    return pl.pallas_call(
        functools.partial(half_field_kernel, line),
        in_specs=[VMEM] * (2 + len(own)),
        out_specs=[VMEM] * 2,
        out_shape=[jax.ShapeDtypeStruct(shape, BF16)] * 2,
        compiler_params=limit(4),
        cost_estimate=pl.CostEstimate(
            flops=4 * k * math.prod(shape), bytes_accessed=4 * math.prod(shape), transcendentals=0
        ),
        name="half_field",
    )(inverse, onset_times, *own)


def merge_kernel(line, mine, theirs, out_ref, made, sems):
    core = own_place(line)[3]
    copy, rows = strip_copies(made, out_ref, sems, STRIPS)

    def body(strip, carry):
        for row in range(rows):
            p = strip * rows + row
            for at, (flip, step) in enumerate(relative(line)):
                columns = pl.ds(chip_columns(line, False, flip, step), 2 * LANES)
                part = pl.ds(at * LANES, LANES)
                made[p, :, columns] = join_cores(core, mine[p, :, part], theirs[p, :, part])
        copy(strip).start()
        return carry

    lax.fori_loop(0, STRIPS, body, 0)
    for strip in range(STRIPS):
        copy(strip).wait()


def merge(mine, theirs, line):
    focal, samples, width = mine.shape
    shape = (focal, samples, 2 * width)
    return pl.pallas_call(
        functools.partial(merge_kernel, line),
        in_specs=[VMEM] * 2,
        out_specs=ANY,
        out_shape=jax.ShapeDtypeStruct(shape, BF16),
        scratch_shapes=[pltpu.VMEM(shape, BF16), pltpu.SemaphoreType.DMA((STRIPS,))],
        compiler_params=limit(6),
        cost_estimate=pl.CostEstimate(flops=0, bytes_accessed=8 * mine.size, transcendentals=0),
        name="merge",
    )(mine, theirs)


def field_kernel(line, has_plus, inverse_ref, onset_ref, *refs):
    core = own_place(line)[3]
    places = relative(line)
    own, other = refs[: len(places)], refs[len(places) : 2 * len(places)]
    rest = list(refs[2 * len(places) :])
    plus_ref = rest.pop(0) if has_plus else None
    out_ref, made, out_sems, *spare = rest
    samples = out_ref.shape[1]
    out_copy, rows = strip_copies(made, out_ref, out_sems, STRIPS)
    if has_plus:
        plus, plus_sems = spare
        plus_copy, _ = strip_copies(plus_ref, plus, plus_sems, STRIPS)
        for strip in range(STRIPS):
            plus_copy(strip).start()
    time = lax.axis_index("blk") * samples + lax.broadcasted_iota(jnp.int32, (samples, 2 * LANES), 0)

    def body(strip, carry):
        if has_plus:
            plus_copy(strip).wait()
        for row in range(rows):
            p = strip * rows + row
            for at, (flip, step) in enumerate(places):
                columns = pl.ds(chip_columns(line, False, flip, step), 2 * LANES)
                spec = join_cores(core, own[at][p], other[at][p])
                values = jnp.dot(inverse_ref[...], spec, preferred_element_type=F32)
                values = jnp.where(time < onset_ref[pl.ds(p, 1), columns], values, 0.0)
                if has_plus:
                    values += plus[p, :, columns].astype(F32)
                made[p, :, columns] = values.astype(BF16)
        out_copy(strip).start()
        return carry

    lax.fori_loop(0, STRIPS, body, 0)
    for strip in range(STRIPS):
        out_copy(strip).wait()


def field(own, other, inverse, onset_times, line, plus_start=None):
    own, other = sum(own, []), sum(other, [])
    focal, k, _ = own[0].shape
    samples = inverse.shape[0]
    shape = (focal, samples, onset_times.shape[1])
    plus = [] if plus_start is None else [plus_start]
    moved = [pltpu.VMEM(shape, BF16), pltpu.SemaphoreType.DMA((STRIPS,))]
    return pl.pallas_call(
        functools.partial(field_kernel, line, bool(plus)),
        in_specs=[VMEM] * (2 + len(own) + len(other)) + [ANY] * len(plus),
        out_specs=ANY,
        out_shape=jax.ShapeDtypeStruct(shape, BF16),
        scratch_shapes=moved * (1 + len(plus)),
        compiler_params=limit(12),
        cost_estimate=pl.CostEstimate(
            flops=2 * k * math.prod(shape),
            bytes_accessed=4 * math.prod(shape) + 2 * k * focal * shape[2],
            transcendentals=0,
        ),
        name="field",
    )(inverse, onset_times, *own, *other, *plus)


def add(*parts):
    total = parts[0].astype(F32)
    for part in parts[1:]:
        total += part.astype(F32)
    return total


def after(value, *others):
    return lax.optimization_barrier((value, *others))[0] if others else value


def reduce_scatter(places, keep0, keep1, send0, send1):
    size = places.line
    got1 = places.send(send1, places.core())
    got0 = places.send(send0, places.core())
    far = [add(keep, got).astype(BF16) for keep, got in zip(keep1, got1)]
    across = {step: places.send(far[step], places.pair()) for step in range(2, size)}
    beside = [places.send(far[1], places.shift(1))] if size > 1 else []
    parts = [keep0[0], got0[0]]

    def pass_on(steps, shift, *first):
        carried, sent = [], []
        for step in steps:
            crossed = [after(across[step], *first)] if step in across else []
            carried = [places.send(add(keep0[step], got0[step], *crossed, *carried).astype(BF16), places.shift(shift))]
            sent += carried
        return sent

    ahead = pass_on(range(size // 2, 0, -1), 1)
    behind = pass_on(range(size // 2 + 1, size), size - 1, *ahead[:1])
    parts += ahead[-1:] + behind[-1:]
    across[0] = places.send(add(keep1[0], got1[0], *beside).astype(BF16), places.pair())
    return parts + [across[0]]


def gather_chips(places, block, work=None):
    size = places.line
    near = [1, size - 1] if size > 2 else [1] if size > 1 else []
    far = list(range(2, size - 1))
    made = {}

    def run(flip, steps, pieces, *others):
        if work is None:
            return []
        for step in steps:
            made[flip, step] = work(after(pieces[step], *others), flip, step)
        return [made[flip, step] for step in steps]

    line = {0: block}
    for step in near:
        line[step] = places.send(block, places.shift(step))
    across = {0: places.send(block, places.pair())}
    own = run(0, [0], line)
    for step in range(2, size // 2 + 1):
        line[step] = places.send(after(line[step - 1], across[0], *own), places.shift(1))
    for step in range(size - 2, size // 2, -1):
        line[step] = places.send(after(line[step + 1], *own), places.shift(size - 1))
    for step in near:
        if step == 1:
            across[step] = places.send(across[0], places.shift(1))
        else:
            across[step] = places.send(line[step], places.pair())
    middle = run(1, [0], across) + run(0, near, line)
    for step in far:
        across[step] = places.send(after(line[step], *middle), places.pair())
    late = run(0, far, line) + run(1, near, across)
    run(1, far, across, *late)
    pieces = [[side[step] for step in range(size)] for side in (line, across)]
    results = [[made[flip, step] for step in range(size)] for flip in range(2)] if work else None
    return pieces, results


def swap_cores(places, pieces):
    return [places.send(piece, places.core()) for piece in pieces]


def local(plus_start, reflection, onset_times):
    size = lax.axis_size("blk")
    places = Places("blk", size)
    line = places.line
    focal, samples, _ = plus_start.shape
    forward, inverse = tables_of(jnp.arange(NT, dtype=jnp.int32))
    own_samples = lax.axis_index("blk") * samples + jnp.arange(samples, dtype=jnp.int32)
    own_forward, own_inverse = tables_of(own_samples)
    chip_samples = lax.axis_index("blk") // 2 * (2 * samples) + jnp.arange(2 * samples, dtype=jnp.int32)
    _, chip_inverse = tables_of(chip_samples)
    sure = contract("kt,tj->kj", forward[:, :SURE], inverse[:SURE]).astype(BF16)
    forward = jnp.concatenate([forward[:, SURE:], sure], axis=1)
    inverse = inverse[SURE:]

    def window_piece(piece, flip, step):
        return window_at(piece, forward, inverse, onset_times, line, flip, step)

    parts = reduce_scatter(places, *first_analysis(plus_start, own_forward, line))
    start = add(*parts).astype(BF16)
    start = jnp.transpose(start, (1, 0, 2)).reshape(NFW, 2, focal, LANES)
    spectrum_plus = start
    for iteration in range(ITERS):
        last = iteration + 1 == ITERS
        parts = reduce_scatter(places, *convolve(spectrum_plus, reflection, line))
        windowed = window(parts, forward, inverse, onset_times, want_spec=last)
        if last:
            upgoing_spec, own = gather_chips(places, windowed, window_piece)
            other = [swap_cores(places, side) for side in own]
            downgoing_spec = correlate_all(own, other, reflection, line)
            break
        own, _ = gather_chips(places, windowed)
        half = correlate(own[0], swap_cores(places, own[0]), reflection, line, 0)
        across = [own[1][step] if step in (0, line - 1) else after(own[1][step], half) for step in range(line)]
        downgoing_spec = correlate(own[1], swap_cores(places, across), reflection, line, 1, half)
        spectrum_plus = window([downgoing_spec], forward, inverse, onset_times, base=start)
    mine, theirs = half_field(upgoing_spec, chip_inverse, onset_times, line)
    theirs = places.send(theirs, places.core())

    def before_far(piece, flip, step):
        return mine if (flip, step) == (1, 0) else piece

    own, _ = gather_chips(places, downgoing_spec, before_far)
    upgoing = merge(mine, theirs, line)
    other = [swap_cores(places, own[0])]
    across = [own[1][step] if step in (0, 1, line - 1) else after(own[1][step], upgoing) for step in range(line)]
    other.append(swap_cores(places, across))
    downgoing = field(own, other, own_inverse, onset_times, line, plus_start)
    return upgoing, downgoing


def analyze(values, forward):
    total = jnp.einsum("kt,ptx->kpx", forward, values, preferred_element_type=F32)
    return total.reshape(NFW, 2, values.shape[0], values.shape[2])


def synthesize(spectrum, inverse):
    flat = spectrum.reshape(2 * NFW, spectrum.shape[2], spectrum.shape[3])
    return jnp.einsum("tk,kpx->ptx", inverse, flat, preferred_element_type=F32)


def contract(form, left, right):
    return jnp.einsum(form, left, right, preferred_element_type=F32)


def local_any(plus_start, reflection, onset_times):
    samples = plus_start.shape[1]
    width = reflection.shape[2]
    me = lax.axis_index("blk")
    forward, inverse = tables_of(jnp.arange(NT, dtype=jnp.int32))
    own_forward, own_inverse = tables_of(me * samples + jnp.arange(samples, dtype=jnp.int32))
    onset = lax.dynamic_slice_in_dim(onset_times, me * width, width, 1)
    keep = jnp.arange(NT, dtype=jnp.int32)[None, :, None] < onset[:, None, :]
    time = me * samples + jnp.arange(samples, dtype=jnp.int32)
    own_keep = time[None, :, None] < onset_times[:, None, :]

    def scatter(partial):
        return lax.psum_scatter(partial.astype(BF16), "blk", scatter_dimension=3, tiled=True).astype(BF16)

    def gather(block):
        return lax.all_gather(block, "blk", axis=3, tiled=True)

    start = scatter(analyze(plus_start, own_forward))
    spectrum = start
    for iteration in range(ITERS):
        real = contract("wrs,wpr->wps", reflection[0], spectrum[:, 0]) - contract(
            "wrs,wpr->wps", reflection[1], spectrum[:, 1]
        )
        imag = contract("wrs,wpr->wps", reflection[0], spectrum[:, 1]) + contract(
            "wrs,wpr->wps", reflection[1], spectrum[:, 0]
        )
        upgoing_spec = scatter(jnp.stack([real, imag], axis=1))
        kept = jnp.where(keep, synthesize(upgoing_spec, inverse), 0.0).astype(BF16)
        minus = gather(analyze(kept, forward).astype(BF16))
        real = contract("wrs,wps->wpr", reflection[0], minus[:, 0]) + contract(
            "wrs,wps->wpr", reflection[1], minus[:, 1]
        )
        imag = contract("wrs,wps->wpr", reflection[0], minus[:, 1]) - contract(
            "wrs,wps->wpr", reflection[1], minus[:, 0]
        )
        downgoing_spec = jnp.stack([real, imag], axis=1).astype(BF16)
        if iteration + 1 < ITERS:
            kept = jnp.where(keep, synthesize(downgoing_spec, inverse), 0.0).astype(BF16)
            spectrum = (start.astype(F32) + analyze(kept, forward)).astype(BF16)
    upgoing = jnp.where(own_keep, synthesize(gather(upgoing_spec), own_inverse), 0.0).astype(BF16)
    change = jnp.where(own_keep, synthesize(gather(downgoing_spec), own_inverse), 0.0)
    return upgoing, (plus_start.astype(F32) + change).astype(BF16)


def solution(mesh):
    size = mesh.shape["blk"]

    def run(plus_start, reflection, onset_times):
        width = reflection.shape[2] // size
        fits = width == LANES and size % 4 == 0 and (plus_start.shape[1] // size) % 16 == 0
        return jax.shard_map(
            local if fits else local_any,
            mesh=mesh,
            in_specs=(P("groups", "blk", None), P(None, None, "blk", None), P("groups", None)),
            out_specs=(P("groups", "blk", None), P("groups", "blk", None)),
            check_vma=False,
        )(plus_start, reflection, onset_times)

    return run
```

```python
import functools
import math

import jax
import jax.numpy as jnp
from jax import lax
from jax.experimental import pallas as pl
from jax.experimental.pallas import tpu as pltpu
from jax.sharding import PartitionSpec as P

NT = 512
NFW = 32
FREQ0 = 16
ITERS = 2
SURE = 128
LANES = 128
F32 = jnp.float32
BF16 = jnp.bfloat16


def basis_of(samples):
    freqs = FREQ0 + jnp.arange(NFW, dtype=jnp.int32)
    turns = freqs[:, None] * samples[None, :] % NT
    phase = turns.astype(F32) * (2.0 * math.pi / NT)
    return jnp.stack([jnp.cos(phase), -jnp.sin(phase)], axis=1)


def tables_of(samples):
    basis = basis_of(samples).reshape(2 * NFW, samples.shape[0])
    forward = (basis * (1.0 / math.sqrt(NT))).astype(BF16)
    inverse = (basis * math.sqrt(2.0 / NFW)).astype(BF16)
    return forward, inverse.T


class Places:
    def __init__(self, axis, size):
        self.axis = axis
        self.size = size
        self.line = size // 4

    def core(self):
        return [(b, b ^ 1) for b in range(self.size)]

    def pair(self):
        return [(b, b ^ 2) for b in range(self.size)]

    def shift(self, step):
        return [(b, (b // 4 + step) % self.line * 4 + b % 4) for b in range(self.size)]

    def send(self, array, pairs):
        return lax.ppermute(array, self.axis, pairs)


def own_place(line):
    me = lax.axis_index("blk")
    return me, me // 4, (me // 2) % 2, me % 2


def chip_columns(line, ahead, flip, step):
    _, l, m, _ = own_place(line)
    other = lax.rem(l + step, line) if ahead else lax.rem(l - step + line, line)
    chip = other * 2 + (lax.rem(m + flip, 2))
    return pl.multiple_of(chip * (2 * LANES), 2 * LANES)


def relative(line):
    return [(flip, step) for flip in range(2) for step in range(line)]


def split_cores(core, block):
    low, high = block[:, :LANES], block[:, LANES:]
    first = core == 0
    return jnp.where(first, low, high), jnp.where(first, high, low)


def join_cores(core, own, other):
    first = core == 0
    return jnp.concatenate([jnp.where(first, own, other), jnp.where(first, other, own)], axis=1)


VMEM = pl.BlockSpec(memory_space=pltpu.VMEM)
ANY = pl.BlockSpec(memory_space=pl.ANY)
CHUNKS = 8
STRIPS = 4
SLOTS = 4


def limit(mebibytes):
    return pltpu.CompilerParams(vmem_limit_bytes=mebibytes << 20)


def strip_copies(source, target, sems, strips):
    rows = source.shape[0] // strips

    def copy(strip):
        part = pl.ds(strip * rows, rows)
        return pltpu.make_async_copy(source.at[part], target.at[part], sems.at[strip])

    return copy, rows


def analysis_kernel(line, forward_ref, plus_ref, keep0, keep1, send0, send1, held, sems):
    core = own_place(line)[3]
    keep, send = (keep0, keep1), (send0, send1)
    copy, rows = strip_copies(plus_ref, held, sems, STRIPS)
    for strip in range(STRIPS):
        copy(strip).start()

    def body(strip, carry):
        copy(strip).wait()
        for row in range(rows):
            p = strip * rows + row
            for flip, step in relative(line):
                columns = pl.ds(chip_columns(line, True, flip, step), 2 * LANES)
                block = jnp.dot(forward_ref[...], held[p, :, columns], preferred_element_type=F32)
                mine, theirs = split_cores(core, block.astype(BF16))
                keep[flip][step, p] = mine
                send[flip][step, p] = theirs
        return carry

    lax.fori_loop(0, STRIPS, body, 0)


def first_analysis(plus_start, forward, line):
    focal, samples, width = plus_start.shape
    out = jax.ShapeDtypeStruct((line, focal, 2 * NFW, LANES), BF16)
    return pl.pallas_call(
        functools.partial(analysis_kernel, line),
        in_specs=[VMEM, ANY],
        out_specs=[VMEM] * 4,
        out_shape=[out] * 4,
        scratch_shapes=[pltpu.VMEM(plus_start.shape, BF16), pltpu.SemaphoreType.DMA((STRIPS,))],
        compiler_params=limit(8),
        cost_estimate=pl.CostEstimate(
            flops=4 * NFW * focal * samples * width,
            bytes_accessed=2 * focal * samples * width + 4 * NFW * focal * width,
            transcendentals=0,
        ),
        name="first_analysis",
    )(forward, plus_start)


def fetch_panels(line, ahead, flip, panel_ref, held, sems):
    chunks, _, _, rows = held.shape[:4]

    def copy(chunk, step):
        columns = pl.ds(chip_columns(line, ahead, flip, step), 2 * LANES)
        source = panel_ref.at[:, pl.ds(chunk * rows, rows), :, columns]
        return pltpu.make_async_copy(source, held.at[chunk, step], sems.at[chunk, step])

    for chunk in range(chunks):
        for step in range(line):
            copy(chunk, step).start()

    def wait(chunk):
        for step in range(line):
            copy(chunk, step).wait()

    return wait


def panel_scratch(line):
    rows = NFW // CHUNKS
    return [
        pltpu.VMEM((CHUNKS, line, 2, rows, LANES, 2 * LANES), BF16),
        pltpu.SemaphoreType.DMA((CHUNKS, line)),
    ]


def convolve_kernel(line, spec_ref, panel_ref, keep0, keep1, send0, send1, held, sems):
    core = own_place(line)[3]
    keep, send = (keep0, keep1), (send0, send1)
    focal = spec_ref.shape[2]
    rows = NFW // CHUNKS

    slots = held.shape[0]

    def copy(chunk):
        slot = lax.rem(chunk, slots)
        part = pl.ds(chunk * rows, rows)
        return pltpu.make_async_copy(panel_ref.at[:, part], held.at[slot], sems.at[slot])

    for chunk in range(slots):
        copy(chunk).start()

    def body(chunk, carry):
        copy(chunk).wait()
        slot = lax.rem(chunk, slots)
        for row in range(rows):
            w = chunk * rows + row
            real, imag = spec_ref[w, 0], spec_ref[w, 1]
            left = jnp.concatenate(
                [jnp.concatenate([real, -imag], axis=1), jnp.concatenate([imag, real], axis=1)], axis=0
            )
            for flip, step in relative(line):
                columns = pl.ds(chip_columns(line, True, flip, step), 2 * LANES)
                panel = held[slot, :, row, :, columns].reshape(2 * LANES, 2 * LANES)
                block = jnp.dot(left, panel, preferred_element_type=F32)
                mine, theirs = split_cores(core, block.astype(BF16))
                keep[flip][step, w] = mine.reshape(2, focal, LANES)
                send[flip][step, w] = theirs.reshape(2, focal, LANES)

        @pl.when(chunk + slots < CHUNKS)
        def _():
            copy(chunk + slots).start()

        return carry

    lax.fori_loop(0, CHUNKS, body, 0)


def panel_cost(focal, sources):
    return pl.CostEstimate(
        flops=8 * NFW * focal * LANES * sources,
        bytes_accessed=4 * NFW * sources * (LANES + focal),
        transcendentals=0,
    )


def convolve(spectrum, reflection, line):
    focal = spectrum.shape[2]
    out = jax.ShapeDtypeStruct((line, NFW, 2, focal, LANES), BF16)
    return pl.pallas_call(
        functools.partial(convolve_kernel, line),
        in_specs=[VMEM, ANY],
        out_specs=[VMEM] * 4,
        out_shape=[out] * 4,
        scratch_shapes=[
            pltpu.VMEM((SLOTS, 2, NFW // CHUNKS, LANES, reflection.shape[3]), BF16),
            pltpu.SemaphoreType.DMA((SLOTS,)),
        ],
        compiler_params=limit(20),
        cost_estimate=panel_cost(focal, reflection.shape[3]),
        name="convolve",
    )(spectrum, reflection)


def correlate_kernel(line, flip, has_base, final, *refs):
    core = own_place(line)[3]
    own, other, panel_ref = refs[:line], refs[line : 2 * line], refs[2 * line]
    base_ref = refs[2 * line + 1] if has_base else None
    out_ref, held, sems, *spare = refs[2 * line + 1 + has_base :]
    focal = own[0].shape[2]
    rows = held.shape[3]
    wait = fetch_panels(line, False, flip, panel_ref, held, sems)

    def body(chunk, carry):
        wait(chunk)
        for row in range(rows):
            w = chunk * rows + row
            panels, specs = [], []
            for step in range(line):
                panels.append(held[chunk, step, :, row].reshape(2 * LANES, 2 * LANES))
                mine, theirs = own[step][w], other[step][w]
                specs.append(
                    join_cores(core, mine.reshape(2 * focal, LANES), theirs.reshape(2 * focal, LANES))
                )
            total = lax.dot_general(
                jnp.concatenate(specs, axis=1),
                jnp.concatenate(panels, axis=1),
                (((1,), (1,)), ((), ())),
                preferred_element_type=F32,
            )
            real = total[:focal, :LANES] + total[focal:, LANES:]
            imag = total[focal:, :LANES] - total[:focal, LANES:]
            if has_base:
                real += base_ref[w, 0]
                imag += base_ref[w, 1]
            if final:
                spare[0][pl.ds(2 * w * focal, focal), :] = real
                spare[0][pl.ds((2 * w + 1) * focal, focal), :] = imag
            else:
                out_ref[w, 0] = real
                out_ref[w, 1] = imag
        return carry

    lax.fori_loop(0, CHUNKS, body, 0)
    if final:
        for p in range(focal):
            out_ref[p] = spare[0][pl.ds(p, 2 * NFW, stride=focal), :].astype(BF16)


def correlate(own, other, reflection, line, flip, base=None, final=False):
    focal = own[0].shape[2]
    more = [] if base is None else [base]
    shape = jax.ShapeDtypeStruct((NFW, 2, focal, LANES), F32)
    if final:
        shape = jax.ShapeDtypeStruct((focal, 2 * NFW, LANES), BF16)
    spare = [pltpu.VMEM((2 * NFW * focal, LANES), F32)] if final else []
    return pl.pallas_call(
        functools.partial(correlate_kernel, line, flip, bool(more), final),
        in_specs=[VMEM] * (2 * line) + [ANY] + [VMEM] * len(more),
        out_specs=VMEM,
        out_shape=shape,
        scratch_shapes=panel_scratch(line) + spare,
        compiler_params=limit(24),
        cost_estimate=panel_cost(focal, reflection.shape[3] // 2),
        name=f"correlate{flip}",
    )(*own, *other, reflection, *more)


def windowed_spectrum(pair, onset, forward, inverse):
    time = SURE + lax.broadcasted_iota(jnp.int32, (NT - SURE, 2 * LANES), 0)
    spectra = jnp.concatenate(pair, axis=1)
    values = jnp.dot(inverse, spectra, preferred_element_type=F32)
    kept = jnp.where(time < jnp.concatenate(onset, axis=1), values, 0.0).astype(BF16)
    return jnp.dot(forward, jnp.concatenate([kept, spectra], axis=0), preferred_element_type=F32)


def window_kernel(parts, has_base, want_spec, *refs):
    refs = list(refs)
    forward_ref, inverse_ref, onset_ref = refs[:3]
    part_refs = refs[3 : 3 + parts]
    rest = refs[3 + parts :]
    base_ref = rest.pop(0) if has_base else None
    out_ref = rest.pop(0)
    held, result = rest
    focal = part_refs[0].shape[2]
    k = 2 * NFW
    total = part_refs[0][...].astype(F32)
    for ref in part_refs[1:]:
        total += ref[...].astype(F32)
    held[...] = total.reshape(k * focal, LANES)
    me = lax.axis_index("blk")
    columns = pl.ds(pl.multiple_of(me * LANES, LANES), LANES)
    if want_spec:
        for p in range(focal):
            out_ref[p] = held[pl.ds(p, k, stride=focal), :].astype(BF16)
        return
    for p in range(0, focal, 2):
        pair = [held[pl.ds(p + q, k, stride=focal), :].astype(BF16) for q in range(2)]
        onset = [onset_ref[p + q : p + q + 1, columns] for q in range(2)]
        spectrum = windowed_spectrum(pair, onset, forward_ref[...], inverse_ref[...])
        for q in range(2):
            result[pl.ds(p + q, k, stride=focal), :] = spectrum[:, q * LANES : (q + 1) * LANES]
    final = result[...].reshape(NFW, 2, focal, LANES)
    if base_ref is not None:
        final += base_ref[...].astype(F32)
    out_ref[...] = final.astype(BF16)


def window(parts, forward, inverse, onset_times, base=None, want_spec=False):
    focal = parts[0].shape[2]
    k = 2 * NFW
    operands = [forward, inverse, onset_times, *parts] + ([] if base is None else [base])
    out = jax.ShapeDtypeStruct((NFW, 2, focal, LANES), BF16)
    if want_spec:
        out = jax.ShapeDtypeStruct((focal, k, LANES), BF16)
    return pl.pallas_call(
        functools.partial(window_kernel, len(parts), base is not None, want_spec),
        in_specs=[VMEM] * len(operands),
        out_specs=VMEM,
        out_shape=out,
        scratch_shapes=[pltpu.VMEM((k * focal, LANES), F32)] * 2,
        compiler_params=limit(8),
        cost_estimate=pl.CostEstimate(
            flops=4 * k * NT * focal * LANES, bytes_accessed=2 * k * focal * LANES * 6, transcendentals=0
        ),
        name="window",
    )(*operands)


def window_at_kernel(line, flip, step, begun, *refs):
    forward_ref, inverse_ref, onset_ref, chip_inverse_ref, spec_ref = refs[:5]
    out_ref, keep_ref, send_ref, result, made, sems = refs[5 + 2 * begun :]
    core = own_place(line)[3]
    focal, k, _ = spec_ref.shape
    start = chip_columns(line, False, flip, step) + core * LANES
    columns = pl.ds(pl.multiple_of(start, LANES), LANES)
    samples = made.shape[2]
    first = (lax.axis_index("blk") // 2) * (2 * samples)
    time = first + lax.broadcasted_iota(jnp.int32, (2 * samples, 2 * LANES), 0)

    def pair_of(p):
        onset = [onset_ref[p + q : p + q + 1, columns] for q in range(2)]
        return [spec_ref[p + q] for q in range(2)], onset

    for p in range(0, focal, 2):
        pair, onset = pair_of(p)
        values = jnp.dot(
            chip_inverse_ref[...], jnp.concatenate(pair, axis=1), preferred_element_type=F32
        )
        values = jnp.where(time < jnp.concatenate(onset, axis=1), values, 0.0).astype(BF16)
        low, high = values[:samples], values[samples:]
        mine, theirs = jnp.where(core == 0, low, high), jnp.where(core == 0, high, low)
        for q in range(2):
            part = slice(q * LANES, (q + 1) * LANES)
            made[0, p + q] = mine[:, part]
            made[1, p + q] = theirs[:, part]
    place = pl.ds((flip * line + step) * LANES, LANES)
    copies = [
        pltpu.make_async_copy(made.at[side], target.at[:, :, place], sems.at[side])
        for side, target in enumerate((keep_ref, send_ref))
    ]
    for copy in copies:
        copy.start()
    for p in range(0, focal, 2):
        pair, onset = pair_of(p)
        spectrum = windowed_spectrum(pair, onset, forward_ref[...], inverse_ref[...])
        for q in range(2):
            result[pl.ds(p + q, k, stride=focal), :] = spectrum[:, q * LANES : (q + 1) * LANES]
    out_ref[...] = result[...].reshape(NFW, 2, focal, LANES).astype(BF16)
    for copy in copies:
        copy.wait()


def window_at(spec, forward, inverse, onset_times, chip_inverse, line, flip, step, fields):
    focal, k, _ = spec.shape
    samples = chip_inverse.shape[0] // 2
    field_shape = jax.ShapeDtypeStruct((focal, samples, 2 * line * LANES), BF16)
    begun = bool(fields)
    return pl.pallas_call(
        functools.partial(window_at_kernel, line, flip, step, begun),
        in_specs=[VMEM] * 5 + [ANY] * len(fields),
        out_specs=[VMEM, ANY, ANY],
        out_shape=[jax.ShapeDtypeStruct((NFW, 2, focal, LANES), BF16), field_shape, field_shape],
        input_output_aliases={5: 1, 6: 2} if begun else {},
        scratch_shapes=[
            pltpu.VMEM((k * focal, LANES), F32),
            pltpu.VMEM((2, focal, samples, LANES), BF16),
            pltpu.SemaphoreType.DMA((2,)),
        ],
        compiler_params=limit(8),
        cost_estimate=pl.CostEstimate(
            flops=4 * k * NT * focal * LANES, bytes_accessed=2 * k * focal * LANES * 6, transcendentals=0
        ),
        name="window_at",
    )(forward, inverse, onset_times, chip_inverse, spec, *fields)


def merge_kernel(line, mine, theirs, out_ref, made, sems):
    core = own_place(line)[3]
    copy, rows = strip_copies(made, out_ref, sems, STRIPS)

    def body(strip, carry):
        for row in range(rows):
            p = strip * rows + row
            for at, (flip, step) in enumerate(relative(line)):
                columns = pl.ds(chip_columns(line, False, flip, step), 2 * LANES)
                part = pl.ds(at * LANES, LANES)
                made[p, :, columns] = join_cores(core, mine[p, :, part], theirs[p, :, part])
        copy(strip).start()
        return carry

    lax.fori_loop(0, STRIPS, body, 0)
    for strip in range(STRIPS):
        copy(strip).wait()


def merge(mine, theirs, line):
    focal, samples, width = mine.shape
    shape = (focal, samples, 2 * width)
    return pl.pallas_call(
        functools.partial(merge_kernel, line),
        in_specs=[VMEM] * 2,
        out_specs=ANY,
        out_shape=jax.ShapeDtypeStruct(shape, BF16),
        scratch_shapes=[pltpu.VMEM(shape, BF16), pltpu.SemaphoreType.DMA((STRIPS,))],
        compiler_params=limit(6),
        cost_estimate=pl.CostEstimate(flops=0, bytes_accessed=8 * mine.size, transcendentals=0),
        name="merge",
    )(mine, theirs)


def field_kernel(line, has_plus, inverse_ref, onset_ref, *refs):
    core = own_place(line)[3]
    places = relative(line)
    own, other = refs[: len(places)], refs[len(places) : 2 * len(places)]
    rest = list(refs[2 * len(places) :])
    plus_ref = rest.pop(0) if has_plus else None
    out_ref, made, out_sems, *spare = rest
    samples = out_ref.shape[1]
    out_copy, rows = strip_copies(made, out_ref, out_sems, STRIPS)
    if has_plus:
        plus, plus_sems = spare
        plus_copy, _ = strip_copies(plus_ref, plus, plus_sems, STRIPS)
        for strip in range(STRIPS):
            plus_copy(strip).start()
    time = lax.axis_index("blk") * samples + lax.broadcasted_iota(jnp.int32, (samples, 2 * LANES), 0)

    def body(strip, carry):
        if has_plus:
            plus_copy(strip).wait()
        for row in range(rows):
            p = strip * rows + row
            for at, (flip, step) in enumerate(places):
                columns = pl.ds(chip_columns(line, False, flip, step), 2 * LANES)
                spec = join_cores(core, own[at][p], other[at][p])
                values = jnp.dot(inverse_ref[...], spec, preferred_element_type=F32)
                values = jnp.where(time < onset_ref[pl.ds(p, 1), columns], values, 0.0)
                if has_plus:
                    values += plus[p, :, columns].astype(F32)
                made[p, :, columns] = values.astype(BF16)
        out_copy(strip).start()
        return carry

    lax.fori_loop(0, STRIPS, body, 0)
    for strip in range(STRIPS):
        out_copy(strip).wait()


def field(own, other, inverse, onset_times, line, plus_start=None):
    own, other = sum(own, []), sum(other, [])
    focal, k, _ = own[0].shape
    samples = inverse.shape[0]
    shape = (focal, samples, onset_times.shape[1])
    plus = [] if plus_start is None else [plus_start]
    moved = [pltpu.VMEM(shape, BF16), pltpu.SemaphoreType.DMA((STRIPS,))]
    return pl.pallas_call(
        functools.partial(field_kernel, line, bool(plus)),
        in_specs=[VMEM] * (2 + len(own) + len(other)) + [ANY] * len(plus),
        out_specs=ANY,
        out_shape=jax.ShapeDtypeStruct(shape, BF16),
        scratch_shapes=moved * (1 + len(plus)),
        compiler_params=limit(12),
        cost_estimate=pl.CostEstimate(
            flops=2 * k * math.prod(shape),
            bytes_accessed=4 * math.prod(shape) + 2 * k * focal * shape[2],
            transcendentals=0,
        ),
        name="field",
    )(inverse, onset_times, *own, *other, *plus)


def add(*parts):
    total = parts[0].astype(F32)
    for part in parts[1:]:
        total += part.astype(F32)
    return total


def after(value, *others):
    return lax.optimization_barrier((value, *others))[0] if others else value


def reduce_scatter(places, keep0, keep1, send0, send1):
    size = places.line
    got1 = places.send(send1, places.core())
    got0 = places.send(send0, places.core())
    far = [add(keep, got).astype(BF16) for keep, got in zip(keep1, got1)]
    across = {step: places.send(far[step], places.pair()) for step in range(2, size)}
    beside = [places.send(far[1], places.shift(1))] if size > 1 else []
    parts = [keep0[0], got0[0]]

    def pass_on(steps, shift, *first):
        carried, sent = [], []
        for step in steps:
            crossed = [after(across[step], *first)] if step in across else []
            carried = [places.send(add(keep0[step], got0[step], *crossed, *carried).astype(BF16), places.shift(shift))]
            sent += carried
        return sent

    ahead = pass_on(range(size // 2, 0, -1), 1)
    behind = pass_on(range(size // 2 + 1, size), size - 1, *ahead[:1])
    parts += ahead[-1:] + behind[-1:]
    across[0] = places.send(add(keep1[0], got1[0], *beside).astype(BF16), places.pair())
    return parts + [across[0]]


def gather_chips(places, block, work=None):
    size = places.line
    near = [1, size - 1] if size > 2 else [1] if size > 1 else []
    far = list(range(2, size - 1))
    made = {}

    def run(flip, steps, pieces, *others):
        if work is None:
            return []
        for step in steps:
            made[flip, step] = work(after(pieces[step], *others), flip, step)
        return [made[flip, step] for step in steps]

    line = {0: block}
    for step in near:
        line[step] = places.send(block, places.shift(step))
    across = {0: places.send(block, places.pair())}
    own = run(0, [0], line)
    for step in range(2, size // 2 + 1):
        line[step] = places.send(after(line[step - 1], across[0], *own), places.shift(1))
    for step in range(size - 2, size // 2, -1):
        line[step] = places.send(after(line[step + 1], *own), places.shift(size - 1))
    for step in near:
        if step == 1:
            across[step] = places.send(across[0], places.shift(1))
        else:
            across[step] = places.send(line[step], places.pair())
    middle = run(1, [0], across) + run(0, near, line)
    for step in far:
        across[step] = places.send(after(line[step], *middle), places.pair())
    late = run(0, far, line) + run(1, near, across)
    run(1, far, across, *late)
    pieces = [[side[step] for step in range(size)] for side in (line, across)]
    results = [[made[flip, step] for step in range(size)] for flip in range(2)] if work else None
    return pieces, results


def swap_cores(places, pieces):
    return [places.send(piece, places.core()) for piece in pieces]


def local(plus_start, reflection, onset_times):
    size = lax.axis_size("blk")
    places = Places("blk", size)
    line = places.line
    focal, samples, _ = plus_start.shape
    forward, inverse = tables_of(jnp.arange(NT, dtype=jnp.int32))
    own_samples = lax.axis_index("blk") * samples + jnp.arange(samples, dtype=jnp.int32)
    own_forward, own_inverse = tables_of(own_samples)
    chip_samples = lax.axis_index("blk") // 2 * (2 * samples) + jnp.arange(2 * samples, dtype=jnp.int32)
    _, chip_inverse = tables_of(chip_samples)
    sure = contract("kt,tj->kj", forward[:, :SURE], inverse[:SURE]).astype(BF16)
    forward = jnp.concatenate([forward[:, SURE:], sure], axis=1)
    inverse = inverse[SURE:]

    fields = []

    def window_piece(piece, flip, step):
        spectrum, *fields[:] = window_at(
            piece, forward, inverse, onset_times, chip_inverse, line, flip, step, tuple(fields)
        )
        return spectrum

    parts = reduce_scatter(places, *first_analysis(plus_start, own_forward, line))
    start = add(*parts).astype(BF16)
    start = jnp.transpose(start, (1, 0, 2)).reshape(NFW, 2, focal, LANES)
    spectrum_plus = start
    for iteration in range(ITERS):
        last = iteration + 1 == ITERS
        parts = reduce_scatter(places, *convolve(spectrum_plus, reflection, line))
        windowed = window(parts, forward, inverse, onset_times, want_spec=last)
        if last:
            _, own = gather_chips(places, windowed, window_piece)
        else:
            own, _ = gather_chips(places, windowed)
        half = correlate(own[0], swap_cores(places, own[0]), reflection, line, 0)
        across = [own[1][step] if step in (0, line - 1) else after(own[1][step], half) for step in range(line)]
        downgoing_spec = correlate(own[1], swap_cores(places, across), reflection, line, 1, half, last)
        if not last:
            spectrum_plus = window([downgoing_spec], forward, inverse, onset_times, base=start)
    mine, theirs = fields
    theirs = places.send(after(theirs, downgoing_spec), places.core())
    own, _ = gather_chips(places, after(downgoing_spec, own_inverse))
    upgoing = merge(mine, theirs, line)
    other = [swap_cores(places, own[0])]
    across = [own[1][step] if step in (0, 1, line - 1) else after(own[1][step], upgoing) for step in range(line)]
    other.append(swap_cores(places, across))
    downgoing = field(own, other, own_inverse, onset_times, line, plus_start)
    return upgoing, downgoing


def analyze(values, forward):
    total = jnp.einsum("kt,ptx->kpx", forward, values, preferred_element_type=F32)
    return total.reshape(NFW, 2, values.shape[0], values.shape[2])


def synthesize(spectrum, inverse):
    flat = spectrum.reshape(2 * NFW, spectrum.shape[2], spectrum.shape[3])
    return jnp.einsum("tk,kpx->ptx", inverse, flat, preferred_element_type=F32)


def contract(form, left, right):
    return jnp.einsum(form, left, right, preferred_element_type=F32)


def local_any(plus_start, reflection, onset_times):
    samples = plus_start.shape[1]
    width = reflection.shape[2]
    me = lax.axis_index("blk")
    forward, inverse = tables_of(jnp.arange(NT, dtype=jnp.int32))
    own_forward, own_inverse = tables_of(me * samples + jnp.arange(samples, dtype=jnp.int32))
    onset = lax.dynamic_slice_in_dim(onset_times, me * width, width, 1)
    keep = jnp.arange(NT, dtype=jnp.int32)[None, :, None] < onset[:, None, :]
    time = me * samples + jnp.arange(samples, dtype=jnp.int32)
    own_keep = time[None, :, None] < onset_times[:, None, :]

    def scatter(partial):
        return lax.psum_scatter(partial.astype(BF16), "blk", scatter_dimension=3, tiled=True).astype(BF16)

    def gather(block):
        return lax.all_gather(block, "blk", axis=3, tiled=True)

    start = scatter(analyze(plus_start, own_forward))
    spectrum = start
    for iteration in range(ITERS):
        real = contract("wrs,wpr->wps", reflection[0], spectrum[:, 0]) - contract(
            "wrs,wpr->wps", reflection[1], spectrum[:, 1]
        )
        imag = contract("wrs,wpr->wps", reflection[0], spectrum[:, 1]) + contract(
            "wrs,wpr->wps", reflection[1], spectrum[:, 0]
        )
        upgoing_spec = scatter(jnp.stack([real, imag], axis=1))
        kept = jnp.where(keep, synthesize(upgoing_spec, inverse), 0.0).astype(BF16)
        minus = gather(analyze(kept, forward).astype(BF16))
        real = contract("wrs,wps->wpr", reflection[0], minus[:, 0]) + contract(
            "wrs,wps->wpr", reflection[1], minus[:, 1]
        )
        imag = contract("wrs,wps->wpr", reflection[0], minus[:, 1]) - contract(
            "wrs,wps->wpr", reflection[1], minus[:, 0]
        )
        downgoing_spec = jnp.stack([real, imag], axis=1).astype(BF16)
        if iteration + 1 < ITERS:
            kept = jnp.where(keep, synthesize(downgoing_spec, inverse), 0.0).astype(BF16)
            spectrum = (start.astype(F32) + analyze(kept, forward)).astype(BF16)
    upgoing = jnp.where(own_keep, synthesize(gather(upgoing_spec), own_inverse), 0.0).astype(BF16)
    change = jnp.where(own_keep, synthesize(gather(downgoing_spec), own_inverse), 0.0)
    return upgoing, (plus_start.astype(F32) + change).astype(BF16)


def solution(mesh):
    size = mesh.shape["blk"]

    def run(plus_start, reflection, onset_times):
        width = reflection.shape[2] // size
        fits = width == LANES and size % 4 == 0 and (plus_start.shape[1] // size) % 16 == 0
        return jax.shard_map(
            local if fits else local_any,
            mesh=mesh,
            in_specs=(P("groups", "blk", None), P(None, None, "blk", None), P("groups", None)),
            out_specs=(P("groups", "blk", None), P("groups", "blk", None)),
            check_vma=False,
        )(plus_start, reflection, onset_times)

    return run
```

```python
import functools
import math

import jax
import jax.numpy as jnp
import numpy as np
from jax import lax
from jax.experimental import pallas as pl
from jax.experimental.pallas import tpu as pltpu
from jax.sharding import PartitionSpec as P

NT = 512
NFW = 32
FREQ0 = 16
ITERS = 2
SURE = 128
LANES = 128
F32 = jnp.float32
BF16 = jnp.bfloat16


def basis_of(samples):
    freqs = FREQ0 + jnp.arange(NFW, dtype=jnp.int32)
    turns = freqs[:, None] * samples[None, :] % NT
    phase = turns.astype(F32) * (2.0 * math.pi / NT)
    return jnp.stack([jnp.cos(phase), -jnp.sin(phase)], axis=1)


def tables_of(samples):
    basis = basis_of(samples).reshape(2 * NFW, samples.shape[0])
    forward = (basis * (1.0 / math.sqrt(NT))).astype(BF16)
    inverse = (basis * math.sqrt(2.0 / NFW)).astype(BF16)
    return forward, inverse.T


def constant_tables():
    freqs = FREQ0 + np.arange(NFW, dtype=np.int32)
    turns = freqs[:, None] * np.arange(NT, dtype=np.int32)[None, :] % NT
    phase = turns.astype(np.float32) * np.float32(2.0 * math.pi / NT)
    basis = np.stack([np.cos(phase), -np.sin(phase)], axis=1).reshape(2 * NFW, NT)
    forward = (basis * np.float32(1.0 / math.sqrt(NT))).astype(BF16)
    inverse = (basis * np.float32(math.sqrt(2.0 / NFW))).astype(BF16)
    return forward, np.ascontiguousarray(inverse.T)


class Places:
    def __init__(self, axis, size):
        self.axis = axis
        self.size = size
        self.line = size // 4

    def core(self):
        return [(b, b ^ 1) for b in range(self.size)]

    def pair(self):
        return [(b, b ^ 2) for b in range(self.size)]

    def shift(self, step):
        return [(b, (b // 4 + step) % self.line * 4 + b % 4) for b in range(self.size)]

    def send(self, array, pairs):
        return lax.ppermute(array, self.axis, pairs)


def own_place(line):
    me = lax.axis_index("blk")
    return me, me // 4, (me // 2) % 2, me % 2


def chip_columns(line, ahead, flip, step):
    _, l, m, _ = own_place(line)
    other = lax.rem(l + step, line) if ahead else lax.rem(l - step + line, line)
    chip = other * 2 + (lax.rem(m + flip, 2))
    return pl.multiple_of(chip * (2 * LANES), 2 * LANES)


def relative(line):
    return [(flip, step) for flip in range(2) for step in range(line)]


def split_cores(core, block):
    low, high = block[:, :LANES], block[:, LANES:]
    first = core == 0
    return jnp.where(first, low, high), jnp.where(first, high, low)


def join_cores(core, own, other):
    first = core == 0
    return jnp.concatenate([jnp.where(first, own, other), jnp.where(first, other, own)], axis=1)


VMEM = pl.BlockSpec(memory_space=pltpu.VMEM)
ANY = pl.BlockSpec(memory_space=pl.ANY)
CHUNKS = 16
STRIPS = 4
SLOTS = 5


def limit(mebibytes):
    return pltpu.CompilerParams(vmem_limit_bytes=mebibytes << 20)


def strip_copies(source, target, sems, strips):
    rows = source.shape[0] // strips

    def copy(strip):
        part = pl.ds(strip * rows, rows)
        return pltpu.make_async_copy(source.at[part], target.at[part], sems.at[strip])

    return copy, rows


def analysis_kernel(line, forward_ref, plus_ref, keep0, keep1, send0, send1, held, sems):
    core = own_place(line)[3]
    keep, send = (keep0, keep1), (send0, send1)
    forward = forward_ref[own_place(line)[0]]
    copy, rows = strip_copies(plus_ref, held, sems, STRIPS)
    for strip in range(STRIPS):
        copy(strip).start()

    def body(strip, carry):
        copy(strip).wait()
        for row in range(rows):
            p = strip * rows + row
            for flip, step in relative(line):
                columns = pl.ds(chip_columns(line, True, flip, step), 2 * LANES)
                block = jnp.dot(forward, held[p, :, columns], preferred_element_type=F32)
                mine, theirs = split_cores(core, block.astype(BF16))
                keep[flip][step, p] = mine
                send[flip][step, p] = theirs
        return carry

    lax.fori_loop(0, STRIPS, body, 0)


def first_analysis(plus_start, forward, line):
    focal, samples, width = plus_start.shape
    out = jax.ShapeDtypeStruct((line, focal, 2 * NFW, LANES), BF16)
    return pl.pallas_call(
        functools.partial(analysis_kernel, line),
        in_specs=[VMEM, ANY],
        out_specs=[VMEM] * 4,
        out_shape=[out] * 4,
        scratch_shapes=[pltpu.VMEM(plus_start.shape, BF16), pltpu.SemaphoreType.DMA((STRIPS,))],
        compiler_params=limit(8),
        cost_estimate=pl.CostEstimate(
            flops=4 * NFW * focal * samples * width,
            bytes_accessed=2 * focal * samples * width + 4 * NFW * focal * width,
            transcendentals=0,
        ),
        name="first_analysis",
    )(forward, plus_start)


def fetch_panels(line, ahead, flip, panel_ref, held, sems):
    slots, _, _, rows = held.shape[:4]

    def copy(chunk, step):
        slot = lax.rem(chunk, slots)
        columns = pl.ds(chip_columns(line, ahead, flip, step), 2 * LANES)
        source = panel_ref.at[:, pl.ds(chunk * rows, rows), :, columns]
        return pltpu.make_async_copy(source, held.at[slot, step], sems.at[slot, step])

    def start(chunk):
        for step in range(line):
            copy(chunk, step).start()

    def wait(chunk):
        for step in range(line):
            copy(chunk, step).wait()

    for chunk in range(slots):
        start(chunk)
    return wait, start


def panel_scratch(line):
    rows = NFW // CHUNKS
    return [
        pltpu.VMEM((SLOTS, line, 2, rows, LANES, 2 * LANES), BF16),
        pltpu.SemaphoreType.DMA((SLOTS, line)),
    ]


def convolve_kernel(line, spec_ref, panel_ref, keep0, keep1, send0, send1, held, sems):
    core = own_place(line)[3]
    keep, send = (keep0, keep1), (send0, send1)
    focal = spec_ref.shape[2]
    rows = NFW // CHUNKS

    slots = held.shape[0]

    def copy(chunk):
        slot = lax.rem(chunk, slots)
        part = pl.ds(chunk * rows, rows)
        return pltpu.make_async_copy(panel_ref.at[:, part], held.at[slot], sems.at[slot])

    for chunk in range(slots):
        copy(chunk).start()

    def body(chunk, carry):
        copy(chunk).wait()
        slot = lax.rem(chunk, slots)
        for row in range(rows):
            w = chunk * rows + row
            real, imag = spec_ref[w, 0], spec_ref[w, 1]
            left = jnp.concatenate(
                [jnp.concatenate([real, -imag], axis=1), jnp.concatenate([imag, real], axis=1)], axis=0
            )
            for flip, step in relative(line):
                columns = pl.ds(chip_columns(line, True, flip, step), 2 * LANES)
                panel = held[slot, :, row, :, columns].reshape(2 * LANES, 2 * LANES)
                block = jnp.dot(left, panel, preferred_element_type=F32)
                mine, theirs = split_cores(core, block.astype(BF16))
                keep[flip][step, w] = mine.reshape(2, focal, LANES)
                send[flip][step, w] = theirs.reshape(2, focal, LANES)

        @pl.when(chunk + slots < CHUNKS)
        def _():
            copy(chunk + slots).start()

        return carry

    lax.fori_loop(0, CHUNKS, body, 0)


def panel_cost(focal, sources):
    return pl.CostEstimate(
        flops=8 * NFW * focal * LANES * sources,
        bytes_accessed=4 * NFW * sources * (LANES + focal),
        transcendentals=0,
    )


def convolve(spectrum, reflection, line):
    focal = spectrum.shape[2]
    out = jax.ShapeDtypeStruct((line, NFW, 2, focal, LANES), BF16)
    return pl.pallas_call(
        functools.partial(convolve_kernel, line),
        in_specs=[VMEM, ANY],
        out_specs=[VMEM] * 4,
        out_shape=[out] * 4,
        scratch_shapes=[
            pltpu.VMEM((SLOTS, 2, NFW // CHUNKS, LANES, reflection.shape[3]), BF16),
            pltpu.SemaphoreType.DMA((SLOTS,)),
        ],
        compiler_params=limit(14),
        cost_estimate=panel_cost(focal, reflection.shape[3]),
        name="convolve",
    )(spectrum, reflection)


def correlate_kernel(line, flip, has_base, final, *refs):
    core = own_place(line)[3]
    own, other, panel_ref = refs[:line], refs[line : 2 * line], refs[2 * line]
    base_ref = refs[2 * line + 1] if has_base else None
    out_ref, held, sems, *spare = refs[2 * line + 1 + has_base :]
    focal = own[0].shape[2]
    rows = held.shape[3]
    slots = held.shape[0]
    wait, start = fetch_panels(line, False, flip, panel_ref, held, sems)

    def body(chunk, carry):
        wait(chunk)
        slot = lax.rem(chunk, slots)
        for row in range(rows):
            w = chunk * rows + row
            panels, specs = [], []
            for step in range(line):
                panels.append(held[slot, step, :, row].reshape(2 * LANES, 2 * LANES))
                mine, theirs = own[step][w], other[step][w]
                specs.append(
                    join_cores(core, mine.reshape(2 * focal, LANES), theirs.reshape(2 * focal, LANES))
                )
            total = lax.dot_general(
                jnp.concatenate(specs, axis=1),
                jnp.concatenate(panels, axis=1),
                (((1,), (1,)), ((), ())),
                preferred_element_type=F32,
            )
            real = total[:focal, :LANES] + total[focal:, LANES:]
            imag = total[focal:, :LANES] - total[:focal, LANES:]
            if has_base:
                real += base_ref[w, 0]
                imag += base_ref[w, 1]
            if final:
                spare[0][pl.ds(2 * w * focal, focal), :] = real
                spare[0][pl.ds((2 * w + 1) * focal, focal), :] = imag
            else:
                out_ref[w, 0] = real
                out_ref[w, 1] = imag

        @pl.when(chunk + slots < CHUNKS)
        def _():
            start(chunk + slots)

        return carry

    lax.fori_loop(0, CHUNKS, body, 0)
    if final:
        for p in range(focal):
            out_ref[p] = spare[0][pl.ds(p, 2 * NFW, stride=focal), :].astype(BF16)


def correlate(own, other, reflection, line, flip, base=None, final=False):
    focal = own[0].shape[2]
    more = [] if base is None else [base]
    shape = jax.ShapeDtypeStruct((NFW, 2, focal, LANES), F32)
    if final:
        shape = jax.ShapeDtypeStruct((focal, 2 * NFW, LANES), BF16)
    spare = [pltpu.VMEM((2 * NFW * focal, LANES), F32)] if final else []
    return pl.pallas_call(
        functools.partial(correlate_kernel, line, flip, bool(more), final),
        in_specs=[VMEM] * (2 * line) + [ANY] + [VMEM] * len(more),
        out_specs=VMEM,
        out_shape=shape,
        scratch_shapes=panel_scratch(line) + spare,
        compiler_params=limit(9),
        cost_estimate=panel_cost(focal, reflection.shape[3] // 2),
        name=f"correlate{flip}",
    )(*own, *other, reflection, *more)


def windowed_spectrum(pair, onset, forward, inverse):
    time = SURE + lax.broadcasted_iota(jnp.int32, (NT - SURE, 2 * LANES), 0)
    spectra = jnp.concatenate(pair, axis=1)
    values = jnp.dot(inverse, spectra, preferred_element_type=F32)
    kept = jnp.where(time < jnp.concatenate(onset, axis=1), values, 0.0).astype(BF16)
    return jnp.dot(forward, jnp.concatenate([kept, spectra], axis=0), preferred_element_type=F32)


def window_kernel(parts, has_base, want_spec, *refs):
    refs = list(refs)
    forward_ref, inverse_ref, onset_ref = refs[:3]
    part_refs = refs[3 : 3 + parts]
    rest = refs[3 + parts :]
    base_ref = rest.pop(0) if has_base else None
    out_ref = rest.pop(0)
    held, result = rest
    focal = part_refs[0].shape[2]
    k = 2 * NFW
    total = part_refs[0][...].astype(F32)
    for ref in part_refs[1:]:
        total += ref[...].astype(F32)
    held[...] = total.reshape(k * focal, LANES)
    me = lax.axis_index("blk")
    columns = pl.ds(pl.multiple_of(me * LANES, LANES), LANES)
    if want_spec:
        for p in range(focal):
            out_ref[p] = held[pl.ds(p, k, stride=focal), :].astype(BF16)
        return
    for p in range(0, focal, 2):
        pair = [held[pl.ds(p + q, k, stride=focal), :].astype(BF16) for q in range(2)]
        onset = [onset_ref[p + q : p + q + 1, columns] for q in range(2)]
        spectrum = windowed_spectrum(pair, onset, forward_ref[...], inverse_ref[...])
        for q in range(2):
            result[pl.ds(p + q, k, stride=focal), :] = spectrum[:, q * LANES : (q + 1) * LANES]
    final = result[...].reshape(NFW, 2, focal, LANES)
    if base_ref is not None:
        final += base_ref[...].astype(F32)
    out_ref[...] = final.astype(BF16)


def window(parts, forward, inverse, onset_times, base=None, want_spec=False):
    focal = parts[0].shape[2]
    k = 2 * NFW
    operands = [forward, inverse, onset_times, *parts] + ([] if base is None else [base])
    out = jax.ShapeDtypeStruct((NFW, 2, focal, LANES), BF16)
    if want_spec:
        out = jax.ShapeDtypeStruct((focal, k, LANES), BF16)
    return pl.pallas_call(
        functools.partial(window_kernel, len(parts), base is not None, want_spec),
        in_specs=[VMEM] * len(operands),
        out_specs=VMEM,
        out_shape=out,
        scratch_shapes=[pltpu.VMEM((k * focal, LANES), F32)] * 2,
        compiler_params=limit(8),
        cost_estimate=pl.CostEstimate(
            flops=4 * k * NT * focal * LANES, bytes_accessed=2 * k * focal * LANES * 6, transcendentals=0
        ),
        name="window",
    )(*operands)


def window_at_kernel(line, flip, step, begun, *refs):
    forward_ref, inverse_ref, onset_ref, chip_inverse_ref, spec_ref = refs[:5]
    out_ref, keep_ref, send_ref, result, made, sems = refs[5 + 2 * begun :]
    core = own_place(line)[3]
    focal, k, _ = spec_ref.shape
    start = chip_columns(line, False, flip, step) + core * LANES
    columns = pl.ds(pl.multiple_of(start, LANES), LANES)
    samples = made.shape[2]
    chip = lax.axis_index("blk") // 2
    chip_inverse = chip_inverse_ref[chip]
    first = chip * (2 * samples)
    time = first + lax.broadcasted_iota(jnp.int32, (2 * samples, 2 * LANES), 0)

    def pair_of(p):
        onset = [onset_ref[p + q : p + q + 1, columns] for q in range(2)]
        return [spec_ref[p + q] for q in range(2)], onset

    for p in range(0, focal, 2):
        pair, onset = pair_of(p)
        values = jnp.dot(chip_inverse, jnp.concatenate(pair, axis=1), preferred_element_type=F32)
        values = jnp.where(time < jnp.concatenate(onset, axis=1), values, 0.0).astype(BF16)
        low, high = values[:samples], values[samples:]
        mine, theirs = jnp.where(core == 0, low, high), jnp.where(core == 0, high, low)
        for q in range(2):
            part = slice(q * LANES, (q + 1) * LANES)
            made[0, p + q] = mine[:, part]
            made[1, p + q] = theirs[:, part]
    place = pl.ds((flip * line + step) * LANES, LANES)
    copies = [
        pltpu.make_async_copy(made.at[side], target.at[:, :, place], sems.at[side])
        for side, target in enumerate((keep_ref, send_ref))
    ]
    for copy in copies:
        copy.start()
    for p in range(0, focal, 2):
        pair, onset = pair_of(p)
        spectrum = windowed_spectrum(pair, onset, forward_ref[...], inverse_ref[...])
        for q in range(2):
            result[pl.ds(p + q, k, stride=focal), :] = spectrum[:, q * LANES : (q + 1) * LANES]
    out_ref[...] = result[...].reshape(NFW, 2, focal, LANES).astype(BF16)
    for copy in copies:
        copy.wait()


def window_at(spec, forward, inverse, onset_times, chip_inverse, line, flip, step, fields):
    focal, k, _ = spec.shape
    samples = chip_inverse.shape[1] // 2
    field_shape = jax.ShapeDtypeStruct((focal, samples, 2 * line * LANES), BF16)
    begun = bool(fields)
    return pl.pallas_call(
        functools.partial(window_at_kernel, line, flip, step, begun),
        in_specs=[VMEM] * 5 + [ANY] * len(fields),
        out_specs=[VMEM, ANY, ANY],
        out_shape=[jax.ShapeDtypeStruct((NFW, 2, focal, LANES), BF16), field_shape, field_shape],
        input_output_aliases={5: 1, 6: 2} if begun else {},
        scratch_shapes=[
            pltpu.VMEM((k * focal, LANES), F32),
            pltpu.VMEM((2, focal, samples, LANES), BF16),
            pltpu.SemaphoreType.DMA((2,)),
        ],
        compiler_params=limit(8),
        cost_estimate=pl.CostEstimate(
            flops=4 * k * NT * focal * LANES, bytes_accessed=2 * k * focal * LANES * 6, transcendentals=0
        ),
        name="window_at",
    )(forward, inverse, onset_times, chip_inverse, spec, *fields)


def merge_kernel(line, mine, theirs, out_ref, made, sems):
    core = own_place(line)[3]
    copy, rows = strip_copies(made, out_ref, sems, STRIPS)

    def body(strip, carry):
        for row in range(rows):
            p = strip * rows + row
            for at, (flip, step) in enumerate(relative(line)):
                columns = pl.ds(chip_columns(line, False, flip, step), 2 * LANES)
                part = pl.ds(at * LANES, LANES)
                made[p, :, columns] = join_cores(core, mine[p, :, part], theirs[p, :, part])
        copy(strip).start()
        return carry

    lax.fori_loop(0, STRIPS, body, 0)
    for strip in range(STRIPS):
        copy(strip).wait()


def merge(mine, theirs, line):
    focal, samples, width = mine.shape
    shape = (focal, samples, 2 * width)
    return pl.pallas_call(
        functools.partial(merge_kernel, line),
        in_specs=[VMEM] * 2,
        out_specs=ANY,
        out_shape=jax.ShapeDtypeStruct(shape, BF16),
        scratch_shapes=[pltpu.VMEM(shape, BF16), pltpu.SemaphoreType.DMA((STRIPS,))],
        compiler_params=limit(6),
        cost_estimate=pl.CostEstimate(flops=0, bytes_accessed=8 * mine.size, transcendentals=0),
        name="merge",
    )(mine, theirs)


def field_kernel(line, has_plus, inverse_ref, onset_ref, *refs):
    core = own_place(line)[3]
    places = relative(line)
    own, other = refs[: len(places)], refs[len(places) : 2 * len(places)]
    rest = list(refs[2 * len(places) :])
    plus_ref = rest.pop(0) if has_plus else None
    out_ref, made, out_sems, *spare = rest
    samples = out_ref.shape[1]
    inverse = inverse_ref[own_place(line)[0]]
    out_copy, rows = strip_copies(made, out_ref, out_sems, STRIPS)
    if has_plus:
        plus, plus_sems = spare
        plus_copy, _ = strip_copies(plus_ref, plus, plus_sems, STRIPS)
        for strip in range(STRIPS):
            plus_copy(strip).start()
    time = lax.axis_index("blk") * samples + lax.broadcasted_iota(jnp.int32, (samples, 2 * LANES), 0)

    def body(strip, carry):
        if has_plus:
            plus_copy(strip).wait()
        for row in range(rows):
            p = strip * rows + row
            for at, (flip, step) in enumerate(places):
                columns = pl.ds(chip_columns(line, False, flip, step), 2 * LANES)
                spec = join_cores(core, own[at][p], other[at][p])
                values = jnp.dot(inverse, spec, preferred_element_type=F32)
                values = jnp.where(time < onset_ref[pl.ds(p, 1), columns], values, 0.0)
                if has_plus:
                    values += plus[p, :, columns].astype(F32)
                made[p, :, columns] = values.astype(BF16)
        out_copy(strip).start()
        return carry

    lax.fori_loop(0, STRIPS, body, 0)
    for strip in range(STRIPS):
        out_copy(strip).wait()


def field(own, other, inverse, onset_times, line, plus_start=None):
    own, other = sum(own, []), sum(other, [])
    focal, k, _ = own[0].shape
    samples = inverse.shape[1]
    shape = (focal, samples, onset_times.shape[1])
    plus = [] if plus_start is None else [plus_start]
    moved = [pltpu.VMEM(shape, BF16), pltpu.SemaphoreType.DMA((STRIPS,))]
    return pl.pallas_call(
        functools.partial(field_kernel, line, bool(plus)),
        in_specs=[VMEM] * (2 + len(own) + len(other)) + [ANY] * len(plus),
        out_specs=ANY,
        out_shape=jax.ShapeDtypeStruct(shape, BF16),
        scratch_shapes=moved * (1 + len(plus)),
        compiler_params=limit(12),
        cost_estimate=pl.CostEstimate(
            flops=2 * k * math.prod(shape),
            bytes_accessed=4 * math.prod(shape) + 2 * k * focal * shape[2],
            transcendentals=0,
        ),
        name="field",
    )(inverse, onset_times, *own, *other, *plus)


def add(*parts):
    total = parts[0].astype(F32)
    for part in parts[1:]:
        total += part.astype(F32)
    return total


def after(value, *others):
    return lax.optimization_barrier((value, *others))[0] if others else value


def reduce_scatter(places, keep0, keep1, send0, send1):
    size = places.line
    got1 = places.send(send1, places.core())
    got0 = places.send(send0, places.core())
    far = [add(keep, got).astype(BF16) for keep, got in zip(keep1, got1)]
    across = {step: places.send(far[step], places.pair()) for step in range(2, size)}
    beside = [places.send(far[1], places.shift(1))] if size > 1 else []
    parts = [keep0[0], got0[0]]

    def pass_on(steps, shift, *first):
        carried, sent = [], []
        for step in steps:
            crossed = [after(across[step], *first)] if step in across else []
            carried = [places.send(add(keep0[step], got0[step], *crossed, *carried).astype(BF16), places.shift(shift))]
            sent += carried
        return sent

    ahead = pass_on(range(size // 2, 0, -1), 1)
    behind = pass_on(range(size // 2 + 1, size), size - 1, *ahead[:1])
    parts += ahead[-1:] + behind[-1:]
    across[0] = places.send(add(keep1[0], got1[0], *beside).astype(BF16), places.pair())
    return parts + [across[0]]


def gather_chips(places, block, work=None):
    size = places.line
    near = [1, size - 1] if size > 2 else [1] if size > 1 else []
    far = list(range(2, size - 1))
    made = {}

    def run(flip, steps, pieces, *others):
        if work is None:
            return []
        for step in steps:
            made[flip, step] = work(after(pieces[step], *others), flip, step)
        return [made[flip, step] for step in steps]

    line = {0: block}
    for step in near:
        line[step] = places.send(block, places.shift(step))
    across = {0: places.send(block, places.pair())}
    own = run(0, [0], line)
    for step in range(2, size // 2 + 1):
        line[step] = places.send(after(line[step - 1], across[0], *own), places.shift(1))
    for step in range(size - 2, size // 2, -1):
        line[step] = places.send(after(line[step + 1], *own), places.shift(size - 1))
    for step in near:
        if step == 1:
            across[step] = places.send(after(across[0], line[size - 1]), places.shift(1))
        else:
            across[step] = places.send(line[step], places.pair())
    middle = run(1, [0], across) + run(0, near, line)
    for step in far:
        across[step] = places.send(after(line[step], *middle), places.pair())
    late = run(0, far, line) + run(1, near, across)
    run(1, far, across, *late)
    pieces = [[side[step] for step in range(size)] for side in (line, across)]
    results = [[made[flip, step] for step in range(size)] for flip in range(2)] if work else None
    return pieces, results


def swap_cores(places, pieces):
    return [places.send(piece, places.core()) for piece in pieces]


def local(plus_start, reflection, onset_times):
    size = lax.axis_size("blk")
    places = Places("blk", size)
    line = places.line
    focal, samples, _ = plus_start.shape
    forward, inverse = constant_tables()
    own_forward = np.ascontiguousarray(forward.reshape(2 * NFW, size, samples).transpose(1, 0, 2))
    own_inverse = inverse.reshape(size, samples, 2 * NFW)
    chip_inverse = inverse.reshape(size // 2, 2 * samples, 2 * NFW)
    sure = forward[:, :SURE].astype(np.float32) @ inverse[:SURE].astype(np.float32)
    forward = jnp.asarray(np.concatenate([forward[:, SURE:], sure.astype(BF16)], axis=1))
    inverse = jnp.asarray(inverse[SURE:])
    own_forward, own_inverse, chip_inverse = map(jnp.asarray, (own_forward, own_inverse, chip_inverse))

    fields = []

    def window_piece(piece, flip, step):
        spectrum, *fields[:] = window_at(
            piece, forward, inverse, onset_times, chip_inverse, line, flip, step, tuple(fields)
        )
        return spectrum

    parts = reduce_scatter(places, *first_analysis(plus_start, own_forward, line))
    start = add(*parts).astype(BF16)
    start = jnp.transpose(start, (1, 0, 2)).reshape(NFW, 2, focal, LANES)
    spectrum_plus = start
    for iteration in range(ITERS):
        last = iteration + 1 == ITERS
        parts = reduce_scatter(places, *convolve(spectrum_plus, reflection, line))
        windowed = window(parts, forward, inverse, onset_times, want_spec=last)
        if last:
            _, own = gather_chips(places, windowed, window_piece)
        else:
            own, _ = gather_chips(places, windowed)
        half = correlate(own[0], swap_cores(places, own[0]), reflection, line, 0)
        across = [own[1][step] if step in (0, line - 1) else after(own[1][step], half) for step in range(line)]
        downgoing_spec = correlate(own[1], swap_cores(places, across), reflection, line, 1, half, last)
        if not last:
            spectrum_plus = window([downgoing_spec], forward, inverse, onset_times, base=start)
    mine, theirs = fields
    theirs = places.send(after(theirs, downgoing_spec), places.core())
    own, _ = gather_chips(places, downgoing_spec)
    upgoing = merge(mine, theirs, line)
    other = [swap_cores(places, own[0])]
    across = [own[1][step] if step in (0, 1, line - 1) else after(own[1][step], upgoing) for step in range(line)]
    other.append(swap_cores(places, across))
    downgoing = field(own, other, own_inverse, onset_times, line, plus_start)
    return upgoing, downgoing


def analyze(values, forward):
    total = jnp.einsum("kt,ptx->kpx", forward, values, preferred_element_type=F32)
    return total.reshape(NFW, 2, values.shape[0], values.shape[2])


def synthesize(spectrum, inverse):
    flat = spectrum.reshape(2 * NFW, spectrum.shape[2], spectrum.shape[3])
    return jnp.einsum("tk,kpx->ptx", inverse, flat, preferred_element_type=F32)


def contract(form, left, right):
    return jnp.einsum(form, left, right, preferred_element_type=F32)


def local_any(plus_start, reflection, onset_times):
    samples = plus_start.shape[1]
    width = reflection.shape[2]
    me = lax.axis_index("blk")
    forward, inverse = tables_of(jnp.arange(NT, dtype=jnp.int32))
    own_forward, own_inverse = tables_of(me * samples + jnp.arange(samples, dtype=jnp.int32))
    onset = lax.dynamic_slice_in_dim(onset_times, me * width, width, 1)
    keep = jnp.arange(NT, dtype=jnp.int32)[None, :, None] < onset[:, None, :]
    time = me * samples + jnp.arange(samples, dtype=jnp.int32)
    own_keep = time[None, :, None] < onset_times[:, None, :]

    def scatter(partial):
        return lax.psum_scatter(partial.astype(BF16), "blk", scatter_dimension=3, tiled=True).astype(BF16)

    def gather(block):
        return lax.all_gather(block, "blk", axis=3, tiled=True)

    start = scatter(analyze(plus_start, own_forward))
    spectrum = start
    for iteration in range(ITERS):
        real = contract("wrs,wpr->wps", reflection[0], spectrum[:, 0]) - contract(
            "wrs,wpr->wps", reflection[1], spectrum[:, 1]
        )
        imag = contract("wrs,wpr->wps", reflection[0], spectrum[:, 1]) + contract(
            "wrs,wpr->wps", reflection[1], spectrum[:, 0]
        )
        upgoing_spec = scatter(jnp.stack([real, imag], axis=1))
        kept = jnp.where(keep, synthesize(upgoing_spec, inverse), 0.0).astype(BF16)
        minus = gather(analyze(kept, forward).astype(BF16))
        real = contract("wrs,wps->wpr", reflection[0], minus[:, 0]) + contract(
            "wrs,wps->wpr", reflection[1], minus[:, 1]
        )
        imag = contract("wrs,wps->wpr", reflection[0], minus[:, 1]) - contract(
            "wrs,wps->wpr", reflection[1], minus[:, 0]
        )
        downgoing_spec = jnp.stack([real, imag], axis=1).astype(BF16)
        if iteration + 1 < ITERS:
            kept = jnp.where(keep, synthesize(downgoing_spec, inverse), 0.0).astype(BF16)
            spectrum = (start.astype(F32) + analyze(kept, forward)).astype(BF16)
    upgoing = jnp.where(own_keep, synthesize(gather(upgoing_spec), own_inverse), 0.0).astype(BF16)
    change = jnp.where(own_keep, synthesize(gather(downgoing_spec), own_inverse), 0.0)
    return upgoing, (plus_start.astype(F32) + change).astype(BF16)


def solution(mesh):
    size = mesh.shape["blk"]

    def run(plus_start, reflection, onset_times):
        width = reflection.shape[2] // size
        fits = width == LANES and size % 4 == 0 and (plus_start.shape[1] // size) % 16 == 0
        return jax.shard_map(
            local if fits else local_any,
            mesh=mesh,
            in_specs=(P("groups", "blk", None), P(None, None, "blk", None), P("groups", None)),
            out_specs=(P("groups", "blk", None), P("groups", "blk", None)),
            check_vma=False,
        )(plus_start, reflection, onset_times)

    return run
```

```python
import functools
import math

import jax
import jax.numpy as jnp
import numpy as np
from jax import lax
from jax.experimental import pallas as pl
from jax.experimental.pallas import tpu as pltpu
from jax.sharding import PartitionSpec as P

NT = 512
NFW = 32
FREQ0 = 16
ITERS = 2
SURE = 128
LANES = 128
F32 = jnp.float32
BF16 = jnp.bfloat16


def basis_of(samples):
    freqs = FREQ0 + jnp.arange(NFW, dtype=jnp.int32)
    turns = freqs[:, None] * samples[None, :] % NT
    phase = turns.astype(F32) * (2.0 * math.pi / NT)
    return jnp.stack([jnp.cos(phase), -jnp.sin(phase)], axis=1)


def tables_of(samples):
    basis = basis_of(samples).reshape(2 * NFW, samples.shape[0])
    forward = (basis * (1.0 / math.sqrt(NT))).astype(BF16)
    inverse = (basis * math.sqrt(2.0 / NFW)).astype(BF16)
    return forward, inverse.T


def constant_tables():
    freqs = FREQ0 + np.arange(NFW, dtype=np.int32)
    turns = freqs[:, None] * np.arange(NT, dtype=np.int32)[None, :] % NT
    phase = turns.astype(np.float32) * np.float32(2.0 * math.pi / NT)
    basis = np.stack([np.cos(phase), -np.sin(phase)], axis=1).reshape(2 * NFW, NT)
    forward = (basis * np.float32(1.0 / math.sqrt(NT))).astype(BF16)
    inverse = (basis * np.float32(math.sqrt(2.0 / NFW))).astype(BF16)
    return forward, np.ascontiguousarray(inverse.T)


class Places:
    def __init__(self, axis, size):
        self.axis = axis
        self.size = size
        self.line = size // 4

    def core(self):
        return [(b, b ^ 1) for b in range(self.size)]

    def pair(self):
        return [(b, b ^ 2) for b in range(self.size)]

    def shift(self, step):
        return [(b, (b // 4 + step) % self.line * 4 + b % 4) for b in range(self.size)]

    def send(self, array, pairs):
        return lax.ppermute(array, self.axis, pairs)


def own_place(line):
    me = lax.axis_index("blk")
    return me, me // 4, (me // 2) % 2, me % 2


def chip_columns(line, ahead, flip, step):
    _, l, m, _ = own_place(line)
    other = lax.rem(l + step, line) if ahead else lax.rem(l - step + line, line)
    chip = other * 2 + (lax.rem(m + flip, 2))
    return pl.multiple_of(chip * (2 * LANES), 2 * LANES)


def relative(line):
    return [(flip, step) for flip in range(2) for step in range(line)]


def split_cores(core, block):
    low, high = block[:, :LANES], block[:, LANES:]
    first = core == 0
    return jnp.where(first, low, high), jnp.where(first, high, low)


def join_cores(core, own, other):
    first = core == 0
    return jnp.concatenate([jnp.where(first, own, other), jnp.where(first, other, own)], axis=1)


VMEM = pl.BlockSpec(memory_space=pltpu.VMEM)
FAR = pl.BlockSpec(memory_space=pltpu.HBM)
CHUNKS = 8
STRIPS = 4
SLOTS = 4


def limit(mebibytes):
    return pltpu.CompilerParams(vmem_limit_bytes=mebibytes << 20)


def strip_copies(source, target, sems, strips):
    rows = source.shape[0] // strips

    def copy(strip):
        part = pl.ds(strip * rows, rows)
        return pltpu.make_async_copy(source.at[part], target.at[part], sems.at[strip])

    return copy, rows


def analysis_kernel(line, forward_ref, plus_ref, keep0, keep1, send0, send1, held, sems):
    core = own_place(line)[3]
    keep, send = (keep0, keep1), (send0, send1)
    forward = forward_ref[own_place(line)[0]]
    copy, rows = strip_copies(plus_ref, held, sems, STRIPS)
    for strip in range(STRIPS):
        copy(strip).start()

    def body(strip, carry):
        copy(strip).wait()
        for row in range(rows):
            p = strip * rows + row
            for flip, step in relative(line):
                columns = pl.ds(chip_columns(line, True, flip, step), 2 * LANES)
                block = jnp.dot(forward, held[p, :, columns], preferred_element_type=F32)
                mine, theirs = split_cores(core, block.astype(BF16))
                keep[flip][step, p] = mine
                send[flip][step, p] = theirs
        return carry

    lax.fori_loop(0, STRIPS, body, 0)


def first_analysis(plus_start, forward, line):
    focal, samples, width = plus_start.shape
    out = jax.ShapeDtypeStruct((line, focal, 2 * NFW, LANES), BF16)
    return pl.pallas_call(
        functools.partial(analysis_kernel, line),
        in_specs=[VMEM, FAR],
        out_specs=[VMEM] * 4,
        out_shape=[out] * 4,
        scratch_shapes=[pltpu.VMEM(plus_start.shape, BF16), pltpu.SemaphoreType.DMA((STRIPS,))],
        compiler_params=limit(8),
        cost_estimate=pl.CostEstimate(
            flops=4 * NFW * focal * samples * width,
            bytes_accessed=2 * focal * samples * width + 4 * NFW * focal * width,
            transcendentals=0,
        ),
        name="first_analysis",
    )(forward, plus_start)


def fetch_panels(line, ahead, flip, panel_ref, held, sems):
    slots, _, _, rows = held.shape[:4]

    def copy(chunk, step):
        slot = lax.rem(chunk, slots)
        columns = pl.ds(chip_columns(line, ahead, flip, step), 2 * LANES)
        source = panel_ref.at[:, pl.ds(chunk * rows, rows), :, columns]
        return pltpu.make_async_copy(source, held.at[slot, step], sems.at[slot, step])

    def start(chunk):
        for step in range(line):
            copy(chunk, step).start()

    def wait(chunk):
        for step in range(line):
            copy(chunk, step).wait()

    for chunk in range(slots):
        start(chunk)
    return wait, start


def panel_scratch(line):
    rows = NFW // CHUNKS
    return [
        pltpu.VMEM((SLOTS, line, 2, rows, LANES, 2 * LANES), BF16),
        pltpu.SemaphoreType.DMA((SLOTS, line)),
    ]


def convolve_kernel(line, spec_ref, panel_ref, keep0, keep1, send0, send1, held, sems):
    core = own_place(line)[3]
    keep, send = (keep0, keep1), (send0, send1)
    focal = spec_ref.shape[2]
    rows = NFW // CHUNKS

    slots = held.shape[0]

    def copy(chunk):
        slot = lax.rem(chunk, slots)
        part = pl.ds(chunk * rows, rows)
        return pltpu.make_async_copy(panel_ref.at[:, part], held.at[slot], sems.at[slot])

    for chunk in range(slots):
        copy(chunk).start()

    def body(chunk, carry):
        copy(chunk).wait()
        slot = lax.rem(chunk, slots)
        for row in range(rows):
            w = chunk * rows + row
            real, imag = spec_ref[w, 0], spec_ref[w, 1]
            left = jnp.concatenate(
                [jnp.concatenate([real, -imag], axis=1), jnp.concatenate([imag, real], axis=1)], axis=0
            )
            for flip, step in relative(line):
                columns = pl.ds(chip_columns(line, True, flip, step), 2 * LANES)
                panel = held[slot, :, row, :, columns].reshape(2 * LANES, 2 * LANES)
                block = jnp.dot(left, panel, preferred_element_type=F32)
                mine, theirs = split_cores(core, block.astype(BF16))
                keep[flip][step, w] = mine.reshape(2, focal, LANES)
                send[flip][step, w] = theirs.reshape(2, focal, LANES)

        @pl.when(chunk + slots < CHUNKS)
        def _():
            copy(chunk + slots).start()

        return carry

    lax.fori_loop(0, CHUNKS, body, 0)


def panel_cost(focal, sources):
    return pl.CostEstimate(
        flops=8 * NFW * focal * LANES * sources,
        bytes_accessed=4 * NFW * sources * (LANES + focal),
        transcendentals=0,
    )


def convolve(spectrum, reflection, line):
    focal = spectrum.shape[2]
    out = jax.ShapeDtypeStruct((line, NFW, 2, focal, LANES), BF16)
    return pl.pallas_call(
        functools.partial(convolve_kernel, line),
        in_specs=[VMEM, FAR],
        out_specs=[VMEM] * 4,
        out_shape=[out] * 4,
        scratch_shapes=[
            pltpu.VMEM((SLOTS, 2, NFW // CHUNKS, LANES, reflection.shape[3]), BF16),
            pltpu.SemaphoreType.DMA((SLOTS,)),
        ],
        compiler_params=limit(20),
        cost_estimate=panel_cost(focal, reflection.shape[3]),
        name="convolve",
    )(spectrum, reflection)


def correlate_kernel(line, flip, has_base, final, *refs):
    core = own_place(line)[3]
    own, other, panel_ref = refs[:line], refs[line : 2 * line], refs[2 * line]
    base_ref = refs[2 * line + 1] if has_base else None
    out_ref, held, sems, *spare = refs[2 * line + 1 + has_base :]
    focal = own[0].shape[2]
    rows = held.shape[3]
    slots = held.shape[0]
    wait, start = fetch_panels(line, False, flip, panel_ref, held, sems)

    def body(chunk, carry):
        wait(chunk)
        slot = lax.rem(chunk, slots)
        for row in range(rows):
            w = chunk * rows + row
            panels, specs = [], []
            for step in range(line):
                panels.append(held[slot, step, :, row].reshape(2 * LANES, 2 * LANES))
                mine, theirs = own[step][w], other[step][w]
                specs.append(
                    join_cores(core, mine.reshape(2 * focal, LANES), theirs.reshape(2 * focal, LANES))
                )
            total = lax.dot_general(
                jnp.concatenate(specs, axis=1),
                jnp.concatenate(panels, axis=1),
                (((1,), (1,)), ((), ())),
                preferred_element_type=F32,
            )
            real = total[:focal, :LANES] + total[focal:, LANES:]
            imag = total[focal:, :LANES] - total[:focal, LANES:]
            if has_base:
                real += base_ref[w, 0]
                imag += base_ref[w, 1]
            if final:
                spare[0][pl.ds(2 * w * focal, focal), :] = real
                spare[0][pl.ds((2 * w + 1) * focal, focal), :] = imag
            else:
                out_ref[w, 0] = real
                out_ref[w, 1] = imag

        @pl.when(chunk + slots < CHUNKS)
        def _():
            start(chunk + slots)

        return carry

    lax.fori_loop(0, CHUNKS, body, 0)
    if final:
        for p in range(focal):
            out_ref[p] = spare[0][pl.ds(p, 2 * NFW, stride=focal), :].astype(BF16)


def correlate(own, other, reflection, line, flip, base=None, final=False):
    focal = own[0].shape[2]
    more = [] if base is None else [base]
    shape = jax.ShapeDtypeStruct((NFW, 2, focal, LANES), F32)
    if final:
        shape = jax.ShapeDtypeStruct((focal, 2 * NFW, LANES), BF16)
    spare = [pltpu.VMEM((2 * NFW * focal, LANES), F32)] if final else []
    return pl.pallas_call(
        functools.partial(correlate_kernel, line, flip, bool(more), final),
        in_specs=[VMEM] * (2 * line) + [FAR] + [VMEM] * len(more),
        out_specs=VMEM,
        out_shape=shape,
        scratch_shapes=panel_scratch(line) + spare,
        compiler_params=limit(24),
        cost_estimate=panel_cost(focal, reflection.shape[3] // 2),
        name=f"correlate{flip}",
    )(*own, *other, reflection, *more)


def windowed_spectrum(pair, onset, forward, inverse):
    time = SURE + lax.broadcasted_iota(jnp.int32, (NT - SURE, 2 * LANES), 0)
    spectra = jnp.concatenate(pair, axis=1)
    values = jnp.dot(inverse, spectra, preferred_element_type=F32)
    kept = jnp.where(time < jnp.concatenate(onset, axis=1), values, 0.0).astype(BF16)
    return jnp.dot(forward, jnp.concatenate([kept, spectra], axis=0), preferred_element_type=F32)


def window_kernel(parts, has_base, want_spec, *refs):
    refs = list(refs)
    forward_ref, inverse_ref, onset_ref = refs[:3]
    part_refs = refs[3 : 3 + parts]
    rest = refs[3 + parts :]
    base_ref = rest.pop(0) if has_base else None
    out_ref = rest.pop(0)
    held, result = rest
    focal = part_refs[0].shape[2]
    k = 2 * NFW
    total = part_refs[0][...].astype(F32)
    for ref in part_refs[1:]:
        total += ref[...].astype(F32)
    held[...] = total.reshape(k * focal, LANES)
    me = lax.axis_index("blk")
    columns = pl.ds(pl.multiple_of(me * LANES, LANES), LANES)
    if want_spec:
        for p in range(focal):
            out_ref[p] = held[pl.ds(p, k, stride=focal), :].astype(BF16)
        return
    for p in range(0, focal, 2):
        pair = [held[pl.ds(p + q, k, stride=focal), :].astype(BF16) for q in range(2)]
        onset = [onset_ref[p + q : p + q + 1, columns] for q in range(2)]
        spectrum = windowed_spectrum(pair, onset, forward_ref[...], inverse_ref[...])
        for q in range(2):
            result[pl.ds(p + q, k, stride=focal), :] = spectrum[:, q * LANES : (q + 1) * LANES]
    final = result[...].reshape(NFW, 2, focal, LANES)
    if base_ref is not None:
        final += base_ref[...].astype(F32)
    out_ref[...] = final.astype(BF16)


def window(parts, forward, inverse, onset_times, base=None, want_spec=False):
    focal = parts[0].shape[2]
    k = 2 * NFW
    operands = [forward, inverse, onset_times, *parts] + ([] if base is None else [base])
    out = jax.ShapeDtypeStruct((NFW, 2, focal, LANES), BF16)
    if want_spec:
        out = jax.ShapeDtypeStruct((focal, k, LANES), BF16)
    return pl.pallas_call(
        functools.partial(window_kernel, len(parts), base is not None, want_spec),
        in_specs=[VMEM] * len(operands),
        out_specs=VMEM,
        out_shape=out,
        scratch_shapes=[pltpu.VMEM((k * focal, LANES), F32)] * 2,
        compiler_params=limit(8),
        cost_estimate=pl.CostEstimate(
            flops=4 * k * NT * focal * LANES, bytes_accessed=2 * k * focal * LANES * 6, transcendentals=0
        ),
        name="window",
    )(*operands)


def window_at_kernel(line, flip, step, begun, *refs):
    forward_ref, inverse_ref, onset_ref, chip_inverse_ref, spec_ref = refs[:5]
    out_ref, keep_ref, send_ref, result, made, sems = refs[5 + 2 * begun :]
    core = own_place(line)[3]
    focal, k, _ = spec_ref.shape
    start = chip_columns(line, False, flip, step) + core * LANES
    columns = pl.ds(pl.multiple_of(start, LANES), LANES)
    samples = made.shape[2]
    chip = lax.axis_index("blk") // 2
    chip_inverse = chip_inverse_ref[chip]
    first = chip * (2 * samples)
    time = first + lax.broadcasted_iota(jnp.int32, (2 * samples, 2 * LANES), 0)

    def pair_of(p):
        onset = [onset_ref[p + q : p + q + 1, columns] for q in range(2)]
        return [spec_ref[p + q] for q in range(2)], onset

    for p in range(0, focal, 2):
        pair, onset = pair_of(p)
        values = jnp.dot(chip_inverse, jnp.concatenate(pair, axis=1), preferred_element_type=F32)
        values = jnp.where(time < jnp.concatenate(onset, axis=1), values, 0.0).astype(BF16)
        low, high = values[:samples], values[samples:]
        mine, theirs = jnp.where(core == 0, low, high), jnp.where(core == 0, high, low)
        for q in range(2):
            part = slice(q * LANES, (q + 1) * LANES)
            made[0, p + q] = mine[:, part]
            made[1, p + q] = theirs[:, part]
    place = pl.ds((flip * line + step) * LANES, LANES)
    copies = [
        pltpu.make_async_copy(made.at[side], target.at[:, :, place], sems.at[side])
        for side, target in enumerate((keep_ref, send_ref))
    ]
    for copy in copies:
        copy.start()
    for p in range(0, focal, 2):
        pair, onset = pair_of(p)
        spectrum = windowed_spectrum(pair, onset, forward_ref[...], inverse_ref[...])
        for q in range(2):
            result[pl.ds(p + q, k, stride=focal), :] = spectrum[:, q * LANES : (q + 1) * LANES]
    out_ref[...] = result[...].reshape(NFW, 2, focal, LANES).astype(BF16)
    for copy in copies:
        copy.wait()


def window_at(spec, forward, inverse, onset_times, chip_inverse, line, flip, step, fields):
    focal, k, _ = spec.shape
    samples = chip_inverse.shape[1] // 2
    field_shape = jax.ShapeDtypeStruct((focal, samples, 2 * line * LANES), BF16)
    begun = bool(fields)
    return pl.pallas_call(
        functools.partial(window_at_kernel, line, flip, step, begun),
        in_specs=[VMEM] * 5 + [FAR] * len(fields),
        out_specs=[VMEM, FAR, FAR],
        out_shape=[jax.ShapeDtypeStruct((NFW, 2, focal, LANES), BF16), field_shape, field_shape],
        input_output_aliases={5: 1, 6: 2} if begun else {},
        scratch_shapes=[
            pltpu.VMEM((k * focal, LANES), F32),
            pltpu.VMEM((2, focal, samples, LANES), BF16),
            pltpu.SemaphoreType.DMA((2,)),
        ],
        compiler_params=limit(8),
        cost_estimate=pl.CostEstimate(
            flops=4 * k * NT * focal * LANES, bytes_accessed=2 * k * focal * LANES * 6, transcendentals=0
        ),
        name="window_at",
    )(forward, inverse, onset_times, chip_inverse, spec, *fields)


def merge_kernel(line, mine, theirs, out_ref, made, sems):
    core = own_place(line)[3]
    copy, rows = strip_copies(made, out_ref, sems, STRIPS)

    def body(strip, carry):
        for row in range(rows):
            p = strip * rows + row
            for at, (flip, step) in enumerate(relative(line)):
                columns = pl.ds(chip_columns(line, False, flip, step), 2 * LANES)
                part = pl.ds(at * LANES, LANES)
                made[p, :, columns] = join_cores(core, mine[p, :, part], theirs[p, :, part])
        copy(strip).start()
        return carry

    lax.fori_loop(0, STRIPS, body, 0)
    for strip in range(STRIPS):
        copy(strip).wait()


def merge(mine, theirs, line):
    focal, samples, width = mine.shape
    shape = (focal, samples, 2 * width)
    return pl.pallas_call(
        functools.partial(merge_kernel, line),
        in_specs=[VMEM] * 2,
        out_specs=FAR,
        out_shape=jax.ShapeDtypeStruct(shape, BF16),
        scratch_shapes=[pltpu.VMEM(shape, BF16), pltpu.SemaphoreType.DMA((STRIPS,))],
        compiler_params=limit(6),
        cost_estimate=pl.CostEstimate(flops=0, bytes_accessed=8 * mine.size, transcendentals=0),
        name="merge",
    )(mine, theirs)


def field_kernel(line, has_plus, inverse_ref, onset_ref, *refs):
    core = own_place(line)[3]
    places = relative(line)
    own, other = refs[: len(places)], refs[len(places) : 2 * len(places)]
    rest = list(refs[2 * len(places) :])
    plus_ref = rest.pop(0) if has_plus else None
    out_ref, made, out_sems, *spare = rest
    samples = out_ref.shape[1]
    inverse = inverse_ref[own_place(line)[0]]
    out_copy, rows = strip_copies(made, out_ref, out_sems, STRIPS)
    if has_plus:
        plus, plus_sems = spare
        plus_copy, _ = strip_copies(plus_ref, plus, plus_sems, STRIPS)
        for strip in range(STRIPS):
            plus_copy(strip).start()
    time = lax.axis_index("blk") * samples + lax.broadcasted_iota(jnp.int32, (samples, 2 * LANES), 0)

    def body(strip, carry):
        if has_plus:
            plus_copy(strip).wait()
        for row in range(rows):
            p = strip * rows + row
            for at, (flip, step) in enumerate(places):
                columns = pl.ds(chip_columns(line, False, flip, step), 2 * LANES)
                spec = join_cores(core, own[at][p], other[at][p])
                values = jnp.dot(inverse, spec, preferred_element_type=F32)
                values = jnp.where(time < onset_ref[pl.ds(p, 1), columns], values, 0.0)
                if has_plus:
                    values += plus[p, :, columns].astype(F32)
                made[p, :, columns] = values.astype(BF16)
        out_copy(strip).start()
        return carry

    lax.fori_loop(0, STRIPS, body, 0)
    for strip in range(STRIPS):
        out_copy(strip).wait()


def field(own, other, inverse, onset_times, line, plus_start=None):
    own, other = sum(own, []), sum(other, [])
    focal, k, _ = own[0].shape
    samples = inverse.shape[1]
    shape = (focal, samples, onset_times.shape[1])
    plus = [] if plus_start is None else [plus_start]
    moved = [pltpu.VMEM(shape, BF16), pltpu.SemaphoreType.DMA((STRIPS,))]
    return pl.pallas_call(
        functools.partial(field_kernel, line, bool(plus)),
        in_specs=[VMEM] * (2 + len(own) + len(other)) + [FAR] * len(plus),
        out_specs=FAR,
        out_shape=jax.ShapeDtypeStruct(shape, BF16),
        scratch_shapes=moved * (1 + len(plus)),
        compiler_params=limit(12),
        cost_estimate=pl.CostEstimate(
            flops=2 * k * math.prod(shape),
            bytes_accessed=4 * math.prod(shape) + 2 * k * focal * shape[2],
            transcendentals=0,
        ),
        name="field",
    )(inverse, onset_times, *own, *other, *plus)


def add(*parts):
    total = parts[0].astype(F32)
    for part in parts[1:]:
        total += part.astype(F32)
    return total


def after(value, *others):
    return lax.optimization_barrier((value, *others))[0] if others else value


def reduce_scatter(places, keep0, keep1, send0, send1):
    size = places.line
    got1 = places.send(send1, places.core())
    got0 = places.send(send0, places.core())
    far = [add(keep, got).astype(BF16) for keep, got in zip(keep1, got1)]
    across = {step: places.send(far[step], places.pair()) for step in range(2, size)}
    beside = [places.send(far[1], places.shift(1))] if size > 1 else []
    parts = [keep0[0], got0[0]]

    def pass_on(steps, shift, *first):
        carried, sent = [], []
        for step in steps:
            crossed = [after(across[step], *first)] if step in across else []
            carried = [places.send(add(keep0[step], got0[step], *crossed, *carried).astype(BF16), places.shift(shift))]
            sent += carried
        return sent

    ahead = pass_on(range(size // 2, 0, -1), 1)
    behind = pass_on(range(size // 2 + 1, size), size - 1, *ahead[:1])
    parts += ahead[-1:] + behind[-1:]
    across[0] = places.send(add(keep1[0], got1[0], *beside).astype(BF16), places.pair())
    return parts + [across[0]]


def gather_chips(places, block, work=None, together=False):
    size = places.line
    near = [1, size - 1] if size > 2 else [1] if size > 1 else []
    far = list(range(2, size - 1))
    made = {}

    def run(flip, steps, pieces, *others):
        if work is None:
            return []
        for step in steps:
            made[flip, step] = work(after(pieces[step], *others), flip, step)
        return [made[flip, step] for step in steps]

    line = {0: block}
    for step in near:
        line[step] = places.send(block, places.shift(step))
    across = {0: places.send(block, places.pair())}
    own = run(0, [0], line)
    if together:
        own = [line[size - 1]]
    for step in range(2, size // 2 + 1):
        line[step] = places.send(after(line[step - 1], across[0], *own), places.shift(1))
    for step in range(size - 2, size // 2, -1):
        line[step] = places.send(after(line[step + 1], *own), places.shift(size - 1))
    for step in near:
        if step == 1:
            across[step] = places.send(after(across[0], line[size - 1]), places.shift(1))
        else:
            across[step] = places.send(line[step], places.pair())
    middle = run(1, [0], across) + run(0, near, line)
    for step in far:
        across[step] = places.send(after(line[step], *middle), places.pair())
    late = run(0, far, line) + run(1, near, across)
    run(1, far, across, *late)
    pieces = [[side[step] for step in range(size)] for side in (line, across)]
    results = [[made[flip, step] for step in range(size)] for flip in range(2)] if work else None
    return pieces, results


def swap_cores(places, pieces):
    return [places.send(piece, places.core()) for piece in pieces]


def local(plus_start, reflection, onset_times):
    size = lax.axis_size("blk")
    places = Places("blk", size)
    line = places.line
    focal, samples, _ = plus_start.shape
    forward, inverse = constant_tables()
    own_forward = np.ascontiguousarray(forward.reshape(2 * NFW, size, samples).transpose(1, 0, 2))
    own_inverse = inverse.reshape(size, samples, 2 * NFW)
    chip_inverse = inverse.reshape(size // 2, 2 * samples, 2 * NFW)
    sure = forward[:, :SURE].astype(np.float32) @ inverse[:SURE].astype(np.float32)
    forward = jnp.asarray(np.concatenate([forward[:, SURE:], sure.astype(BF16)], axis=1))
    inverse = jnp.asarray(inverse[SURE:])
    own_forward, own_inverse, chip_inverse = map(jnp.asarray, (own_forward, own_inverse, chip_inverse))

    fields = []

    def window_piece(piece, flip, step):
        spectrum, *fields[:] = window_at(
            piece, forward, inverse, onset_times, chip_inverse, line, flip, step, tuple(fields)
        )
        return spectrum

    parts = reduce_scatter(places, *first_analysis(plus_start, own_forward, line))
    start = add(*parts).astype(BF16)
    start = jnp.transpose(start, (1, 0, 2)).reshape(NFW, 2, focal, LANES)
    spectrum_plus = start
    for iteration in range(ITERS):
        last = iteration + 1 == ITERS
        parts = reduce_scatter(places, *convolve(spectrum_plus, reflection, line))
        windowed = window(parts, forward, inverse, onset_times, want_spec=last)
        if last:
            _, own = gather_chips(places, windowed, window_piece)
        else:
            own, _ = gather_chips(places, windowed)
        half = correlate(own[0], swap_cores(places, own[0]), reflection, line, 0)
        across = [own[1][step] if step in (0, line - 1) else after(own[1][step], half) for step in range(line)]
        downgoing_spec = correlate(own[1], swap_cores(places, across), reflection, line, 1, half, last)
        if not last:
            spectrum_plus = window([downgoing_spec], forward, inverse, onset_times, base=start)
    mine, theirs = fields
    theirs = places.send(after(theirs, downgoing_spec), places.core())
    own, _ = gather_chips(places, downgoing_spec, together=True)
    upgoing = merge(mine, theirs, line)
    other = [swap_cores(places, own[0])]
    across = [own[1][step] if step in (0, 1, line - 1) else after(own[1][step], upgoing) for step in range(line)]
    other.append(swap_cores(places, across))
    downgoing = field(own, other, own_inverse, onset_times, line, plus_start)
    return upgoing, downgoing


def analyze(values, forward):
    total = jnp.einsum("kt,ptx->kpx", forward, values, preferred_element_type=F32)
    return total.reshape(NFW, 2, values.shape[0], values.shape[2])


def synthesize(spectrum, inverse):
    flat = spectrum.reshape(2 * NFW, spectrum.shape[2], spectrum.shape[3])
    return jnp.einsum("tk,kpx->ptx", inverse, flat, preferred_element_type=F32)


def contract(form, left, right):
    return jnp.einsum(form, left, right, preferred_element_type=F32)


def local_any(plus_start, reflection, onset_times):
    samples = plus_start.shape[1]
    width = reflection.shape[2]
    me = lax.axis_index("blk")
    forward, inverse = tables_of(jnp.arange(NT, dtype=jnp.int32))
    own_forward, own_inverse = tables_of(me * samples + jnp.arange(samples, dtype=jnp.int32))
    onset = lax.dynamic_slice_in_dim(onset_times, me * width, width, 1)
    keep = jnp.arange(NT, dtype=jnp.int32)[None, :, None] < onset[:, None, :]
    time = me * samples + jnp.arange(samples, dtype=jnp.int32)
    own_keep = time[None, :, None] < onset_times[:, None, :]

    def scatter(partial):
        return lax.psum_scatter(partial.astype(BF16), "blk", scatter_dimension=3, tiled=True).astype(BF16)

    def gather(block):
        return lax.all_gather(block, "blk", axis=3, tiled=True)

    start = scatter(analyze(plus_start, own_forward))
    spectrum = start
    for iteration in range(ITERS):
        real = contract("wrs,wpr->wps", reflection[0], spectrum[:, 0]) - contract(
            "wrs,wpr->wps", reflection[1], spectrum[:, 1]
        )
        imag = contract("wrs,wpr->wps", reflection[0], spectrum[:, 1]) + contract(
            "wrs,wpr->wps", reflection[1], spectrum[:, 0]
        )
        upgoing_spec = scatter(jnp.stack([real, imag], axis=1))
        kept = jnp.where(keep, synthesize(upgoing_spec, inverse), 0.0).astype(BF16)
        minus = gather(analyze(kept, forward).astype(BF16))
        real = contract("wrs,wps->wpr", reflection[0], minus[:, 0]) + contract(
            "wrs,wps->wpr", reflection[1], minus[:, 1]
        )
        imag = contract("wrs,wps->wpr", reflection[0], minus[:, 1]) - contract(
            "wrs,wps->wpr", reflection[1], minus[:, 0]
        )
        downgoing_spec = jnp.stack([real, imag], axis=1).astype(BF16)
        if iteration + 1 < ITERS:
            kept = jnp.where(keep, synthesize(downgoing_spec, inverse), 0.0).astype(BF16)
            spectrum = (start.astype(F32) + analyze(kept, forward)).astype(BF16)
    upgoing = jnp.where(own_keep, synthesize(gather(upgoing_spec), own_inverse), 0.0).astype(BF16)
    change = jnp.where(own_keep, synthesize(gather(downgoing_spec), own_inverse), 0.0)
    return upgoing, (plus_start.astype(F32) + change).astype(BF16)


def solution(mesh):
    size = mesh.shape["blk"]

    def run(plus_start, reflection, onset_times):
        width = reflection.shape[2] // size
        fits = width == LANES and size % 4 == 0 and (plus_start.shape[1] // size) % 16 == 0
        return jax.shard_map(
            local if fits else local_any,
            mesh=mesh,
            in_specs=(P("groups", "blk", None), P(None, None, "blk", None), P("groups", None)),
            out_specs=(P("groups", "blk", None), P("groups", "blk", None)),
            check_vma=False,
        )(plus_start, reflection, onset_times)

    return run
```

```python
import functools
import math

import jax
import jax.numpy as jnp
import numpy as np
from jax import lax
from jax.experimental import pallas as pl
from jax.experimental.pallas import tpu as pltpu
from jax.sharding import PartitionSpec as P

NT = 512
NFW = 32
FREQ0 = 16
ITERS = 2
SURE = 128
LANES = 128
F32 = jnp.float32
BF16 = jnp.bfloat16


def basis_of(samples):
    freqs = FREQ0 + jnp.arange(NFW, dtype=jnp.int32)
    turns = freqs[:, None] * samples[None, :] % NT
    phase = turns.astype(F32) * (2.0 * math.pi / NT)
    return jnp.stack([jnp.cos(phase), -jnp.sin(phase)], axis=1)


def tables_of(samples):
    basis = basis_of(samples).reshape(2 * NFW, samples.shape[0])
    forward = (basis * (1.0 / math.sqrt(NT))).astype(BF16)
    inverse = (basis * math.sqrt(2.0 / NFW)).astype(BF16)
    return forward, inverse.T


def constant_tables():
    freqs = FREQ0 + np.arange(NFW, dtype=np.int32)
    turns = freqs[:, None] * np.arange(NT, dtype=np.int32)[None, :] % NT
    phase = turns.astype(np.float32) * np.float32(2.0 * math.pi / NT)
    basis = np.stack([np.cos(phase), -np.sin(phase)], axis=1).reshape(2 * NFW, NT)
    forward = (basis * np.float32(1.0 / math.sqrt(NT))).astype(BF16)
    inverse = (basis * np.float32(math.sqrt(2.0 / NFW))).astype(BF16)
    return forward, np.ascontiguousarray(inverse.T)


class Places:
    def __init__(self, axis, size):
        self.axis = axis
        self.size = size
        self.line = size // 4

    def core(self):
        return [(b, b ^ 1) for b in range(self.size)]

    def pair(self):
        return [(b, b ^ 2) for b in range(self.size)]

    def shift(self, step):
        return [(b, (b // 4 + step) % self.line * 4 + b % 4) for b in range(self.size)]

    def send(self, array, pairs):
        return lax.ppermute(array, self.axis, pairs)


def own_place(line):
    me = lax.axis_index("blk")
    return me, me // 4, (me // 2) % 2, me % 2


def chip_columns(line, ahead, flip, step):
    _, l, m, _ = own_place(line)
    other = lax.rem(l + step, line) if ahead else lax.rem(l - step + line, line)
    chip = other * 2 + (lax.rem(m + flip, 2))
    return pl.multiple_of(chip * (2 * LANES), 2 * LANES)


def relative(line):
    return [(flip, step) for flip in range(2) for step in range(line)]


def split_cores(core, block):
    low, high = block[:, :LANES], block[:, LANES:]
    first = core == 0
    return jnp.where(first, low, high), jnp.where(first, high, low)


def join_cores(core, own, other):
    first = core == 0
    return jnp.concatenate([jnp.where(first, own, other), jnp.where(first, other, own)], axis=1)


VMEM = pl.BlockSpec(memory_space=pltpu.VMEM)
FAR = pl.BlockSpec(memory_space=pltpu.HBM)
CHUNKS = 8
STRIPS = 4
SLOTS = 4


def limit(mebibytes):
    return pltpu.CompilerParams(vmem_limit_bytes=mebibytes << 20)


def strip_copies(source, target, sems, strips):
    rows = source.shape[0] // strips

    def copy(strip):
        part = pl.ds(strip * rows, rows)
        return pltpu.make_async_copy(source.at[part], target.at[part], sems.at[strip])

    return copy, rows


def analysis_kernel(line, forward_ref, plus_ref, keep0, keep1, send0, send1, held, sems):
    core = own_place(line)[3]
    keep, send = (keep0, keep1), (send0, send1)
    forward = forward_ref[own_place(line)[0]]
    copy, rows = strip_copies(plus_ref, held, sems, STRIPS)
    for strip in range(STRIPS):
        copy(strip).start()

    def body(strip, carry):
        copy(strip).wait()
        for row in range(rows):
            p = strip * rows + row
            for flip, step in relative(line):
                columns = pl.ds(chip_columns(line, True, flip, step), 2 * LANES)
                block = jnp.dot(forward, held[p, :, columns], preferred_element_type=F32)
                mine, theirs = split_cores(core, block.astype(BF16))
                keep[flip][step, p] = mine
                send[flip][step, p] = theirs
        return carry

    lax.fori_loop(0, STRIPS, body, 0)


def first_analysis(plus_start, forward, line):
    focal, samples, width = plus_start.shape
    out = jax.ShapeDtypeStruct((line, focal, 2 * NFW, LANES), BF16)
    return pl.pallas_call(
        functools.partial(analysis_kernel, line),
        in_specs=[VMEM, FAR],
        out_specs=[VMEM] * 4,
        out_shape=[out] * 4,
        scratch_shapes=[pltpu.VMEM(plus_start.shape, BF16), pltpu.SemaphoreType.DMA((STRIPS,))],
        compiler_params=limit(8),
        cost_estimate=pl.CostEstimate(
            flops=4 * NFW * focal * samples * width,
            bytes_accessed=2 * focal * samples * width + 4 * NFW * focal * width,
            transcendentals=0,
        ),
        name="first_analysis",
    )(forward, plus_start)


def fetch_panels(line, ahead, flip, panel_ref, held, sems):
    slots, _, _, rows = held.shape[:4]

    def copy(chunk, step):
        slot = lax.rem(chunk, slots)
        columns = pl.ds(chip_columns(line, ahead, flip, step), 2 * LANES)
        source = panel_ref.at[:, pl.ds(chunk * rows, rows), :, columns]
        return pltpu.make_async_copy(source, held.at[slot, step], sems.at[slot, step])

    def start(chunk):
        for step in range(line):
            copy(chunk, step).start()

    def wait(chunk):
        for step in range(line):
            copy(chunk, step).wait()

    for chunk in range(slots):
        start(chunk)
    return wait, start


def panel_scratch(line):
    rows = NFW // CHUNKS
    return [
        pltpu.VMEM((SLOTS, line, 2, rows, LANES, 2 * LANES), BF16),
        pltpu.SemaphoreType.DMA((SLOTS, line)),
    ]


def convolve_kernel(line, spec_ref, panel_ref, keep0, keep1, send0, send1, held, sems):
    core = own_place(line)[3]
    keep, send = (keep0, keep1), (send0, send1)
    focal = spec_ref.shape[2]
    rows = NFW // CHUNKS

    slots = held.shape[0]

    def copy(chunk):
        slot = lax.rem(chunk, slots)
        part = pl.ds(chunk * rows, rows)
        return pltpu.make_async_copy(panel_ref.at[:, part], held.at[slot], sems.at[slot])

    for chunk in range(slots):
        copy(chunk).start()

    def body(chunk, carry):
        copy(chunk).wait()
        slot = lax.rem(chunk, slots)
        for row in range(rows):
            w = chunk * rows + row
            real, imag = spec_ref[w, 0], spec_ref[w, 1]
            left = jnp.concatenate(
                [jnp.concatenate([real, -imag], axis=1), jnp.concatenate([imag, real], axis=1)], axis=0
            )
            for flip, step in relative(line):
                columns = pl.ds(chip_columns(line, True, flip, step), 2 * LANES)
                panel = held[slot, :, row, :, columns].reshape(2 * LANES, 2 * LANES)
                block = jnp.dot(left, panel, preferred_element_type=F32)
                mine, theirs = split_cores(core, block.astype(BF16))
                keep[flip][step, w] = mine.reshape(2, focal, LANES)
                send[flip][step, w] = theirs.reshape(2, focal, LANES)

        @pl.when(chunk + slots < CHUNKS)
        def _():
            copy(chunk + slots).start()

        return carry

    lax.fori_loop(0, CHUNKS, body, 0)


def panel_cost(focal, sources):
    return pl.CostEstimate(
        flops=8 * NFW * focal * LANES * sources,
        bytes_accessed=4 * NFW * sources * (LANES + focal),
        transcendentals=0,
    )


def convolve(spectrum, reflection, line):
    focal = spectrum.shape[2]
    out = jax.ShapeDtypeStruct((line, NFW, 2, focal, LANES), BF16)
    return pl.pallas_call(
        functools.partial(convolve_kernel, line),
        in_specs=[VMEM, FAR],
        out_specs=[VMEM] * 4,
        out_shape=[out] * 4,
        scratch_shapes=[
            pltpu.VMEM((SLOTS, 2, NFW // CHUNKS, LANES, reflection.shape[3]), BF16),
            pltpu.SemaphoreType.DMA((SLOTS,)),
        ],
        compiler_params=limit(20),
        cost_estimate=panel_cost(focal, reflection.shape[3]),
        name="convolve",
    )(spectrum, reflection)


def correlate_kernel(line, flip, has_base, final, *refs):
    core = own_place(line)[3]
    own, other, panel_ref = refs[:line], refs[line : 2 * line], refs[2 * line]
    base_ref = refs[2 * line + 1] if has_base else None
    out_ref, held, sems, *spare = refs[2 * line + 1 + has_base :]
    focal = own[0].shape[2]
    rows = held.shape[3]
    slots = held.shape[0]
    wait, start = fetch_panels(line, False, flip, panel_ref, held, sems)

    def body(chunk, carry):
        wait(chunk)
        slot = lax.rem(chunk, slots)
        for row in range(rows):
            w = chunk * rows + row
            panels, specs = [], []
            for step in range(line):
                panels.append(held[slot, step, :, row].reshape(2 * LANES, 2 * LANES))
                mine, theirs = own[step][w], other[step][w]
                specs.append(
                    join_cores(core, mine.reshape(2 * focal, LANES), theirs.reshape(2 * focal, LANES))
                )
            total = lax.dot_general(
                jnp.concatenate(specs, axis=1),
                jnp.concatenate(panels, axis=1),
                (((1,), (1,)), ((), ())),
                preferred_element_type=F32,
            )
            real = total[:focal, :LANES] + total[focal:, LANES:]
            imag = total[focal:, :LANES] - total[:focal, LANES:]
            if has_base:
                real += base_ref[w, 0]
                imag += base_ref[w, 1]
            if final:
                spare[0][pl.ds(2 * w * focal, focal), :] = real
                spare[0][pl.ds((2 * w + 1) * focal, focal), :] = imag
            else:
                out_ref[w, 0] = real
                out_ref[w, 1] = imag

        @pl.when(chunk + slots < CHUNKS)
        def _():
            start(chunk + slots)

        return carry

    lax.fori_loop(0, CHUNKS, body, 0)
    if final:
        for p in range(focal):
            out_ref[p] = spare[0][pl.ds(p, 2 * NFW, stride=focal), :].astype(BF16)


def correlate(own, other, reflection, line, flip, base=None, final=False):
    focal = own[0].shape[2]
    more = [] if base is None else [base]
    shape = jax.ShapeDtypeStruct((NFW, 2, focal, LANES), F32)
    if final:
        shape = jax.ShapeDtypeStruct((focal, 2 * NFW, LANES), BF16)
    spare = [pltpu.VMEM((2 * NFW * focal, LANES), F32)] if final else []
    return pl.pallas_call(
        functools.partial(correlate_kernel, line, flip, bool(more), final),
        in_specs=[VMEM] * (2 * line) + [FAR] + [VMEM] * len(more),
        out_specs=VMEM,
        out_shape=shape,
        scratch_shapes=panel_scratch(line) + spare,
        compiler_params=limit(24),
        cost_estimate=panel_cost(focal, reflection.shape[3] // 2),
        name=f"correlate{flip}",
    )(*own, *other, reflection, *more)


def windowed_spectrum(pair, onset, forward, inverse):
    time = SURE + lax.broadcasted_iota(jnp.int32, (NT - SURE, 2 * LANES), 0)
    spectra = jnp.concatenate(pair, axis=1)
    values = jnp.dot(inverse, spectra, preferred_element_type=F32)
    kept = jnp.where(time < jnp.concatenate(onset, axis=1), values, 0.0).astype(BF16)
    return jnp.dot(forward, jnp.concatenate([kept, spectra], axis=0), preferred_element_type=F32)


def window_kernel(parts, has_base, want_spec, *refs):
    refs = list(refs)
    forward_ref, inverse_ref, onset_ref = refs[:3]
    part_refs = refs[3 : 3 + parts]
    rest = refs[3 + parts :]
    base_ref = rest.pop(0) if has_base else None
    out_ref = rest.pop(0)
    held, result = rest
    focal = part_refs[0].shape[2]
    k = 2 * NFW
    total = part_refs[0][...].astype(F32)
    for ref in part_refs[1:]:
        total += ref[...].astype(F32)
    held[...] = total.reshape(k * focal, LANES)
    me = lax.axis_index("blk")
    columns = pl.ds(pl.multiple_of(me * LANES, LANES), LANES)
    if want_spec:
        for p in range(focal):
            out_ref[p] = held[pl.ds(p, k, stride=focal), :].astype(BF16)
        return
    for p in range(0, focal, 2):
        pair = [held[pl.ds(p + q, k, stride=focal), :].astype(BF16) for q in range(2)]
        onset = [onset_ref[p + q : p + q + 1, columns] for q in range(2)]
        spectrum = windowed_spectrum(pair, onset, forward_ref[...], inverse_ref[...])
        for q in range(2):
            result[pl.ds(p + q, k, stride=focal), :] = spectrum[:, q * LANES : (q + 1) * LANES]
    final = result[...].reshape(NFW, 2, focal, LANES)
    if base_ref is not None:
        final += base_ref[...].astype(F32)
    out_ref[...] = final.astype(BF16)


def window(parts, forward, inverse, onset_times, base=None, want_spec=False):
    focal = parts[0].shape[2]
    k = 2 * NFW
    operands = [forward, inverse, onset_times, *parts] + ([] if base is None else [base])
    out = jax.ShapeDtypeStruct((NFW, 2, focal, LANES), BF16)
    if want_spec:
        out = jax.ShapeDtypeStruct((focal, k, LANES), BF16)
    return pl.pallas_call(
        functools.partial(window_kernel, len(parts), base is not None, want_spec),
        in_specs=[VMEM] * len(operands),
        out_specs=VMEM,
        out_shape=out,
        scratch_shapes=[pltpu.VMEM((k * focal, LANES), F32)] * 2,
        compiler_params=limit(8),
        cost_estimate=pl.CostEstimate(
            flops=4 * k * NT * focal * LANES, bytes_accessed=2 * k * focal * LANES * 6, transcendentals=0
        ),
        name="window",
    )(*operands)


def window_at_kernel(line, flip, step, begun, *refs):
    forward_ref, inverse_ref, onset_ref, chip_inverse_ref, spec_ref = refs[:5]
    out_ref, keep_ref, send_ref, result, made, sems = refs[5 + 2 * begun :]
    core = own_place(line)[3]
    focal, k, _ = spec_ref.shape
    start = chip_columns(line, False, flip, step) + core * LANES
    columns = pl.ds(pl.multiple_of(start, LANES), LANES)
    samples = made.shape[2]
    chip = lax.axis_index("blk") // 2
    chip_inverse = chip_inverse_ref[chip]
    first = chip * (2 * samples)
    time = first + lax.broadcasted_iota(jnp.int32, (2 * samples, 2 * LANES), 0)

    def pair_of(p):
        onset = [onset_ref[p + q : p + q + 1, columns] for q in range(2)]
        return [spec_ref[p + q] for q in range(2)], onset

    for p in range(0, focal, 2):
        pair, onset = pair_of(p)
        values = jnp.dot(chip_inverse, jnp.concatenate(pair, axis=1), preferred_element_type=F32)
        values = jnp.where(time < jnp.concatenate(onset, axis=1), values, 0.0).astype(BF16)
        low, high = values[:samples], values[samples:]
        mine, theirs = jnp.where(core == 0, low, high), jnp.where(core == 0, high, low)
        for q in range(2):
            part = slice(q * LANES, (q + 1) * LANES)
            made[0, p + q] = mine[:, part]
            made[1, p + q] = theirs[:, part]
    place = pl.ds((flip * line + step) * LANES, LANES)
    copies = [
        pltpu.make_async_copy(made.at[side], target.at[:, :, place], sems.at[side])
        for side, target in enumerate((keep_ref, send_ref))
    ]
    for copy in copies:
        copy.start()
    for p in range(0, focal, 2):
        pair, onset = pair_of(p)
        spectrum = windowed_spectrum(pair, onset, forward_ref[...], inverse_ref[...])
        for q in range(2):
            result[pl.ds(p + q, k, stride=focal), :] = spectrum[:, q * LANES : (q + 1) * LANES]
    out_ref[...] = result[...].reshape(NFW, 2, focal, LANES).astype(BF16)
    for copy in copies:
        copy.wait()


def window_at(spec, forward, inverse, onset_times, chip_inverse, line, flip, step, fields):
    focal, k, _ = spec.shape
    samples = chip_inverse.shape[1] // 2
    field_shape = jax.ShapeDtypeStruct((focal, samples, 2 * line * LANES), BF16)
    begun = bool(fields)
    return pl.pallas_call(
        functools.partial(window_at_kernel, line, flip, step, begun),
        in_specs=[VMEM] * 5 + [FAR] * len(fields),
        out_specs=[VMEM, FAR, FAR],
        out_shape=[jax.ShapeDtypeStruct((NFW, 2, focal, LANES), BF16), field_shape, field_shape],
        input_output_aliases={5: 1, 6: 2} if begun else {},
        scratch_shapes=[
            pltpu.VMEM((k * focal, LANES), F32),
            pltpu.VMEM((2, focal, samples, LANES), BF16),
            pltpu.SemaphoreType.DMA((2,)),
        ],
        compiler_params=limit(8),
        cost_estimate=pl.CostEstimate(
            flops=4 * k * NT * focal * LANES, bytes_accessed=2 * k * focal * LANES * 6, transcendentals=0
        ),
        name="window_at",
    )(forward, inverse, onset_times, chip_inverse, spec, *fields)


def merge_kernel(line, mine, theirs, out_ref, made, sems):
    core = own_place(line)[3]
    copy, rows = strip_copies(made, out_ref, sems, STRIPS)

    def body(strip, carry):
        for row in range(rows):
            p = strip * rows + row
            for at, (flip, step) in enumerate(relative(line)):
                columns = pl.ds(chip_columns(line, False, flip, step), 2 * LANES)
                part = pl.ds(at * LANES, LANES)
                made[p, :, columns] = join_cores(core, mine[p, :, part], theirs[p, :, part])
        copy(strip).start()
        return carry

    lax.fori_loop(0, STRIPS, body, 0)
    for strip in range(STRIPS):
        copy(strip).wait()


def merge(mine, theirs, line):
    focal, samples, width = mine.shape
    shape = (focal, samples, 2 * width)
    return pl.pallas_call(
        functools.partial(merge_kernel, line),
        in_specs=[VMEM] * 2,
        out_specs=FAR,
        out_shape=jax.ShapeDtypeStruct(shape, BF16),
        scratch_shapes=[pltpu.VMEM(shape, BF16), pltpu.SemaphoreType.DMA((STRIPS,))],
        compiler_params=limit(6),
        cost_estimate=pl.CostEstimate(flops=0, bytes_accessed=8 * mine.size, transcendentals=0),
        name="merge",
    )(mine, theirs)


def field_kernel(line, has_plus, inverse_ref, onset_ref, *refs):
    core = own_place(line)[3]
    places = relative(line)
    own, other = refs[: len(places)], refs[len(places) : 2 * len(places)]
    rest = list(refs[2 * len(places) :])
    plus_ref = rest.pop(0) if has_plus else None
    out_ref, made, out_sems, *spare = rest
    samples = out_ref.shape[1]
    inverse = inverse_ref[own_place(line)[0]]
    out_copy, rows = strip_copies(made, out_ref, out_sems, STRIPS)
    if has_plus:
        plus, plus_sems = spare
        plus_copy, _ = strip_copies(plus_ref, plus, plus_sems, STRIPS)
        for strip in range(STRIPS):
            plus_copy(strip).start()
    time = lax.axis_index("blk") * samples + lax.broadcasted_iota(jnp.int32, (samples, 2 * LANES), 0)

    def body(strip, carry):
        if has_plus:
            plus_copy(strip).wait()
        for row in range(rows):
            p = strip * rows + row
            for at, (flip, step) in enumerate(places):
                columns = pl.ds(chip_columns(line, False, flip, step), 2 * LANES)
                spec = join_cores(core, own[at][p], other[at][p])
                values = jnp.dot(inverse, spec, preferred_element_type=F32)
                values = jnp.where(time < onset_ref[pl.ds(p, 1), columns], values, 0.0)
                if has_plus:
                    values += plus[p, :, columns].astype(F32)
                made[p, :, columns] = values.astype(BF16)
        out_copy(strip).start()
        return carry

    lax.fori_loop(0, STRIPS, body, 0)
    for strip in range(STRIPS):
        out_copy(strip).wait()


def field(own, other, inverse, onset_times, line, plus_start=None):
    own, other = sum(own, []), sum(other, [])
    focal, k, _ = own[0].shape
    samples = inverse.shape[1]
    shape = (focal, samples, onset_times.shape[1])
    plus = [] if plus_start is None else [plus_start]
    moved = [pltpu.VMEM(shape, BF16), pltpu.SemaphoreType.DMA((STRIPS,))]
    return pl.pallas_call(
        functools.partial(field_kernel, line, bool(plus)),
        in_specs=[VMEM] * (2 + len(own) + len(other)) + [FAR] * len(plus),
        out_specs=FAR,
        out_shape=jax.ShapeDtypeStruct(shape, BF16),
        scratch_shapes=moved * (1 + len(plus)),
        compiler_params=limit(12),
        cost_estimate=pl.CostEstimate(
            flops=2 * k * math.prod(shape),
            bytes_accessed=4 * math.prod(shape) + 2 * k * focal * shape[2],
            transcendentals=0,
        ),
        name="field",
    )(inverse, onset_times, *own, *other, *plus)


def add(*parts):
    total = parts[0].astype(F32)
    for part in parts[1:]:
        total += part.astype(F32)
    return total


def after(value, *others):
    return lax.optimization_barrier((value, *others))[0] if others else value


def reduce_scatter(places, keep0, keep1, send0, send1):
    size = places.line
    got1 = places.send(send1, places.core())
    got0 = places.send(send0, places.core())
    far = [add(keep, got).astype(BF16) for keep, got in zip(keep1, got1)]
    across = {step: places.send(far[step], places.pair()) for step in range(2, size)}
    beside = [places.send(far[1], places.shift(1))] if size > 1 else []
    parts = [keep0[0], got0[0]]

    def pass_on(steps, shift, *first):
        carried, sent = [], []
        for step in steps:
            crossed = [after(across[step], *first)] if step in across else []
            carried = [places.send(add(keep0[step], got0[step], *crossed, *carried).astype(BF16), places.shift(shift))]
            sent += carried
        return sent

    ahead = pass_on(range(size // 2, 0, -1), 1)
    behind = pass_on(range(size // 2 + 1, size), size - 1, *ahead[:1])
    parts += ahead[-1:] + behind[-1:]
    across[0] = places.send(add(keep1[0], got1[0], *beside).astype(BF16), places.pair())
    return parts + [across[0]]


def gather_chips(places, block, work=None, together=False):
    size = places.line
    near = [1, size - 1] if size > 2 else [1] if size > 1 else []
    far = list(range(2, size - 1))
    made = {}

    def run(flip, steps, pieces, *others):
        if work is None:
            return []
        for step in steps:
            made[flip, step] = work(after(pieces[step], *others), flip, step)
        return [made[flip, step] for step in steps]

    line = {0: block}
    for step in near:
        line[step] = places.send(block, places.shift(step))
    across = {0: places.send(block, places.pair())}
    own = run(0, [0], line)
    if together:
        own = [line[size - 1]]
    for step in range(2, size // 2 + 1):
        line[step] = places.send(after(line[step - 1], across[0], *own), places.shift(1))
    for step in range(size - 2, size // 2, -1):
        line[step] = places.send(after(line[step + 1], *own), places.shift(size - 1))
    for step in near:
        if step == 1:
            across[step] = places.send(after(across[0], line[size - 1]), places.shift(1))
        else:
            across[step] = places.send(line[step], places.pair())
    middle = [across[step] for step in near] if together else run(1, [0], across) + run(0, near, line)
    for step in far:
        across[step] = places.send(after(line[step], *middle), places.pair())
    late = run(0, far, line) + run(1, near, across)
    run(1, far, across, *late)
    pieces = [[side[step] for step in range(size)] for side in (line, across)]
    results = [[made[flip, step] for step in range(size)] for flip in range(2)] if work else None
    return pieces, results


def swap_cores(places, pieces):
    return [places.send(piece, places.core()) for piece in pieces]


def local(plus_start, reflection, onset_times):
    size = lax.axis_size("blk")
    places = Places("blk", size)
    line = places.line
    focal, samples, _ = plus_start.shape
    forward, inverse = constant_tables()
    own_forward = np.ascontiguousarray(forward.reshape(2 * NFW, size, samples).transpose(1, 0, 2))
    own_inverse = inverse.reshape(size, samples, 2 * NFW)
    chip_inverse = inverse.reshape(size // 2, 2 * samples, 2 * NFW)
    sure = forward[:, :SURE].astype(np.float32) @ inverse[:SURE].astype(np.float32)
    forward = jnp.asarray(np.concatenate([forward[:, SURE:], sure.astype(BF16)], axis=1))
    inverse = jnp.asarray(inverse[SURE:])
    own_forward, own_inverse, chip_inverse = map(jnp.asarray, (own_forward, own_inverse, chip_inverse))

    fields = []

    def window_piece(piece, flip, step):
        spectrum, *fields[:] = window_at(
            piece, forward, inverse, onset_times, chip_inverse, line, flip, step, tuple(fields)
        )
        return spectrum

    parts = reduce_scatter(places, *first_analysis(plus_start, own_forward, line))
    start = add(*parts).astype(BF16)
    start = jnp.transpose(start, (1, 0, 2)).reshape(NFW, 2, focal, LANES)
    spectrum_plus = start
    for iteration in range(ITERS):
        last = iteration + 1 == ITERS
        parts = reduce_scatter(places, *convolve(spectrum_plus, reflection, line))
        windowed = window(parts, forward, inverse, onset_times, want_spec=last)
        if last:
            _, own = gather_chips(places, windowed, window_piece)
        else:
            own, _ = gather_chips(places, windowed)
        half = correlate(own[0], swap_cores(places, own[0]), reflection, line, 0)
        across = [own[1][step] if step == 0 else after(own[1][step], half) for step in range(line)]
        downgoing_spec = correlate(own[1], swap_cores(places, across), reflection, line, 1, half, last)
        if not last:
            spectrum_plus = window([downgoing_spec], forward, inverse, onset_times, base=start)
    mine, theirs = fields
    theirs = places.send(after(theirs, downgoing_spec), places.core())
    own, _ = gather_chips(places, downgoing_spec, together=True)
    upgoing = merge(mine, theirs, line)
    other = [swap_cores(places, own[0])]
    across = [own[1][step] if step in (0, 1, line - 1) else after(own[1][step], upgoing) for step in range(line)]
    other.append(swap_cores(places, across))
    downgoing = field(own, other, own_inverse, onset_times, line, plus_start)
    return upgoing, downgoing


def analyze(values, forward):
    total = jnp.einsum("kt,ptx->kpx", forward, values, preferred_element_type=F32)
    return total.reshape(NFW, 2, values.shape[0], values.shape[2])


def synthesize(spectrum, inverse):
    flat = spectrum.reshape(2 * NFW, spectrum.shape[2], spectrum.shape[3])
    return jnp.einsum("tk,kpx->ptx", inverse, flat, preferred_element_type=F32)


def contract(form, left, right):
    return jnp.einsum(form, left, right, preferred_element_type=F32)


def local_any(plus_start, reflection, onset_times):
    samples = plus_start.shape[1]
    width = reflection.shape[2]
    me = lax.axis_index("blk")
    forward, inverse = tables_of(jnp.arange(NT, dtype=jnp.int32))
    own_forward, own_inverse = tables_of(me * samples + jnp.arange(samples, dtype=jnp.int32))
    onset = lax.dynamic_slice_in_dim(onset_times, me * width, width, 1)
    keep = jnp.arange(NT, dtype=jnp.int32)[None, :, None] < onset[:, None, :]
    time = me * samples + jnp.arange(samples, dtype=jnp.int32)
    own_keep = time[None, :, None] < onset_times[:, None, :]

    def scatter(partial):
        return lax.psum_scatter(partial.astype(BF16), "blk", scatter_dimension=3, tiled=True).astype(BF16)

    def gather(block):
        return lax.all_gather(block, "blk", axis=3, tiled=True)

    start = scatter(analyze(plus_start, own_forward))
    spectrum = start
    for iteration in range(ITERS):
        real = contract("wrs,wpr->wps", reflection[0], spectrum[:, 0]) - contract(
            "wrs,wpr->wps", reflection[1], spectrum[:, 1]
        )
        imag = contract("wrs,wpr->wps", reflection[0], spectrum[:, 1]) + contract(
            "wrs,wpr->wps", reflection[1], spectrum[:, 0]
        )
        upgoing_spec = scatter(jnp.stack([real, imag], axis=1))
        kept = jnp.where(keep, synthesize(upgoing_spec, inverse), 0.0).astype(BF16)
        minus = gather(analyze(kept, forward).astype(BF16))
        real = contract("wrs,wps->wpr", reflection[0], minus[:, 0]) + contract(
            "wrs,wps->wpr", reflection[1], minus[:, 1]
        )
        imag = contract("wrs,wps->wpr", reflection[0], minus[:, 1]) - contract(
            "wrs,wps->wpr", reflection[1], minus[:, 0]
        )
        downgoing_spec = jnp.stack([real, imag], axis=1).astype(BF16)
        if iteration + 1 < ITERS:
            kept = jnp.where(keep, synthesize(downgoing_spec, inverse), 0.0).astype(BF16)
            spectrum = (start.astype(F32) + analyze(kept, forward)).astype(BF16)
    upgoing = jnp.where(own_keep, synthesize(gather(upgoing_spec), own_inverse), 0.0).astype(BF16)
    change = jnp.where(own_keep, synthesize(gather(downgoing_spec), own_inverse), 0.0)
    return upgoing, (plus_start.astype(F32) + change).astype(BF16)


def solution(mesh):
    size = mesh.shape["blk"]

    def run(plus_start, reflection, onset_times):
        width = reflection.shape[2] // size
        fits = width == LANES and size % 4 == 0 and (plus_start.shape[1] // size) % 16 == 0
        return jax.shard_map(
            local if fits else local_any,
            mesh=mesh,
            in_specs=(P("groups", "blk", None), P(None, None, "blk", None), P("groups", None)),
            out_specs=(P("groups", "blk", None), P("groups", "blk", None)),
            check_vma=False,
        )(plus_start, reflection, onset_times)

    return run
```

```python
import functools
import math

import jax
import jax.numpy as jnp
import numpy as np
from jax import lax
from jax.experimental import pallas as pl
from jax.experimental.pallas import tpu as pltpu
from jax.sharding import PartitionSpec as P

NT = 512
NFW = 32
FREQ0 = 16
ITERS = 2
SURE = 128
LANES = 128
F32 = jnp.float32
BF16 = jnp.bfloat16


def basis_of(samples):
    freqs = FREQ0 + jnp.arange(NFW, dtype=jnp.int32)
    turns = freqs[:, None] * samples[None, :] % NT
    phase = turns.astype(F32) * (2.0 * math.pi / NT)
    return jnp.stack([jnp.cos(phase), -jnp.sin(phase)], axis=1)


def tables_of(samples):
    basis = basis_of(samples).reshape(2 * NFW, samples.shape[0])
    forward = (basis * (1.0 / math.sqrt(NT))).astype(BF16)
    inverse = (basis * math.sqrt(2.0 / NFW)).astype(BF16)
    return forward, inverse.T


def constant_tables():
    freqs = FREQ0 + np.arange(NFW, dtype=np.int32)
    turns = freqs[:, None] * np.arange(NT, dtype=np.int32)[None, :] % NT
    phase = turns.astype(np.float32) * np.float32(2.0 * math.pi / NT)
    basis = np.stack([np.cos(phase), -np.sin(phase)], axis=1).reshape(2 * NFW, NT)
    forward = (basis * np.float32(1.0 / math.sqrt(NT))).astype(BF16)
    inverse = (basis * np.float32(math.sqrt(2.0 / NFW))).astype(BF16)
    return forward, np.ascontiguousarray(inverse.T)


class Places:
    def __init__(self, axis, size):
        self.axis = axis
        self.size = size
        self.line = size // 4

    def core(self):
        return [(b, b ^ 1) for b in range(self.size)]

    def pair(self):
        return [(b, b ^ 2) for b in range(self.size)]

    def shift(self, step):
        return [(b, (b // 4 + step) % self.line * 4 + b % 4) for b in range(self.size)]

    def send(self, array, pairs):
        return lax.ppermute(array, self.axis, pairs)


def own_place(line):
    me = lax.axis_index("blk")
    return me, me // 4, (me // 2) % 2, me % 2


def chip_columns(line, ahead, flip, step):
    _, l, m, _ = own_place(line)
    other = lax.rem(l + step, line) if ahead else lax.rem(l - step + line, line)
    chip = other * 2 + (lax.rem(m + flip, 2))
    return pl.multiple_of(chip * (2 * LANES), 2 * LANES)


def relative(line):
    return [(flip, step) for flip in range(2) for step in range(line)]


def split_cores(core, block):
    low, high = block[:, :LANES], block[:, LANES:]
    first = core == 0
    return jnp.where(first, low, high), jnp.where(first, high, low)


def join_cores(core, own, other):
    first = core == 0
    return jnp.concatenate([jnp.where(first, own, other), jnp.where(first, other, own)], axis=1)


VMEM = pl.BlockSpec(memory_space=pltpu.VMEM)
FAR = pl.BlockSpec(memory_space=pltpu.HBM)
CHUNKS = 8
STRIPS = 4
SLOTS = 4


def limit(mebibytes):
    return pltpu.CompilerParams(vmem_limit_bytes=mebibytes << 20)


def strip_copies(source, target, sems, strips):
    rows = source.shape[0] // strips

    def copy(strip):
        part = pl.ds(strip * rows, rows)
        return pltpu.make_async_copy(source.at[part], target.at[part], sems.at[strip])

    return copy, rows


def analysis_kernel(line, forward_ref, plus_ref, keep0, keep1, send0, send1, held, sems):
    core = own_place(line)[3]
    keep, send = (keep0, keep1), (send0, send1)
    forward = forward_ref[own_place(line)[0]]
    copy, rows = strip_copies(plus_ref, held, sems, STRIPS)
    for strip in range(STRIPS):
        copy(strip).start()

    def body(strip, carry):
        copy(strip).wait()
        for row in range(rows):
            p = strip * rows + row
            for flip, step in relative(line):
                columns = pl.ds(chip_columns(line, True, flip, step), 2 * LANES)
                block = jnp.dot(forward, held[p, :, columns], preferred_element_type=F32)
                mine, theirs = split_cores(core, block.astype(BF16))
                keep[flip][step, p] = mine
                send[flip][step, p] = theirs
        return carry

    lax.fori_loop(0, STRIPS, body, 0)


def first_analysis(plus_start, forward, line):
    focal, samples, width = plus_start.shape
    out = jax.ShapeDtypeStruct((line, focal, 2 * NFW, LANES), BF16)
    return pl.pallas_call(
        functools.partial(analysis_kernel, line),
        in_specs=[VMEM, FAR],
        out_specs=[VMEM] * 4,
        out_shape=[out] * 4,
        scratch_shapes=[pltpu.VMEM(plus_start.shape, BF16), pltpu.SemaphoreType.DMA((STRIPS,))],
        compiler_params=limit(8),
        cost_estimate=pl.CostEstimate(
            flops=4 * NFW * focal * samples * width,
            bytes_accessed=2 * focal * samples * width + 4 * NFW * focal * width,
            transcendentals=0,
        ),
        name="first_analysis",
    )(forward, plus_start)


def fetch_panels(line, ahead, flip, panel_ref, held, sems):
    slots, _, _, rows = held.shape[:4]

    def copy(chunk, step):
        slot = lax.rem(chunk, slots)
        columns = pl.ds(chip_columns(line, ahead, flip, step), 2 * LANES)
        source = panel_ref.at[:, pl.ds(chunk * rows, rows), :, columns]
        return pltpu.make_async_copy(source, held.at[slot, step], sems.at[slot, step])

    def start(chunk):
        for step in range(line):
            copy(chunk, step).start()

    def wait(chunk):
        for step in range(line):
            copy(chunk, step).wait()

    for chunk in range(slots):
        start(chunk)
    return wait, start


def panel_scratch(line):
    rows = NFW // CHUNKS
    return [
        pltpu.VMEM((SLOTS, line, 2, rows, LANES, 2 * LANES), BF16),
        pltpu.SemaphoreType.DMA((SLOTS, line)),
    ]


def convolve_kernel(line, spec_ref, panel_ref, keep0, keep1, send0, send1, held, sems):
    core = own_place(line)[3]
    keep, send = (keep0, keep1), (send0, send1)
    focal = spec_ref.shape[2]
    rows = NFW // CHUNKS

    slots = held.shape[0]

    def copy(chunk):
        slot = lax.rem(chunk, slots)
        part = pl.ds(chunk * rows, rows)
        return pltpu.make_async_copy(panel_ref.at[:, part], held.at[slot], sems.at[slot])

    for chunk in range(slots):
        copy(chunk).start()

    def body(chunk, carry):
        copy(chunk).wait()
        slot = lax.rem(chunk, slots)
        for row in range(rows):
            w = chunk * rows + row
            real, imag = spec_ref[w, 0], spec_ref[w, 1]
            left = jnp.concatenate(
                [jnp.concatenate([real, -imag], axis=1), jnp.concatenate([imag, real], axis=1)], axis=0
            )
            for flip, step in relative(line):
                columns = pl.ds(chip_columns(line, True, flip, step), 2 * LANES)
                panel = held[slot, :, row, :, columns].reshape(2 * LANES, 2 * LANES)
                block = jnp.dot(left, panel, preferred_element_type=F32)
                mine, theirs = split_cores(core, block.astype(BF16))
                keep[flip][step, w] = mine.reshape(2, focal, LANES)
                send[flip][step, w] = theirs.reshape(2, focal, LANES)

        @pl.when(chunk + slots < CHUNKS)
        def _():
            copy(chunk + slots).start()

        return carry

    lax.fori_loop(0, CHUNKS, body, 0)


def panel_cost(focal, sources):
    return pl.CostEstimate(
        flops=8 * NFW * focal * LANES * sources,
        bytes_accessed=4 * NFW * sources * (LANES + focal),
        transcendentals=0,
    )


def convolve(spectrum, reflection, line):
    focal = spectrum.shape[2]
    out = jax.ShapeDtypeStruct((line, NFW, 2, focal, LANES), BF16)
    return pl.pallas_call(
        functools.partial(convolve_kernel, line),
        in_specs=[VMEM, FAR],
        out_specs=[VMEM] * 4,
        out_shape=[out] * 4,
        scratch_shapes=[
            pltpu.VMEM((SLOTS, 2, NFW // CHUNKS, LANES, reflection.shape[3]), BF16),
            pltpu.SemaphoreType.DMA((SLOTS,)),
        ],
        compiler_params=limit(20),
        cost_estimate=panel_cost(focal, reflection.shape[3]),
        name="convolve",
    )(spectrum, reflection)


def correlate_kernel(line, flip, has_base, final, *refs):
    core = own_place(line)[3]
    own, other, panel_ref = refs[:line], refs[line : 2 * line], refs[2 * line]
    base_ref = refs[2 * line + 1] if has_base else None
    out_ref, held, sems, *spare = refs[2 * line + 1 + has_base :]
    focal = own[0].shape[2]
    rows = held.shape[3]
    slots = held.shape[0]
    wait, start = fetch_panels(line, False, flip, panel_ref, held, sems)

    def body(chunk, carry):
        wait(chunk)
        slot = lax.rem(chunk, slots)
        for row in range(rows):
            w = chunk * rows + row
            panels, specs = [], []
            for step in range(line):
                panels.append(held[slot, step, :, row].reshape(2 * LANES, 2 * LANES))
                mine, theirs = own[step][w], other[step][w]
                specs.append(
                    join_cores(core, mine.reshape(2 * focal, LANES), theirs.reshape(2 * focal, LANES))
                )
            total = lax.dot_general(
                jnp.concatenate(specs, axis=1),
                jnp.concatenate(panels, axis=1),
                (((1,), (1,)), ((), ())),
                preferred_element_type=F32,
            )
            real = total[:focal, :LANES] + total[focal:, LANES:]
            imag = total[focal:, :LANES] - total[:focal, LANES:]
            if has_base:
                real += base_ref[w, 0]
                imag += base_ref[w, 1]
            if final:
                spare[0][pl.ds(2 * w * focal, focal), :] = real
                spare[0][pl.ds((2 * w + 1) * focal, focal), :] = imag
            else:
                out_ref[w, 0] = real
                out_ref[w, 1] = imag

        @pl.when(chunk + slots < CHUNKS)
        def _():
            start(chunk + slots)

        return carry

    lax.fori_loop(0, CHUNKS, body, 0)
    if final:
        for p in range(focal):
            out_ref[p] = spare[0][pl.ds(p, 2 * NFW, stride=focal), :].astype(BF16)


def correlate(own, other, reflection, line, flip, base=None, final=False):
    focal = own[0].shape[2]
    more = [] if base is None else [base]
    shape = jax.ShapeDtypeStruct((NFW, 2, focal, LANES), F32)
    if final:
        shape = jax.ShapeDtypeStruct((focal, 2 * NFW, LANES), BF16)
    spare = [pltpu.VMEM((2 * NFW * focal, LANES), F32)] if final else []
    return pl.pallas_call(
        functools.partial(correlate_kernel, line, flip, bool(more), final),
        in_specs=[VMEM] * (2 * line) + [FAR] + [VMEM] * len(more),
        out_specs=VMEM,
        out_shape=shape,
        scratch_shapes=panel_scratch(line) + spare,
        compiler_params=limit(24),
        cost_estimate=panel_cost(focal, reflection.shape[3] // 2),
        name=f"correlate{flip}",
    )(*own, *other, reflection, *more)


def windowed_spectrum(pair, onset, forward, inverse):
    time = SURE + lax.broadcasted_iota(jnp.int32, (NT - SURE, 2 * LANES), 0)
    spectra = jnp.concatenate(pair, axis=1)
    values = jnp.dot(inverse, spectra, preferred_element_type=F32)
    kept = jnp.where(time < jnp.concatenate(onset, axis=1), values, 0.0).astype(BF16)
    return jnp.dot(forward, jnp.concatenate([kept, spectra], axis=0), preferred_element_type=F32)


def window_kernel(parts, has_base, want_spec, *refs):
    refs = list(refs)
    forward_ref, inverse_ref, onset_ref = refs[:3]
    part_refs = refs[3 : 3 + parts]
    rest = refs[3 + parts :]
    base_ref = rest.pop(0) if has_base else None
    out_ref = rest.pop(0)
    held, result = rest
    focal = part_refs[0].shape[2]
    k = 2 * NFW
    total = part_refs[0][...].astype(F32)
    for ref in part_refs[1:]:
        total += ref[...].astype(F32)
    held[...] = total.reshape(k * focal, LANES)
    me = lax.axis_index("blk")
    columns = pl.ds(pl.multiple_of(me * LANES, LANES), LANES)
    if want_spec:
        for p in range(focal):
            out_ref[p] = held[pl.ds(p, k, stride=focal), :].astype(BF16)
        return
    for p in range(0, focal, 2):
        pair = [held[pl.ds(p + q, k, stride=focal), :].astype(BF16) for q in range(2)]
        onset = [onset_ref[p + q : p + q + 1, columns] for q in range(2)]
        spectrum = windowed_spectrum(pair, onset, forward_ref[...], inverse_ref[...])
        for q in range(2):
            result[pl.ds(p + q, k, stride=focal), :] = spectrum[:, q * LANES : (q + 1) * LANES]
    final = result[...].reshape(NFW, 2, focal, LANES)
    if base_ref is not None:
        final += base_ref[...].astype(F32)
    out_ref[...] = final.astype(BF16)


def window(parts, forward, inverse, onset_times, base=None, want_spec=False):
    focal = parts[0].shape[2]
    k = 2 * NFW
    operands = [forward, inverse, onset_times, *parts] + ([] if base is None else [base])
    out = jax.ShapeDtypeStruct((NFW, 2, focal, LANES), BF16)
    if want_spec:
        out = jax.ShapeDtypeStruct((focal, k, LANES), BF16)
    return pl.pallas_call(
        functools.partial(window_kernel, len(parts), base is not None, want_spec),
        in_specs=[VMEM] * len(operands),
        out_specs=VMEM,
        out_shape=out,
        scratch_shapes=[pltpu.VMEM((k * focal, LANES), F32)] * 2,
        compiler_params=limit(8),
        cost_estimate=pl.CostEstimate(
            flops=4 * k * NT * focal * LANES, bytes_accessed=2 * k * focal * LANES * 6, transcendentals=0
        ),
        name="window",
    )(*operands)


def window_at_kernel(line, flip, step, begun, *refs):
    forward_ref, inverse_ref, onset_ref, chip_inverse_ref, spec_ref = refs[:5]
    out_ref, keep_ref, send_ref, result, made, sems = refs[5 + 2 * begun :]
    core = own_place(line)[3]
    focal, k, _ = spec_ref.shape
    start = chip_columns(line, False, flip, step) + core * LANES
    columns = pl.ds(pl.multiple_of(start, LANES), LANES)
    samples = made.shape[2]
    chip = lax.axis_index("blk") // 2
    chip_inverse = chip_inverse_ref[chip]
    first = chip * (2 * samples)
    time = first + lax.broadcasted_iota(jnp.int32, (2 * samples, 2 * LANES), 0)

    def pair_of(p):
        onset = [onset_ref[p + q : p + q + 1, columns] for q in range(2)]
        return [spec_ref[p + q] for q in range(2)], onset

    for p in range(0, focal, 2):
        pair, onset = pair_of(p)
        values = jnp.dot(chip_inverse, jnp.concatenate(pair, axis=1), preferred_element_type=F32)
        values = jnp.where(time < jnp.concatenate(onset, axis=1), values, 0.0).astype(BF16)
        low, high = values[:samples], values[samples:]
        mine, theirs = jnp.where(core == 0, low, high), jnp.where(core == 0, high, low)
        for q in range(2):
            part = slice(q * LANES, (q + 1) * LANES)
            made[0, p + q] = mine[:, part]
            made[1, p + q] = theirs[:, part]
    place = pl.ds((flip * line + step) * LANES, LANES)
    copies = [
        pltpu.make_async_copy(made.at[side], target.at[:, :, place], sems.at[side])
        for side, target in enumerate((keep_ref, send_ref))
    ]
    for copy in copies:
        copy.start()
    for p in range(0, focal, 2):
        pair, onset = pair_of(p)
        spectrum = windowed_spectrum(pair, onset, forward_ref[...], inverse_ref[...])
        for q in range(2):
            result[pl.ds(p + q, k, stride=focal), :] = spectrum[:, q * LANES : (q + 1) * LANES]
    out_ref[...] = result[...].reshape(NFW, 2, focal, LANES).astype(BF16)
    for copy in copies:
        copy.wait()


def window_at(spec, forward, inverse, onset_times, chip_inverse, line, flip, step, fields):
    focal, k, _ = spec.shape
    samples = chip_inverse.shape[1] // 2
    field_shape = jax.ShapeDtypeStruct((focal, samples, 2 * line * LANES), BF16)
    begun = bool(fields)
    return pl.pallas_call(
        functools.partial(window_at_kernel, line, flip, step, begun),
        in_specs=[VMEM] * 5 + [FAR] * len(fields),
        out_specs=[VMEM, FAR, FAR],
        out_shape=[jax.ShapeDtypeStruct((NFW, 2, focal, LANES), BF16), field_shape, field_shape],
        input_output_aliases={5: 1, 6: 2} if begun else {},
        scratch_shapes=[
            pltpu.VMEM((k * focal, LANES), F32),
            pltpu.VMEM((2, focal, samples, LANES), BF16),
            pltpu.SemaphoreType.DMA((2,)),
        ],
        compiler_params=limit(8),
        cost_estimate=pl.CostEstimate(
            flops=4 * k * NT * focal * LANES, bytes_accessed=2 * k * focal * LANES * 6, transcendentals=0
        ),
        name="window_at",
    )(forward, inverse, onset_times, chip_inverse, spec, *fields)


def merge_kernel(line, mine, theirs, out_ref, made, sems):
    core = own_place(line)[3]
    copy, rows = strip_copies(made, out_ref, sems, STRIPS)

    def body(strip, carry):
        for row in range(rows):
            p = strip * rows + row
            for at, (flip, step) in enumerate(relative(line)):
                columns = pl.ds(chip_columns(line, False, flip, step), 2 * LANES)
                part = pl.ds(at * LANES, LANES)
                made[p, :, columns] = join_cores(core, mine[p, :, part], theirs[p, :, part])
        copy(strip).start()
        return carry

    lax.fori_loop(0, STRIPS, body, 0)
    for strip in range(STRIPS):
        copy(strip).wait()


def merge(mine, theirs, line):
    focal, samples, width = mine.shape
    shape = (focal, samples, 2 * width)
    return pl.pallas_call(
        functools.partial(merge_kernel, line),
        in_specs=[VMEM] * 2,
        out_specs=FAR,
        out_shape=jax.ShapeDtypeStruct(shape, BF16),
        scratch_shapes=[pltpu.VMEM(shape, BF16), pltpu.SemaphoreType.DMA((STRIPS,))],
        compiler_params=limit(6),
        cost_estimate=pl.CostEstimate(flops=0, bytes_accessed=8 * mine.size, transcendentals=0),
        name="merge",
    )(mine, theirs)


def field_kernel(line, has_plus, inverse_ref, onset_ref, *refs):
    core = own_place(line)[3]
    places = relative(line)
    own, other = refs[: len(places)], refs[len(places) : 2 * len(places)]
    rest = list(refs[2 * len(places) :])
    plus_ref = rest.pop(0) if has_plus else None
    out_ref, made, out_sems, *spare = rest
    samples = out_ref.shape[1]
    inverse = inverse_ref[own_place(line)[0]]
    out_copy, rows = strip_copies(made, out_ref, out_sems, STRIPS)
    if has_plus:
        plus, plus_sems = spare
        plus_copy, _ = strip_copies(plus_ref, plus, plus_sems, STRIPS)
        for strip in range(STRIPS):
            plus_copy(strip).start()
    time = lax.axis_index("blk") * samples + lax.broadcasted_iota(jnp.int32, (samples, 2 * LANES), 0)

    def body(strip, carry):
        if has_plus:
            plus_copy(strip).wait()
        for row in range(rows):
            p = strip * rows + row
            for at, (flip, step) in enumerate(places):
                columns = pl.ds(chip_columns(line, False, flip, step), 2 * LANES)
                spec = join_cores(core, own[at][p], other[at][p])
                values = jnp.dot(inverse, spec, preferred_element_type=F32)
                values = jnp.where(time < onset_ref[pl.ds(p, 1), columns], values, 0.0)
                if has_plus:
                    values += plus[p, :, columns].astype(F32)
                made[p, :, columns] = values.astype(BF16)
        out_copy(strip).start()
        return carry

    lax.fori_loop(0, STRIPS, body, 0)
    for strip in range(STRIPS):
        out_copy(strip).wait()


def field(own, other, inverse, onset_times, line, plus_start=None):
    own, other = sum(own, []), sum(other, [])
    focal, k, _ = own[0].shape
    samples = inverse.shape[1]
    shape = (focal, samples, onset_times.shape[1])
    plus = [] if plus_start is None else [plus_start]
    moved = [pltpu.VMEM(shape, BF16), pltpu.SemaphoreType.DMA((STRIPS,))]
    return pl.pallas_call(
        functools.partial(field_kernel, line, bool(plus)),
        in_specs=[VMEM] * (2 + len(own) + len(other)) + [FAR] * len(plus),
        out_specs=FAR,
        out_shape=jax.ShapeDtypeStruct(shape, BF16),
        scratch_shapes=moved * (1 + len(plus)),
        compiler_params=limit(12),
        cost_estimate=pl.CostEstimate(
            flops=2 * k * math.prod(shape),
            bytes_accessed=4 * math.prod(shape) + 2 * k * focal * shape[2],
            transcendentals=0,
        ),
        name="field",
    )(inverse, onset_times, *own, *other, *plus)


def add(*parts):
    total = parts[0].astype(F32)
    for part in parts[1:]:
        total += part.astype(F32)
    return total


def after(value, *others):
    return lax.optimization_barrier((value, *others))[0] if others else value


def reduce_scatter(places, keep0, keep1, send0, send1):
    size = places.line
    got1 = places.send(send1, places.core())
    got0 = places.send(send0, places.core())
    far = [add(keep, got).astype(BF16) for keep, got in zip(keep1, got1)]
    across = {step: places.send(far[step], places.pair()) for step in range(2, size)}
    beside = [places.send(far[1], places.shift(1))] if size > 1 else []
    parts = [keep0[0], got0[0]]

    def pass_on(steps, shift, *first):
        carried, sent = [], []
        for step in steps:
            crossed = [after(across[step], *first)] if step in across else []
            carried = [places.send(add(keep0[step], got0[step], *crossed, *carried).astype(BF16), places.shift(shift))]
            sent += carried
        return sent

    ahead = pass_on(range(size // 2, 0, -1), 1)
    behind = pass_on(range(size // 2 + 1, size), size - 1, *ahead[:1])
    parts += ahead[-1:] + behind[-1:]
    across[0] = places.send(add(keep1[0], got1[0], *beside).astype(BF16), places.pair())
    return parts + [across[0]]


def gather_chips(places, block, work=None, together=False):
    size = places.line
    near = [1, size - 1] if size > 2 else [1] if size > 1 else []
    far = list(range(2, size - 1))
    made = {}

    def run(flip, steps, pieces, *others):
        if work is None:
            return []
        for step in steps:
            made[flip, step] = work(after(pieces[step], *others), flip, step)
        return [made[flip, step] for step in steps]

    line = {0: block}
    for step in near:
        line[step] = places.send(block, places.shift(step))
    across = {0: places.send(block, places.pair())}
    own = run(0, [0], line)
    for step in range(2, size // 2 + 1):
        line[step] = places.send(after(line[step - 1], across[0], *own), places.shift(1))
    for step in range(size - 2, size // 2, -1):
        line[step] = places.send(after(line[step + 1], *own), places.shift(size - 1))
    for step in near:
        if step == 1:
            across[step] = places.send(after(across[0], line[size - 1]), places.shift(1))
        else:
            across[step] = places.send(line[step], places.pair())
    middle = [across[step] for step in near] if together else run(1, [0], across) + run(0, near, line)
    for step in far:
        across[step] = places.send(after(line[step], *middle), places.pair())
    late = run(0, far, line) + run(1, near, across)
    run(1, far, across, *late)
    pieces = [[side[step] for step in range(size)] for side in (line, across)]
    results = [[made[flip, step] for step in range(size)] for flip in range(2)] if work else None
    return pieces, results


def swap_cores(places, pieces):
    return [places.send(piece, places.core()) for piece in pieces]


def local(plus_start, reflection, onset_times):
    size = lax.axis_size("blk")
    places = Places("blk", size)
    line = places.line
    focal, samples, _ = plus_start.shape
    forward, inverse = constant_tables()
    own_forward = np.ascontiguousarray(forward.reshape(2 * NFW, size, samples).transpose(1, 0, 2))
    own_inverse = inverse.reshape(size, samples, 2 * NFW)
    chip_inverse = inverse.reshape(size // 2, 2 * samples, 2 * NFW)
    sure = forward[:, :SURE].astype(np.float32) @ inverse[:SURE].astype(np.float32)
    forward = jnp.asarray(np.concatenate([forward[:, SURE:], sure.astype(BF16)], axis=1))
    inverse = jnp.asarray(inverse[SURE:])
    own_forward, own_inverse, chip_inverse = map(jnp.asarray, (own_forward, own_inverse, chip_inverse))

    fields = []

    def window_piece(piece, flip, step):
        spectrum, *fields[:] = window_at(
            piece, forward, inverse, onset_times, chip_inverse, line, flip, step, tuple(fields)
        )
        return spectrum

    parts = reduce_scatter(places, *first_analysis(plus_start, own_forward, line))
    start = add(*parts).astype(BF16)
    start = jnp.transpose(start, (1, 0, 2)).reshape(NFW, 2, focal, LANES)
    spectrum_plus = start
    for iteration in range(ITERS):
        last = iteration + 1 == ITERS
        parts = reduce_scatter(places, *convolve(spectrum_plus, reflection, line))
        windowed = window(parts, forward, inverse, onset_times, want_spec=last)
        if last:
            _, own = gather_chips(places, windowed, window_piece)
        else:
            own, _ = gather_chips(places, windowed)
        half = correlate(own[0], swap_cores(places, own[0]), reflection, line, 0)
        across = [own[1][step] if step == 0 else after(own[1][step], half) for step in range(line)]
        downgoing_spec = correlate(own[1], swap_cores(places, across), reflection, line, 1, half, last)
        if not last:
            spectrum_plus = window([downgoing_spec], forward, inverse, onset_times, base=start)
    mine, theirs = fields
    theirs = places.send(after(theirs, downgoing_spec), places.core())
    own, _ = gather_chips(places, downgoing_spec, together=True)
    upgoing = merge(mine, theirs, line)
    other = [swap_cores(places, own[0])]
    across = [own[1][step] if step in (0, 1, line - 1) else after(own[1][step], upgoing) for step in range(line)]
    other.append(swap_cores(places, across))
    downgoing = field(own, other, own_inverse, onset_times, line, plus_start)
    return upgoing, downgoing


def analyze(values, forward):
    total = jnp.einsum("kt,ptx->kpx", forward, values, preferred_element_type=F32)
    return total.reshape(NFW, 2, values.shape[0], values.shape[2])


def synthesize(spectrum, inverse):
    flat = spectrum.reshape(2 * NFW, spectrum.shape[2], spectrum.shape[3])
    return jnp.einsum("tk,kpx->ptx", inverse, flat, preferred_element_type=F32)


def contract(form, left, right):
    return jnp.einsum(form, left, right, preferred_element_type=F32)


def local_any(plus_start, reflection, onset_times):
    samples = plus_start.shape[1]
    width = reflection.shape[2]
    me = lax.axis_index("blk")
    forward, inverse = tables_of(jnp.arange(NT, dtype=jnp.int32))
    own_forward, own_inverse = tables_of(me * samples + jnp.arange(samples, dtype=jnp.int32))
    onset = lax.dynamic_slice_in_dim(onset_times, me * width, width, 1)
    keep = jnp.arange(NT, dtype=jnp.int32)[None, :, None] < onset[:, None, :]
    time = me * samples + jnp.arange(samples, dtype=jnp.int32)
    own_keep = time[None, :, None] < onset_times[:, None, :]

    def scatter(partial):
        return lax.psum_scatter(partial.astype(BF16), "blk", scatter_dimension=3, tiled=True).astype(BF16)

    def gather(block):
        return lax.all_gather(block, "blk", axis=3, tiled=True)

    start = scatter(analyze(plus_start, own_forward))
    spectrum = start
    for iteration in range(ITERS):
        real = contract("wrs,wpr->wps", reflection[0], spectrum[:, 0]) - contract(
            "wrs,wpr->wps", reflection[1], spectrum[:, 1]
        )
        imag = contract("wrs,wpr->wps", reflection[0], spectrum[:, 1]) + contract(
            "wrs,wpr->wps", reflection[1], spectrum[:, 0]
        )
        upgoing_spec = scatter(jnp.stack([real, imag], axis=1))
        kept = jnp.where(keep, synthesize(upgoing_spec, inverse), 0.0).astype(BF16)
        minus = gather(analyze(kept, forward).astype(BF16))
        real = contract("wrs,wps->wpr", reflection[0], minus[:, 0]) + contract(
            "wrs,wps->wpr", reflection[1], minus[:, 1]
        )
        imag = contract("wrs,wps->wpr", reflection[0], minus[:, 1]) - contract(
            "wrs,wps->wpr", reflection[1], minus[:, 0]
        )
        downgoing_spec = jnp.stack([real, imag], axis=1).astype(BF16)
        if iteration + 1 < ITERS:
            kept = jnp.where(keep, synthesize(downgoing_spec, inverse), 0.0).astype(BF16)
            spectrum = (start.astype(F32) + analyze(kept, forward)).astype(BF16)
    upgoing = jnp.where(own_keep, synthesize(gather(upgoing_spec), own_inverse), 0.0).astype(BF16)
    change = jnp.where(own_keep, synthesize(gather(downgoing_spec), own_inverse), 0.0)
    return upgoing, (plus_start.astype(F32) + change).astype(BF16)


def solution(mesh):
    size = mesh.shape["blk"]

    def run(plus_start, reflection, onset_times):
        width = reflection.shape[2] // size
        fits = width == LANES and size % 4 == 0 and (plus_start.shape[1] // size) % 16 == 0
        return jax.shard_map(
            local if fits else local_any,
            mesh=mesh,
            in_specs=(P("groups", "blk", None), P(None, None, "blk", None), P("groups", None)),
            out_specs=(P("groups", "blk", None), P("groups", "blk", None)),
            check_vma=False,
        )(plus_start, reflection, onset_times)

    return run
```

```python
import functools
import math

import jax
import jax.numpy as jnp
import numpy as np
from jax import lax
from jax.experimental import pallas as pl
from jax.experimental.pallas import tpu as pltpu
from jax.sharding import PartitionSpec as P

NT = 512
NFW = 32
FREQ0 = 16
ITERS = 2
SURE = 128
LANES = 128
F32 = jnp.float32
BF16 = jnp.bfloat16


def basis_of(samples):
    freqs = FREQ0 + jnp.arange(NFW, dtype=jnp.int32)
    turns = freqs[:, None] * samples[None, :] % NT
    phase = turns.astype(F32) * (2.0 * math.pi / NT)
    return jnp.stack([jnp.cos(phase), -jnp.sin(phase)], axis=1)


def tables_of(samples):
    basis = basis_of(samples).reshape(2 * NFW, samples.shape[0])
    forward = (basis * (1.0 / math.sqrt(NT))).astype(BF16)
    inverse = (basis * math.sqrt(2.0 / NFW)).astype(BF16)
    return forward, inverse.T


def constant_tables():
    freqs = FREQ0 + np.arange(NFW, dtype=np.int32)
    turns = freqs[:, None] * np.arange(NT, dtype=np.int32)[None, :] % NT
    phase = turns.astype(np.float32) * np.float32(2.0 * math.pi / NT)
    basis = np.stack([np.cos(phase), -np.sin(phase)], axis=1).reshape(2 * NFW, NT)
    forward = (basis * np.float32(1.0 / math.sqrt(NT))).astype(BF16)
    inverse = (basis * np.float32(math.sqrt(2.0 / NFW))).astype(BF16)
    return forward, np.ascontiguousarray(inverse.T)


class Places:
    def __init__(self, axis, size):
        self.axis = axis
        self.size = size
        self.line = size // 4

    def core(self):
        return [(b, b ^ 1) for b in range(self.size)]

    def pair(self):
        return [(b, b ^ 2) for b in range(self.size)]

    def shift(self, step):
        return [(b, (b // 4 + step) % self.line * 4 + b % 4) for b in range(self.size)]

    def send(self, array, pairs):
        return lax.ppermute(array, self.axis, pairs)


def own_place(line):
    me = lax.axis_index("blk")
    return me, me // 4, (me // 2) % 2, me % 2


def chip_columns(line, ahead, flip, step):
    _, l, m, _ = own_place(line)
    other = lax.rem(l + step, line) if ahead else lax.rem(l - step + line, line)
    chip = other * 2 + (lax.rem(m + flip, 2))
    return pl.multiple_of(chip * (2 * LANES), 2 * LANES)


def relative(line):
    return [(flip, step) for flip in range(2) for step in range(line)]


def split_cores(core, block):
    low, high = block[:, :LANES], block[:, LANES:]
    first = core == 0
    return jnp.where(first, low, high), jnp.where(first, high, low)


def join_cores(core, own, other):
    first = core == 0
    return jnp.concatenate([jnp.where(first, own, other), jnp.where(first, other, own)], axis=1)


VMEM = pl.BlockSpec(memory_space=pltpu.VMEM)
FAR = pl.BlockSpec(memory_space=pltpu.HBM)
CHUNKS = 8
STRIPS = 4
SLOTS = 4


def limit(mebibytes):
    return pltpu.CompilerParams(vmem_limit_bytes=mebibytes << 20)


def strip_copies(source, target, sems, strips):
    rows = source.shape[0] // strips

    def copy(strip):
        part = pl.ds(strip * rows, rows)
        return pltpu.make_async_copy(source.at[part], target.at[part], sems.at[strip])

    return copy, rows


def analysis_kernel(line, forward_ref, plus_ref, keep0, keep1, send0, send1, held, sems):
    core = own_place(line)[3]
    keep, send = (keep0, keep1), (send0, send1)
    forward = forward_ref[own_place(line)[0]]
    copy, rows = strip_copies(plus_ref, held, sems, STRIPS)
    for strip in range(STRIPS):
        copy(strip).start()

    def body(strip, carry):
        copy(strip).wait()
        for row in range(rows):
            p = strip * rows + row
            for flip, step in relative(line):
                columns = pl.ds(chip_columns(line, True, flip, step), 2 * LANES)
                block = jnp.dot(forward, held[p, :, columns], preferred_element_type=F32)
                mine, theirs = split_cores(core, block.astype(BF16))
                keep[flip][step, p] = mine
                send[flip][step, p] = theirs
        return carry

    lax.fori_loop(0, STRIPS, body, 0)


def first_analysis(plus_start, forward, line):
    focal, samples, width = plus_start.shape
    out = jax.ShapeDtypeStruct((line, focal, 2 * NFW, LANES), BF16)
    return pl.pallas_call(
        functools.partial(analysis_kernel, line),
        in_specs=[VMEM, FAR],
        out_specs=[VMEM] * 4,
        out_shape=[out] * 4,
        scratch_shapes=[pltpu.VMEM(plus_start.shape, BF16), pltpu.SemaphoreType.DMA((STRIPS,))],
        compiler_params=limit(8),
        cost_estimate=pl.CostEstimate(
            flops=4 * NFW * focal * samples * width,
            bytes_accessed=2 * focal * samples * width + 4 * NFW * focal * width,
            transcendentals=0,
        ),
        name="first_analysis",
    )(forward, plus_start)


def fetch_panels(line, ahead, flip, panel_ref, held, sems):
    slots, _, _, rows = held.shape[:4]

    def copy(chunk, step):
        slot = lax.rem(chunk, slots)
        columns = pl.ds(chip_columns(line, ahead, flip, step), 2 * LANES)
        source = panel_ref.at[:, pl.ds(chunk * rows, rows), :, columns]
        return pltpu.make_async_copy(source, held.at[slot, step], sems.at[slot, step])

    def start(chunk):
        for step in range(line):
            copy(chunk, step).start()

    def wait(chunk):
        for step in range(line):
            copy(chunk, step).wait()

    for chunk in range(slots):
        start(chunk)
    return wait, start


def panel_scratch(line):
    rows = NFW // CHUNKS
    return [
        pltpu.VMEM((SLOTS, line, 2, rows, LANES, 2 * LANES), BF16),
        pltpu.SemaphoreType.DMA((SLOTS, line)),
    ]


def convolve_kernel(line, spec_ref, panel_ref, keep0, keep1, send0, send1, held, sems):
    core = own_place(line)[3]
    keep, send = (keep0, keep1), (send0, send1)
    focal = spec_ref.shape[2]
    rows = NFW // CHUNKS

    slots = held.shape[0]

    def copy(chunk):
        slot = lax.rem(chunk, slots)
        part = pl.ds(chunk * rows, rows)
        return pltpu.make_async_copy(panel_ref.at[:, part], held.at[slot], sems.at[slot])

    for chunk in range(slots):
        copy(chunk).start()

    def body(chunk, carry):
        copy(chunk).wait()
        slot = lax.rem(chunk, slots)
        for row in range(rows):
            w = chunk * rows + row
            real, imag = spec_ref[w, 0], spec_ref[w, 1]
            left = jnp.concatenate(
                [jnp.concatenate([real, -imag], axis=1), jnp.concatenate([imag, real], axis=1)], axis=0
            )
            for flip, step in relative(line):
                columns = pl.ds(chip_columns(line, True, flip, step), 2 * LANES)
                panel = held[slot, :, row, :, columns].reshape(2 * LANES, 2 * LANES)
                block = jnp.dot(left, panel, preferred_element_type=F32)
                mine, theirs = split_cores(core, block.astype(BF16))
                keep[flip][step, w] = mine.reshape(2, focal, LANES)
                send[flip][step, w] = theirs.reshape(2, focal, LANES)

        @pl.when(chunk + slots < CHUNKS)
        def _():
            copy(chunk + slots).start()

        return carry

    lax.fori_loop(0, CHUNKS, body, 0)


def panel_cost(focal, sources):
    return pl.CostEstimate(
        flops=8 * NFW * focal * LANES * sources,
        bytes_accessed=4 * NFW * sources * (LANES + focal),
        transcendentals=0,
    )


def convolve(spectrum, reflection, line):
    focal = spectrum.shape[2]
    out = jax.ShapeDtypeStruct((line, NFW, 2, focal, LANES), BF16)
    return pl.pallas_call(
        functools.partial(convolve_kernel, line),
        in_specs=[VMEM, FAR],
        out_specs=[VMEM] * 4,
        out_shape=[out] * 4,
        scratch_shapes=[
            pltpu.VMEM((SLOTS, 2, NFW // CHUNKS, LANES, reflection.shape[3]), BF16),
            pltpu.SemaphoreType.DMA((SLOTS,)),
        ],
        compiler_params=limit(20),
        cost_estimate=panel_cost(focal, reflection.shape[3]),
        name="convolve",
    )(spectrum, reflection)


def correlate_kernel(line, flip, has_base, final, *refs):
    core = own_place(line)[3]
    own, other, panel_ref = refs[:line], refs[line : 2 * line], refs[2 * line]
    base_ref = refs[2 * line + 1] if has_base else None
    out_ref, held, sems, *spare = refs[2 * line + 1 + has_base :]
    focal = own[0].shape[2]
    rows = held.shape[3]
    slots = held.shape[0]
    wait, start = fetch_panels(line, False, flip, panel_ref, held, sems)

    def body(chunk, carry):
        wait(chunk)
        slot = lax.rem(chunk, slots)
        for row in range(rows):
            w = chunk * rows + row
            panels, specs = [], []
            for step in range(line):
                panels.append(held[slot, step, :, row].reshape(2 * LANES, 2 * LANES))
                mine, theirs = own[step][w], other[step][w]
                specs.append(
                    join_cores(core, mine.reshape(2 * focal, LANES), theirs.reshape(2 * focal, LANES))
                )
            total = lax.dot_general(
                jnp.concatenate(specs, axis=1),
                jnp.concatenate(panels, axis=1),
                (((1,), (1,)), ((), ())),
                preferred_element_type=F32,
            )
            real = total[:focal, :LANES] + total[focal:, LANES:]
            imag = total[focal:, :LANES] - total[:focal, LANES:]
            if has_base:
                real += base_ref[w, 0]
                imag += base_ref[w, 1]
            if final:
                spare[0][pl.ds(2 * w * focal, focal), :] = real
                spare[0][pl.ds((2 * w + 1) * focal, focal), :] = imag
            else:
                out_ref[w, 0] = real
                out_ref[w, 1] = imag

        @pl.when(chunk + slots < CHUNKS)
        def _():
            start(chunk + slots)

        return carry

    lax.fori_loop(0, CHUNKS, body, 0)
    if final:
        for p in range(focal):
            out_ref[p] = spare[0][pl.ds(p, 2 * NFW, stride=focal), :].astype(BF16)


def correlate(own, other, reflection, line, flip, base=None, final=False):
    focal = own[0].shape[2]
    more = [] if base is None else [base]
    shape = jax.ShapeDtypeStruct((NFW, 2, focal, LANES), F32)
    if final:
        shape = jax.ShapeDtypeStruct((focal, 2 * NFW, LANES), BF16)
    spare = [pltpu.VMEM((2 * NFW * focal, LANES), F32)] if final else []
    return pl.pallas_call(
        functools.partial(correlate_kernel, line, flip, bool(more), final),
        in_specs=[VMEM] * (2 * line) + [FAR] + [VMEM] * len(more),
        out_specs=VMEM,
        out_shape=shape,
        scratch_shapes=panel_scratch(line) + spare,
        compiler_params=limit(24),
        cost_estimate=panel_cost(focal, reflection.shape[3] // 2),
        name=f"correlate{flip}",
    )(*own, *other, reflection, *more)


def windowed_spectrum(pair, onset, forward, inverse):
    time = SURE + lax.broadcasted_iota(jnp.int32, (NT - SURE, 2 * LANES), 0)
    spectra = jnp.concatenate(pair, axis=1)
    values = jnp.dot(inverse, spectra, preferred_element_type=F32)
    kept = jnp.where(time < jnp.concatenate(onset, axis=1), values, 0.0).astype(BF16)
    return jnp.dot(forward, jnp.concatenate([kept, spectra], axis=0), preferred_element_type=F32)


def window_kernel(parts, has_base, want_spec, *refs):
    refs = list(refs)
    forward_ref, inverse_ref, onset_ref = refs[:3]
    part_refs = refs[3 : 3 + parts]
    rest = refs[3 + parts :]
    base_ref = rest.pop(0) if has_base else None
    out_ref = rest.pop(0)
    held, result = rest
    focal = part_refs[0].shape[2]
    k = 2 * NFW
    total = part_refs[0][...].astype(F32)
    for ref in part_refs[1:]:
        total += ref[...].astype(F32)
    held[...] = total.reshape(k * focal, LANES)
    me = lax.axis_index("blk")
    columns = pl.ds(pl.multiple_of(me * LANES, LANES), LANES)
    if want_spec:
        for p in range(focal):
            out_ref[p] = held[pl.ds(p, k, stride=focal), :].astype(BF16)
        return
    for p in range(0, focal, 2):
        pair = [held[pl.ds(p + q, k, stride=focal), :].astype(BF16) for q in range(2)]
        onset = [onset_ref[p + q : p + q + 1, columns] for q in range(2)]
        spectrum = windowed_spectrum(pair, onset, forward_ref[...], inverse_ref[...])
        for q in range(2):
            result[pl.ds(p + q, k, stride=focal), :] = spectrum[:, q * LANES : (q + 1) * LANES]
    final = result[...].reshape(NFW, 2, focal, LANES)
    if base_ref is not None:
        final += base_ref[...].astype(F32)
    out_ref[...] = final.astype(BF16)


def window(parts, forward, inverse, onset_times, base=None, want_spec=False):
    focal = parts[0].shape[2]
    k = 2 * NFW
    operands = [forward, inverse, onset_times, *parts] + ([] if base is None else [base])
    out = jax.ShapeDtypeStruct((NFW, 2, focal, LANES), BF16)
    if want_spec:
        out = jax.ShapeDtypeStruct((focal, k, LANES), BF16)
    return pl.pallas_call(
        functools.partial(window_kernel, len(parts), base is not None, want_spec),
        in_specs=[VMEM] * len(operands),
        out_specs=VMEM,
        out_shape=out,
        scratch_shapes=[pltpu.VMEM((k * focal, LANES), F32)] * 2,
        compiler_params=limit(8),
        cost_estimate=pl.CostEstimate(
            flops=4 * k * NT * focal * LANES, bytes_accessed=2 * k * focal * LANES * 6, transcendentals=0
        ),
        name="window",
    )(*operands)


def window_at_kernel(line, flip, step, begun, *refs):
    forward_ref, inverse_ref, onset_ref, chip_inverse_ref, spec_ref = refs[:5]
    out_ref, keep_ref, send_ref, result, made, sems = refs[5 + 2 * begun :]
    core = own_place(line)[3]
    focal, k, _ = spec_ref.shape
    start = chip_columns(line, False, flip, step) + core * LANES
    columns = pl.ds(pl.multiple_of(start, LANES), LANES)
    samples = made.shape[2]
    chip = lax.axis_index("blk") // 2
    chip_inverse = chip_inverse_ref[chip]
    first = chip * (2 * samples)
    time = first + lax.broadcasted_iota(jnp.int32, (2 * samples, 2 * LANES), 0)

    def pair_of(p):
        onset = [onset_ref[p + q : p + q + 1, columns] for q in range(2)]
        return [spec_ref[p + q] for q in range(2)], onset

    for p in range(0, focal, 2):
        pair, onset = pair_of(p)
        values = jnp.dot(chip_inverse, jnp.concatenate(pair, axis=1), preferred_element_type=F32)
        values = jnp.where(time < jnp.concatenate(onset, axis=1), values, 0.0).astype(BF16)
        low, high = values[:samples], values[samples:]
        mine, theirs = jnp.where(core == 0, low, high), jnp.where(core == 0, high, low)
        for q in range(2):
            part = slice(q * LANES, (q + 1) * LANES)
            made[0, p + q] = mine[:, part]
            made[1, p + q] = theirs[:, part]
    place = pl.ds((flip * line + step) * LANES, LANES)
    copies = [
        pltpu.make_async_copy(made.at[side], target.at[:, :, place], sems.at[side])
        for side, target in enumerate((keep_ref, send_ref))
    ]
    for copy in copies:
        copy.start()
    for p in range(0, focal, 2):
        pair, onset = pair_of(p)
        spectrum = windowed_spectrum(pair, onset, forward_ref[...], inverse_ref[...])
        for q in range(2):
            result[pl.ds(p + q, k, stride=focal), :] = spectrum[:, q * LANES : (q + 1) * LANES]
    out_ref[...] = result[...].reshape(NFW, 2, focal, LANES).astype(BF16)
    for copy in copies:
        copy.wait()


def window_at(spec, forward, inverse, onset_times, chip_inverse, line, flip, step, fields):
    focal, k, _ = spec.shape
    samples = chip_inverse.shape[1] // 2
    field_shape = jax.ShapeDtypeStruct((focal, samples, 2 * line * LANES), BF16)
    begun = bool(fields)
    return pl.pallas_call(
        functools.partial(window_at_kernel, line, flip, step, begun),
        in_specs=[VMEM] * 5 + [FAR] * len(fields),
        out_specs=[VMEM, FAR, FAR],
        out_shape=[jax.ShapeDtypeStruct((NFW, 2, focal, LANES), BF16), field_shape, field_shape],
        input_output_aliases={5: 1, 6: 2} if begun else {},
        scratch_shapes=[
            pltpu.VMEM((k * focal, LANES), F32),
            pltpu.VMEM((2, focal, samples, LANES), BF16),
            pltpu.SemaphoreType.DMA((2,)),
        ],
        compiler_params=limit(8),
        cost_estimate=pl.CostEstimate(
            flops=4 * k * NT * focal * LANES, bytes_accessed=2 * k * focal * LANES * 6, transcendentals=0
        ),
        name="window_at",
    )(forward, inverse, onset_times, chip_inverse, spec, *fields)


def merge_kernel(line, mine, theirs, out_ref, made, sems):
    core = own_place(line)[3]
    copy, rows = strip_copies(made, out_ref, sems, STRIPS)

    def body(strip, carry):
        for row in range(rows):
            p = strip * rows + row
            for at, (flip, step) in enumerate(relative(line)):
                columns = pl.ds(chip_columns(line, False, flip, step), 2 * LANES)
                part = pl.ds(at * LANES, LANES)
                made[p, :, columns] = join_cores(core, mine[p, :, part], theirs[p, :, part])
        copy(strip).start()
        return carry

    lax.fori_loop(0, STRIPS, body, 0)
    for strip in range(STRIPS):
        copy(strip).wait()


def merge(mine, theirs, line):
    focal, samples, width = mine.shape
    shape = (focal, samples, 2 * width)
    return pl.pallas_call(
        functools.partial(merge_kernel, line),
        in_specs=[VMEM] * 2,
        out_specs=FAR,
        out_shape=jax.ShapeDtypeStruct(shape, BF16),
        scratch_shapes=[pltpu.VMEM(shape, BF16), pltpu.SemaphoreType.DMA((STRIPS,))],
        compiler_params=limit(6),
        cost_estimate=pl.CostEstimate(flops=0, bytes_accessed=8 * mine.size, transcendentals=0),
        name="merge",
    )(mine, theirs)


def field_kernel(line, has_plus, inverse_ref, onset_ref, *refs):
    core = own_place(line)[3]
    places = relative(line)
    own, other = refs[: len(places)], refs[len(places) : 2 * len(places)]
    rest = list(refs[2 * len(places) :])
    plus_ref = rest.pop(0) if has_plus else None
    out_ref, made, out_sems, *spare = rest
    samples = out_ref.shape[1]
    inverse = inverse_ref[own_place(line)[0]]
    out_copy, rows = strip_copies(made, out_ref, out_sems, STRIPS)
    if has_plus:
        plus, plus_sems = spare
        plus_copy, _ = strip_copies(plus_ref, plus, plus_sems, STRIPS)
        for strip in range(STRIPS):
            plus_copy(strip).start()
    time = lax.axis_index("blk") * samples + lax.broadcasted_iota(jnp.int32, (samples, 2 * LANES), 0)

    def body(strip, carry):
        if has_plus:
            plus_copy(strip).wait()
        for row in range(rows):
            p = strip * rows + row
            for at, (flip, step) in enumerate(places):
                columns = pl.ds(chip_columns(line, False, flip, step), 2 * LANES)
                spec = join_cores(core, own[at][p], other[at][p])
                values = jnp.dot(inverse, spec, preferred_element_type=F32)
                values = jnp.where(time < onset_ref[pl.ds(p, 1), columns], values, 0.0)
                if has_plus:
                    values += plus[p, :, columns].astype(F32)
                made[p, :, columns] = values.astype(BF16)
        out_copy(strip).start()
        return carry

    lax.fori_loop(0, STRIPS, body, 0)
    for strip in range(STRIPS):
        out_copy(strip).wait()


def field(own, other, inverse, onset_times, line, plus_start=None):
    own, other = sum(own, []), sum(other, [])
    focal, k, _ = own[0].shape
    samples = inverse.shape[1]
    shape = (focal, samples, onset_times.shape[1])
    plus = [] if plus_start is None else [plus_start]
    moved = [pltpu.VMEM(shape, BF16), pltpu.SemaphoreType.DMA((STRIPS,))]
    return pl.pallas_call(
        functools.partial(field_kernel, line, bool(plus)),
        in_specs=[VMEM] * (2 + len(own) + len(other)) + [FAR] * len(plus),
        out_specs=FAR,
        out_shape=jax.ShapeDtypeStruct(shape, BF16),
        scratch_shapes=moved * (1 + len(plus)),
        compiler_params=limit(12),
        cost_estimate=pl.CostEstimate(
            flops=2 * k * math.prod(shape),
            bytes_accessed=4 * math.prod(shape) + 2 * k * focal * shape[2],
            transcendentals=0,
        ),
        name="field",
    )(inverse, onset_times, *own, *other, *plus)


def add(*parts):
    total = parts[0].astype(F32)
    for part in parts[1:]:
        total += part.astype(F32)
    return total


def after(value, *others):
    return lax.optimization_barrier((value, *others))[0] if others else value


def reduce_scatter(places, keep0, keep1, send0, send1):
    size = places.line
    got1 = places.send(send1, places.core())
    got0 = places.send(send0, places.core())
    far = [add(keep, got).astype(BF16) for keep, got in zip(keep1, got1)]
    across = {step: places.send(far[step], places.pair()) for step in range(2, size)}
    beside = [places.send(far[1], places.shift(1))] if size > 1 else []
    parts = [keep0[0], got0[0]]

    def pass_on(steps, shift, *first):
        carried, sent = [], []
        for step in steps:
            crossed = [after(across[step], *first)] if step in across else []
            carried = [places.send(add(keep0[step], got0[step], *crossed, *carried).astype(BF16), places.shift(shift))]
            sent += carried
        return sent

    ahead = pass_on(range(size // 2, 0, -1), 1)
    behind = pass_on(range(size // 2 + 1, size), size - 1, *beside)
    parts += ahead[-1:] + behind[-1:]
    across[0] = places.send(add(keep1[0], got1[0], *beside).astype(BF16), places.pair())
    return parts + [across[0]]


def gather_chips(places, block, work=None, together=False):
    size = places.line
    near = [1, size - 1] if size > 2 else [1] if size > 1 else []
    far = list(range(2, size - 1))
    made = {}

    def run(flip, steps, pieces, *others):
        if work is None:
            return []
        for step in steps:
            made[flip, step] = work(after(pieces[step], *others), flip, step)
        return [made[flip, step] for step in steps]

    line = {0: block}
    for step in near:
        line[step] = places.send(block, places.shift(step))
    across = {0: places.send(block, places.pair())}
    own = run(0, [0], line)
    for step in range(2, size // 2 + 1):
        line[step] = places.send(after(line[step - 1], across[0], *own), places.shift(1))
    for step in range(size - 2, size // 2, -1):
        line[step] = places.send(after(line[step + 1], *own), places.shift(size - 1))
    for step in near:
        if step == 1:
            across[step] = places.send(after(across[0], line[size - 1]), places.shift(1))
        else:
            across[step] = places.send(line[step], places.pair())
    middle = [across[step] for step in near] if together else run(1, [0], across) + run(0, near, line)
    for step in far:
        across[step] = places.send(after(line[step], *middle), places.pair())
    late = run(0, far, line) + run(1, near, across)
    run(1, far, across, *late)
    pieces = [[side[step] for step in range(size)] for side in (line, across)]
    results = [[made[flip, step] for step in range(size)] for flip in range(2)] if work else None
    return pieces, results


def swap_cores(places, pieces):
    return [places.send(piece, places.core()) for piece in pieces]


def local(plus_start, reflection, onset_times):
    size = lax.axis_size("blk")
    places = Places("blk", size)
    line = places.line
    focal, samples, _ = plus_start.shape
    forward, inverse = constant_tables()
    own_forward = np.ascontiguousarray(forward.reshape(2 * NFW, size, samples).transpose(1, 0, 2))
    own_inverse = inverse.reshape(size, samples, 2 * NFW)
    chip_inverse = inverse.reshape(size // 2, 2 * samples, 2 * NFW)
    sure = forward[:, :SURE].astype(np.float32) @ inverse[:SURE].astype(np.float32)
    forward = jnp.asarray(np.concatenate([forward[:, SURE:], sure.astype(BF16)], axis=1))
    inverse = jnp.asarray(inverse[SURE:])
    own_forward, own_inverse, chip_inverse = map(jnp.asarray, (own_forward, own_inverse, chip_inverse))

    fields = []

    def window_piece(piece, flip, step):
        spectrum, *fields[:] = window_at(
            piece, forward, inverse, onset_times, chip_inverse, line, flip, step, tuple(fields)
        )
        return spectrum

    parts = reduce_scatter(places, *first_analysis(plus_start, own_forward, line))
    start = add(*parts).astype(BF16)
    start = jnp.transpose(start, (1, 0, 2)).reshape(NFW, 2, focal, LANES)
    spectrum_plus = start
    for iteration in range(ITERS):
        last = iteration + 1 == ITERS
        parts = reduce_scatter(places, *convolve(spectrum_plus, reflection, line))
        windowed = window(parts, forward, inverse, onset_times, want_spec=last)
        if last:
            _, own = gather_chips(places, windowed, window_piece)
        else:
            own, _ = gather_chips(places, windowed)
        half = correlate(own[0], swap_cores(places, own[0]), reflection, line, 0)
        across = [own[1][step] if step == 0 else after(own[1][step], half) for step in range(line)]
        downgoing_spec = correlate(own[1], swap_cores(places, across), reflection, line, 1, half, last)
        if not last:
            spectrum_plus = window([downgoing_spec], forward, inverse, onset_times, base=start)
    mine, theirs = fields
    theirs = places.send(after(theirs, downgoing_spec), places.core())
    own, _ = gather_chips(places, downgoing_spec, together=True)
    upgoing = merge(mine, theirs, line)
    other = [swap_cores(places, own[0])]
    across = [own[1][step] if step in (0, 1, line - 1) else after(own[1][step], upgoing) for step in range(line)]
    other.append(swap_cores(places, across))
    downgoing = field(own, other, own_inverse, onset_times, line, plus_start)
    return upgoing, downgoing


def analyze(values, forward):
    total = jnp.einsum("kt,ptx->kpx", forward, values, preferred_element_type=F32)
    return total.reshape(NFW, 2, values.shape[0], values.shape[2])


def synthesize(spectrum, inverse):
    flat = spectrum.reshape(2 * NFW, spectrum.shape[2], spectrum.shape[3])
    return jnp.einsum("tk,kpx->ptx", inverse, flat, preferred_element_type=F32)


def contract(form, left, right):
    return jnp.einsum(form, left, right, preferred_element_type=F32)


def local_any(plus_start, reflection, onset_times):
    samples = plus_start.shape[1]
    width = reflection.shape[2]
    me = lax.axis_index("blk")
    forward, inverse = tables_of(jnp.arange(NT, dtype=jnp.int32))
    own_forward, own_inverse = tables_of(me * samples + jnp.arange(samples, dtype=jnp.int32))
    onset = lax.dynamic_slice_in_dim(onset_times, me * width, width, 1)
    keep = jnp.arange(NT, dtype=jnp.int32)[None, :, None] < onset[:, None, :]
    time = me * samples + jnp.arange(samples, dtype=jnp.int32)
    own_keep = time[None, :, None] < onset_times[:, None, :]

    def scatter(partial):
        return lax.psum_scatter(partial.astype(BF16), "blk", scatter_dimension=3, tiled=True).astype(BF16)

    def gather(block):
        return lax.all_gather(block, "blk", axis=3, tiled=True)

    start = scatter(analyze(plus_start, own_forward))
    spectrum = start
    for iteration in range(ITERS):
        real = contract("wrs,wpr->wps", reflection[0], spectrum[:, 0]) - contract(
            "wrs,wpr->wps", reflection[1], spectrum[:, 1]
        )
        imag = contract("wrs,wpr->wps", reflection[0], spectrum[:, 1]) + contract(
            "wrs,wpr->wps", reflection[1], spectrum[:, 0]
        )
        upgoing_spec = scatter(jnp.stack([real, imag], axis=1))
        kept = jnp.where(keep, synthesize(upgoing_spec, inverse), 0.0).astype(BF16)
        minus = gather(analyze(kept, forward).astype(BF16))
        real = contract("wrs,wps->wpr", reflection[0], minus[:, 0]) + contract(
            "wrs,wps->wpr", reflection[1], minus[:, 1]
        )
        imag = contract("wrs,wps->wpr", reflection[0], minus[:, 1]) - contract(
            "wrs,wps->wpr", reflection[1], minus[:, 0]
        )
        downgoing_spec = jnp.stack([real, imag], axis=1).astype(BF16)
        if iteration + 1 < ITERS:
            kept = jnp.where(keep, synthesize(downgoing_spec, inverse), 0.0).astype(BF16)
            spectrum = (start.astype(F32) + analyze(kept, forward)).astype(BF16)
    upgoing = jnp.where(own_keep, synthesize(gather(upgoing_spec), own_inverse), 0.0).astype(BF16)
    change = jnp.where(own_keep, synthesize(gather(downgoing_spec), own_inverse), 0.0)
    return upgoing, (plus_start.astype(F32) + change).astype(BF16)


def solution(mesh):
    size = mesh.shape["blk"]

    def run(plus_start, reflection, onset_times):
        width = reflection.shape[2] // size
        fits = width == LANES and size % 4 == 0 and (plus_start.shape[1] // size) % 16 == 0
        return jax.shard_map(
            local if fits else local_any,
            mesh=mesh,
            in_specs=(P("groups", "blk", None), P(None, None, "blk", None), P("groups", None)),
            out_specs=(P("groups", "blk", None), P("groups", "blk", None)),
            check_vma=False,
        )(plus_start, reflection, onset_times)

    return run
```
